128 devices in a mesh: tm: 16 (over y_hi, x, core), tensor: 8 (over z, y_lo).
Axes of the slice: x: 4, y: 4 (y_hi: 2, y_lo: 2; y = y_hi * 2 + y_lo), z: 4, core: 2. Of those that a mesh axis runs over, the one named last changes fastest.
Arguments:
- tokens: bfloat16 [12288, 3072], P('tm', 'tensor'), may hold values from -8 to 8
- w_qkv: bfloat16 [3, 3072, 3072], P(None, None, 'tensor'), may hold values from -1 to 1
- gamma: float32 [3, 3072], P(None, 'tensor'), may hold values from -1.5 to 1.5
- beta: float32 [3, 3072], P(None, 'tensor'), may hold values from -1.5 to 1.5
- out_grad: bfloat16 [12288, 3072], P('tm', 'tensor'), may hold values from -6 to 6
- tile_frame: int32 [32], replicated, may hold values from 0 to 15, as said below
- tile_keep: int32 [32, 5], replicated, may hold values from 0 to 1, as said below
Outputs:
- attended: bfloat16 [12288, 3072], P('tm', 'tensor')
- grad_gamma: float32 [3, 3072], P(None, 'tensor')
- grad_beta: float32 [3, 3072], P(None, 'tensor')
The draws below stay inside these ranges and needn't reach their ends.
Inputs may be any that keep to these rules, and one draw needn't show every extreme that they name: `tile_frame`: starts at 0 and never falls, rising by 0 or 1 from one tile to the next; the last tile holds the largest value. `tile_keep`: columns 1, 2 and 3 (a tile with itself and its two neighbouring tiles) are 1 in every row.
All inputs are finite; a program needn't handle non-finite values.
Results may differ from the reference program's by a relative error of at most 0.0094.
Values may be sent and summed in bfloat16 or wider, within the bound.
No kernel may reach another device: no remote copies, remote signals or barrier semaphores. Data moves between devices by JAX's collectives and lax.ppermute only.
A program may use at most 192 MiB of HBM per device.

```python
import jax
import jax.numpy as jnp
from jax import lax

D = 3072
HEADS = 24
HEAD = 128
TILE = 384
TPD = 2
TILES = 32
TOKENS = 12288
N_TM = 16


def draw_tokens(key, part):
    key = jax.random.fold_in(key, 11)
    noise_key = jax.random.fold_in(key, 0)
    base = jax.random.normal(noise_key, (TOKENS, D), jnp.float32)
    return jnp.clip(base, -8.0, 8.0).astype(jnp.bfloat16)


def draw_w_qkv(key, part):
    key = jax.random.fold_in(key, 5)
    main_key = jax.random.fold_in(key, 0)
    scale = D ** (-0.5)
    base = jax.random.normal(main_key, (3, D, D), jnp.float32)
    return jnp.clip(base * scale, -6.0 * scale, 6.0 * scale).astype(jnp.bfloat16)


def draw_tile_frame(key, part):
    key = jax.random.fold_in(key, 23)
    order = jax.random.permutation(key, TILES - 1)
    rising = (order < (TILES - 1) // 2).astype(jnp.int32)
    stepping = jnp.concatenate([jnp.zeros((1,), jnp.int32), rising])
    return jnp.cumsum(stepping).astype(jnp.int32)


def draw_tile_keep(key, part):
    key = jax.random.fold_in(key, 37)
    level = jax.random.randint(key, (TILES, 2 * TPD + 1), 0, 100, dtype=jnp.int32)
    limit = 20 + 70 * jnp.arange(TILES, dtype=jnp.int32) // TILES
    keep = (level < limit[:, None]).astype(jnp.int32)
    center = (jnp.abs(jnp.arange(2 * TPD + 1, dtype=jnp.int32) - TPD) <= 1)[None, :]
    return jnp.where(center, 1, keep).astype(jnp.int32)


def steps_of(own_key, extent, shards, smallest, high):
    def one(position, blocks):
        heights = jax.random.uniform(jax.random.fold_in(jax.random.fold_in(own_key, 6), position), (blocks,), jnp.float32, smallest / len(shards), high / len(shards))
        return jnp.repeat(jnp.exp(heights), extent[position] // blocks).reshape((-1,) + (1,) * (len(extent) - position - 1))

    loudness = one(*shards[0])
    for cut in shards[1:]:
        loudness = loudness * one(*cut)
    return loudness


def noise(stream_key, dims, deviation, most, cuts=(), kind=jnp.bfloat16):
    entries = deviation * jax.random.normal(stream_key, dims, jnp.float32)
    if cuts:
        entries = entries * steps_of(stream_key, dims, cuts, -0.22, 0.18)
    return jnp.clip(entries, -most, most).astype(kind)


def setup_inputs(seed: int = 0) -> dict:
    arg_keys = jax.random.split(jax.random.key(seed), 8)
    return {
        "tokens": draw_tokens(jax.random.fold_in(arg_keys[7], 71), 0),
        "w_qkv": draw_w_qkv(jax.random.fold_in(arg_keys[7], 71), 0),
        "gamma": jnp.clip(jax.random.uniform(arg_keys[2], (3, D), jnp.float32, -1.5, 1.5) * steps_of(arg_keys[2], (3, D), ((1, 8),), -0.4, 0.0), -1.5, 1.5),
        "beta": jnp.clip(jax.random.uniform(arg_keys[3], (3, D), jnp.float32, -1.5, 1.5) * steps_of(arg_keys[3], (3, D), ((1, 8),), -0.4, 0.0), -1.5, 1.5),
        "out_grad": noise(arg_keys[4], (TOKENS, D), 1.0, 6.0, ((0, 16), (1, 8))),
        "tile_frame": draw_tile_frame(jax.random.fold_in(arg_keys[7], 71), 0),
        "tile_keep": draw_tile_keep(jax.random.fold_in(arg_keys[7], 71), 0),
    }


def clip_weights(w_qkv, gamma, beta):
    widened = w_qkv.astype(jnp.float32)
    col_max = jnp.max(widened, axis=1)
    col_min = jnp.min(widened, axis=1)
    upper = jax.nn.sigmoid(gamma)[:, None, :] * col_max[:, None, :]
    lower = jax.nn.sigmoid(beta)[:, None, :] * col_min[:, None, :]
    clipped = jnp.clip(widened, lower, upper).astype(jnp.bfloat16)
    return clipped, widened > upper, widened < lower, col_max, col_min


def tile_window(query_first, query_count, key_first, key_count, frame_pad, keep_pad, window_reach, tile_total):
    query_ids = query_first + jnp.arange(query_count, dtype=jnp.int32)
    key_ids = key_first + jnp.arange(key_count, dtype=jnp.int32)
    query_frames = lax.dynamic_slice_in_dim(frame_pad, (query_first + window_reach).astype(jnp.int32), query_count)
    key_frames = lax.dynamic_slice_in_dim(frame_pad, (key_first + window_reach).astype(jnp.int32), key_count)
    keep_rows = lax.dynamic_slice_in_dim(keep_pad, (query_first + window_reach).astype(jnp.int32), query_count, 0)
    offset = key_ids[None, :] - query_ids[:, None]
    column = offset + window_reach
    choices_range = jnp.arange(2 * window_reach + 1, dtype=jnp.int32)
    picked = jnp.sum(keep_rows[:, None, :] * (column[:, :, None] == choices_range[None, None, :]).astype(jnp.int32), axis=2)
    inside = ((query_ids >= 0) & (query_ids < tile_total))[:, None] & ((key_ids >= 0) & (key_ids < tile_total))[None, :]
    in_reach = jnp.abs(offset) <= window_reach
    near_frame = jnp.abs(query_frames[:, None] - key_frames[None, :]) <= 1
    return inside & in_reach & near_frame & (picked == 1)


def spread(tile_mask):
    return jnp.repeat(jnp.repeat(tile_mask, TILE, axis=0), TILE, axis=1)


def to_half(values):
    return lax.optimization_barrier(values.astype(jnp.bfloat16)).astype(jnp.float32)


def reference(tokens, w_qkv, gamma, beta, out_grad, tile_frame, tile_keep):
    clipped, clipped_high, clipped_low, col_max, col_min = clip_weights(w_qkv, gamma, beta)
    projected = [jnp.dot(tokens, clipped[member], preferred_element_type=jnp.float32).astype(jnp.bfloat16) for member in range(3)]
    block = TPD * TILE
    score_scale = HEAD ** -0.5
    query_all = projected[0].reshape(TOKENS, HEADS, HEAD)
    key_pad = jnp.pad(projected[1], ((block, block), (0, 0))).reshape(TOKENS + 2 * block, HEADS, HEAD)
    value_pad = jnp.pad(projected[2], ((block, block), (0, 0))).reshape(TOKENS + 2 * block, HEADS, HEAD)
    grad_all = out_grad.reshape(TOKENS, HEADS, HEAD)
    frame_pad = jnp.pad(tile_frame, (TPD, TPD))
    keep_pad = jnp.pad(tile_keep, ((TPD, TPD), (0, 0)))

    def step(carry, block_index):
        key_acc, value_acc = carry
        start = (block_index * block).astype(jnp.int32)
        query = lax.dynamic_slice_in_dim(query_all, start, block, 0).astype(jnp.float32)
        grad_out = lax.dynamic_slice_in_dim(grad_all, start, block, 0).astype(jnp.float32)
        keys = lax.dynamic_slice_in_dim(key_pad, start, 3 * block, 0).astype(jnp.float32)
        values = lax.dynamic_slice_in_dim(value_pad, start, 3 * block, 0).astype(jnp.float32)
        tile_first = block_index * TPD
        allowed = spread(tile_window(tile_first, TPD, tile_first - TPD, 3 * TPD, frame_pad, keep_pad, TPD, TILES))[None]
        scores = jnp.einsum("qhe,khe->hqk", query, keys) * score_scale
        scores = jnp.where(allowed, scores, -1e30)
        row_peak = jnp.max(scores, axis=2, keepdims=True)
        weights = jnp.where(allowed, jnp.exp(scores - row_peak), 0.0)
        row_total = jnp.sum(weights, axis=2, keepdims=True)
        probs = weights / row_total
        probs_low = to_half(probs)
        attended = jnp.einsum("hqk,khe->qhe", probs_low, values).astype(jnp.bfloat16)
        dprobs = jnp.einsum("qhe,khe->hqk", grad_out, values)
        row_delta = jnp.sum(probs * dprobs, axis=2, keepdims=True)
        dscores = to_half(probs * (dprobs - row_delta))
        grad_query = (jnp.einsum("hqk,khe->qhe", dscores, keys) * score_scale).astype(jnp.bfloat16)
        key_part = jnp.einsum("hqk,qhe->khe", dscores, query) * score_scale
        value_part = jnp.einsum("hqk,qhe->khe", probs_low, grad_out)
        key_acc = lax.dynamic_update_slice_in_dim(key_acc, lax.dynamic_slice_in_dim(key_acc, start, 3 * block, 0) + key_part, start, 0)
        value_acc = lax.dynamic_update_slice_in_dim(value_acc, lax.dynamic_slice_in_dim(value_acc, start, 3 * block, 0) + value_part, start, 0)
        return (key_acc, value_acc), (attended, grad_query)

    empty = jnp.zeros((TOKENS + 2 * block, HEADS, HEAD), jnp.float32)
    (key_acc, value_acc), (attended, grad_query) = lax.scan(step, (empty, empty), jnp.arange(N_TM, dtype=jnp.int32))
    attended = attended.reshape(TOKENS, D)
    grads = [grad_query.reshape(TOKENS, D), key_acc[block:block + TOKENS].reshape(TOKENS, D).astype(jnp.bfloat16), value_acc[block:block + TOKENS].reshape(TOKENS, D).astype(jnp.bfloat16)]
    high_sums = []
    low_sums = []
    for member in range(3):
        grad_clipped = jnp.dot(tokens.T, grads[member], preferred_element_type=jnp.float32)
        high_sums.append(jnp.sum(jnp.where(clipped_high[member], grad_clipped, 0.0), axis=0))
        low_sums.append(jnp.sum(jnp.where(clipped_low[member], grad_clipped, 0.0), axis=0))
    sig_gamma = jax.nn.sigmoid(gamma)
    sig_beta = jax.nn.sigmoid(beta)
    grad_gamma = sig_gamma * (1.0 - sig_gamma) * col_max * jnp.stack(high_sums)
    grad_beta = sig_beta * (1.0 - sig_beta) * col_min * jnp.stack(low_sums)
    return attended, grad_gamma, grad_beta
```

```python
import functools
import math

import jax
import jax.numpy as jnp
from jax import lax
from jax.experimental import pallas as pl
from jax.experimental.pallas import tpu as pltpu
from jax.sharding import PartitionSpec as P

HEAD = 128
TILE = 384
REACH = 2
WINDOW = 2 * REACH + 1
SCALE = HEAD**-0.5
LOG2E = math.log2(math.e)
NEG = -1e30
VMEM_LIMIT = 56 * 1024 * 1024

NT = (((1,), (1,)), ((), ()))


def dot(a, b):
    return jnp.dot(a, b, preferred_element_type=jnp.float32)


def dot_nt(a, b):
    return lax.dot_general(a, b, NT, preferred_element_type=jnp.float32)


def tensor_routes(z_count):
    def route(f):
        return [(z * 2 + y, f(z, y)) for z in range(z_count) for y in range(2)]

    up = route(lambda z, y: ((z + 1) % z_count) * 2 + y)
    down = route(lambda z, y: ((z - 1) % z_count) * 2 + y)
    swap = route(lambda z, y: z * 2 + 1 - y)
    return up, down, swap


def gather_chunks(rows):
    up, down, swap = tensor_routes(4)
    send = lambda a, route: lax.ppermute(a, "tensor", route)
    half = rows.shape[0] // 2
    from_below = send(rows, up)
    from_above = send(rows, down)
    beside = send(rows, swap)
    far_lo = send(from_below[:half], up)
    far_hi = send(from_above[half:], down)
    beside_below = send(beside, up)
    beside_above = send(beside, down)
    beside_far_lo = send(far_lo, swap)
    beside_far_hi = send(far_hi, swap)
    return (
        rows,
        from_below,
        from_above,
        beside,
        beside_below,
        beside_above,
        far_lo,
        far_hi,
        beside_far_lo,
        beside_far_hi,
    )


def prep_kernel(w_ref, gamma_ref, beta_ref, clipped_ref, mask_ref, coef_ref):
    me = lax.axis_index("tensor")
    z, y = me // 2, lax.rem(me, 2)
    below, above, far = lax.rem(z + 3, 4), lax.rem(z + 1, 4), lax.rem(z + 2, 4)
    slots = (
        z * 2 + y,
        below * 2 + y,
        above * 2 + y,
        z * 2 + 1 - y,
        below * 2 + 1 - y,
        above * 2 + 1 - y,
        far * 2 + y,
        far * 2 + 1 - y,
    )
    depth = clipped_ref.shape[2]
    w = w_ref[0].astype(jnp.float32)
    col_max = jnp.max(w, axis=0, keepdims=True)
    col_min = jnp.min(w, axis=0, keepdims=True)
    sig_gamma = jax.nn.sigmoid(gamma_ref[0])
    sig_beta = jax.nn.sigmoid(beta_ref[0])
    upper = sig_gamma * col_max
    lower = sig_beta * col_min
    coef_ref[0, 0:1] = sig_gamma * (1.0 - sig_gamma) * col_max
    coef_ref[0, 1:2] = sig_beta * (1.0 - sig_beta) * col_min
    for slot, chunk in enumerate(slots):
        block = w_ref[0, pl.ds(pl.multiple_of(chunk * depth, depth), depth), :].astype(jnp.float32)
        clipped_ref[0, slot] = jnp.minimum(jnp.maximum(block, lower), upper).astype(jnp.bfloat16)
        mask_ref[0, slot] = jnp.where(block > upper, 1.0, 0.0).astype(jnp.bfloat16)
        mask_ref[1, slot] = jnp.where(block < lower, 1.0, 0.0).astype(jnp.bfloat16)


def prep(w_qkv, gamma, beta):
    members, rows, width = w_qkv.shape
    depth = rows // 8
    cols = 128
    return pl.pallas_call(
        prep_kernel,
        grid=(members, width // cols),
        in_specs=[
            pl.BlockSpec((1, rows, cols), lambda p, c: (p, 0, c)),
            pl.BlockSpec((1, 1, cols), lambda p, c: (p, 0, c)),
            pl.BlockSpec((1, 1, cols), lambda p, c: (p, 0, c)),
        ],
        out_specs=[
            pl.BlockSpec((1, 8, depth, cols), lambda p, c: (p, 0, 0, c)),
            pl.BlockSpec((2, 8, depth, cols), lambda p, c: (p, 0, 0, c)),
            pl.BlockSpec((1, 2, cols), lambda p, c: (p, 0, c)),
        ],
        out_shape=[
            jax.ShapeDtypeStruct((members, 8, depth, width), jnp.bfloat16),
            jax.ShapeDtypeStruct((2 * members, 8, depth, width), jnp.bfloat16),
            jax.ShapeDtypeStruct((members, 2, width), jnp.float32),
        ],
        compiler_params=pltpu.CompilerParams(vmem_limit_bytes=VMEM_LIMIT),
        cost_estimate=pl.CostEstimate(flops=0, bytes_accessed=28_000_000, transcendentals=0),
        name="clip_weights",
    )(w_qkv, gamma[:, None], beta[:, None])


def load_rows(x_refs, x_scr):
    depth = x_refs[0].shape[1]
    half = x_refs[6].shape[0]
    for slot in range(6):
        x_scr[:, slot * depth : (slot + 1) * depth] = x_refs[slot][...]
    for slot in (6, 7):
        lo, hi = x_refs[2 * slot - 6], x_refs[2 * slot - 5]
        x_scr[0:half, slot * depth : (slot + 1) * depth] = lo[...]
        x_scr[half : 2 * half, slot * depth : (slot + 1) * depth] = hi[...]


def project_kernel(*refs):
    x_refs, w_ref, q_ref, kv_ref, x_scr = refs[:10], refs[10], refs[11], refs[12], refs[13]
    member = pl.program_id(0)

    @pl.when(member == 0)
    def _():
        load_rows(x_refs, x_scr)

    full, width = x_scr.shape[1], w_ref.shape[3]
    result = dot(x_scr[...], w_ref[0].reshape(full, width))

    @pl.when(member == 0)
    def _():
        q_ref[...] = (result * (SCALE * LOG2E)).astype(jnp.bfloat16)

    @pl.when(member > 0)
    def _():
        kv_ref[0] = result.astype(jnp.bfloat16)


def mask_kernel(*refs):
    x_refs, w_ref, tq_ref, tkv_ref, x_scr = refs[:10], refs[10], refs[11], refs[12], refs[13]
    member = pl.program_id(0)

    @pl.when(member == 0)
    def _():
        load_rows(x_refs, x_scr)

    full, width = x_scr.shape[1], w_ref.shape[3]
    result = dot(x_scr[...], w_ref[0].reshape(full, width)).astype(jnp.bfloat16)

    @pl.when(member < 2)
    def _():
        tq_ref[0] = result

    @pl.when(member >= 2)
    def _():
        tkv_ref[0] = result


def project(chunks, weights, masks):
    rows = chunks[0].shape[0]
    members, _, depth, width = weights.shape
    if masks:
        kernel, name = mask_kernel, "project_masks"
        first_spec = pl.BlockSpec((1, rows, width), lambda p: (jnp.minimum(p, 1), 0, 0))
        first_shape = (2, rows, width)
        second_spec = pl.BlockSpec((1, rows, width), lambda p: (jnp.maximum(p - 2, 0), 0, 0))
        second_shape = (members - 2, rows, width)
    else:
        kernel, name = project_kernel, "project_qkv"
        first_spec = pl.BlockSpec((rows, width), lambda p: (0, 0))
        first_shape = (rows, width)
        second_spec = pl.BlockSpec((1, rows, width), lambda p: (jnp.maximum(p - 1, 0), 0, 0))
        second_shape = (members - 1, rows, width)
    return pl.pallas_call(
        kernel,
        grid=(members,),
        in_specs=[pl.BlockSpec(c.shape, lambda p: (0, 0)) for c in chunks]
        + [pl.BlockSpec((1, 8, depth, width), lambda p: (p, 0, 0, 0))],
        out_specs=[first_spec, second_spec],
        out_shape=[
            jax.ShapeDtypeStruct(first_shape, jnp.bfloat16),
            jax.ShapeDtypeStruct(second_shape, jnp.bfloat16),
        ],
        scratch_shapes=[pltpu.VMEM((rows, 8 * depth), jnp.bfloat16)],
        compiler_params=pltpu.CompilerParams(vmem_limit_bytes=VMEM_LIMIT),
        cost_estimate=pl.CostEstimate(
            flops=2 * rows * 8 * depth * width * members,
            bytes_accessed=members * 8 * depth * width * 2,
            transcendentals=0,
        ),
        name=name,
    )(*chunks, weights)


def attend_kernel(frame_ref, keep_ref, *refs):
    q_refs, kv_refs, grad_ref = refs[0:2], refs[2:8], refs[8]
    att_ref, e_ref, ds_ref, inv_ref, gq_ref, k_scr, v_scr = refs[9:]
    for index, kv in enumerate(kv_refs):
        k_scr[index * TILE : (index + 1) * TILE] = kv[0]
        v_scr[index * TILE : (index + 1) * TILE] = kv[1]
    first = lax.axis_index("tm") * 2
    tiles = frame_ref.shape[0]
    for i in range(2):
        a = first + i
        bias = []
        for t in range(WINDOW):
            b = a + (t - REACH)
            b_in = jnp.clip(b, 0, tiles - 1)
            ok = (
                (b >= 0)
                & (b < tiles)
                & (jnp.abs(frame_ref[a] - frame_ref[b_in]) <= 1)
                & (keep_ref[a, t] == 1)
            )
            bias.append(jnp.where(ok, 0.0, NEG))
        q = q_refs[i][...]
        rows = slice(i * TILE, (i + 1) * TILE)
        grad = grad_ref[rows, :]
        k = k_scr[i * TILE : i * TILE + WINDOW * TILE]
        v = v_scr[i * TILE : i * TILE + WINDOW * TILE]
        scores = dot_nt(q, k)
        parts = [scores[:, t * TILE : (t + 1) * TILE] for t in range(WINDOW)]
        peak = functools.reduce(
            jnp.maximum,
            [jnp.max(p, axis=1, keepdims=True) + bias[t] for t, p in enumerate(parts)],
        )
        weights = [jnp.exp2(p - (peak - bias[t])) for t, p in enumerate(parts)]
        total = sum(jnp.sum(w, axis=1, keepdims=True) for w in weights)
        e = jnp.concatenate(weights, axis=1)
        e_low = e.astype(jnp.bfloat16)
        inv = 1.0 / total
        out = dot(e_low, v) * inv
        att_ref[rows, :] = out.astype(jnp.bfloat16)
        delta = jnp.sum(out * grad.astype(jnp.float32), axis=1, keepdims=True)
        dprobs = dot_nt(grad, v)
        ds = (e * (dprobs - delta)).astype(jnp.bfloat16)
        e_ref[0, i] = e_low
        ds_ref[0, i] = ds
        inv_ref[rows, :] = jnp.broadcast_to(inv, (TILE, HEAD))
        gq_ref[rows, :] = (dot(ds, k) * (inv * SCALE)).astype(jnp.bfloat16)


def attend(tile_frame, tile_keep, queries, kvs, out_grad):
    rows, width = out_grad.shape
    heads = width // HEAD
    span = WINDOW * TILE
    column = pl.BlockSpec((rows, HEAD), lambda h, *_: (0, h))
    big = pl.BlockSpec((1, 2, TILE, span), lambda h, *_: (h, 0, 0, 0))
    return pl.pallas_call(
        attend_kernel,
        grid_spec=pltpu.PrefetchScalarGridSpec(
            num_scalar_prefetch=2,
            grid=(heads,),
            in_specs=[pl.BlockSpec((TILE, HEAD), lambda h, *_: (0, h))] * 2
            + [pl.BlockSpec((2, TILE, HEAD), lambda h, *_: (0, 0, h))] * 6
            + [column],
            out_specs=[column, big, big, column, column],
            scratch_shapes=[pltpu.VMEM((6 * TILE, HEAD), jnp.bfloat16)] * 2,
        ),
        out_shape=[
            jax.ShapeDtypeStruct((rows, width), jnp.bfloat16),
            jax.ShapeDtypeStruct((heads, 2, TILE, span), jnp.bfloat16),
            jax.ShapeDtypeStruct((heads, 2, TILE, span), jnp.bfloat16),
            jax.ShapeDtypeStruct((rows, width), jnp.float32),
            jax.ShapeDtypeStruct((rows, width), jnp.bfloat16),
        ],
        compiler_params=pltpu.CompilerParams(vmem_limit_bytes=VMEM_LIMIT),
        cost_estimate=pl.CostEstimate(
            flops=2 * 4 * rows * span * width, bytes_accessed=25_000_000, transcendentals=rows * span * heads
        ),
        name="attend",
    )(tile_frame, tile_keep, *queries, *kvs, out_grad)


def sums_kernel(*refs):
    q_refs, tq_refs, tkv_refs = refs[0:2], refs[2:4], refs[4:10]
    grad_ref, e_ref, ds_ref, inv_ref, gq_ref, coef_ref, out_ref, tk_scr, tv_scr = refs[10:]
    for index, tkv in enumerate(tkv_refs):
        rows = slice(index * TILE, (index + 1) * TILE)
        tk_scr[rows, 0:HEAD] = tkv[0]
        tk_scr[rows, HEAD : 2 * HEAD] = tkv[1]
        tv_scr[rows, 0:HEAD] = tkv[2]
        tv_scr[rows, HEAD : 2 * HEAD] = tkv[3]
    sums = [[0.0] * 3 for _ in range(2)]
    for i in range(2):
        rows = slice(i * TILE, (i + 1) * TILE)
        keys = slice(i * TILE, i * TILE + WINDOW * TILE)
        inv = inv_ref[rows, :]
        from_k = dot(ds_ref[0, i], tk_scr[keys])
        from_v = dot(e_ref[0, i], tv_scr[keys])
        gq = gq_ref[rows, :].astype(jnp.float32)
        q = q_refs[i][...].astype(jnp.float32) * (inv * (1.0 / LOG2E))
        grad = grad_ref[rows, :].astype(jnp.float32) * inv
        for side in range(2):
            cols = slice(side * HEAD, (side + 1) * HEAD)
            tq = tq_refs[i][side].astype(jnp.float32)
            sums[side][0] += jnp.sum(gq * tq, axis=0, keepdims=True)
            sums[side][1] += jnp.sum(q * from_k[:, cols], axis=0, keepdims=True)
            sums[side][2] += jnp.sum(grad * from_v[:, cols], axis=0, keepdims=True)
    for side in range(2):
        for member in range(3):
            out_ref[side, member : member + 1] = sums[side][member] * coef_ref[member, side : side + 1]


def column_sums(queries, tqs, tkvs, out_grad, e, ds, inv, gq, coef):
    rows, width = out_grad.shape
    heads = width // HEAD
    span = WINDOW * TILE
    column = pl.BlockSpec((rows, HEAD), lambda h: (0, h))
    big = pl.BlockSpec((1, 2, TILE, span), lambda h: (h, 0, 0, 0))
    return pl.pallas_call(
        sums_kernel,
        grid=(heads,),
        in_specs=[pl.BlockSpec((TILE, HEAD), lambda h: (0, h))] * 2
        + [pl.BlockSpec((2, TILE, HEAD), lambda h: (0, 0, h))] * 2
        + [pl.BlockSpec((4, TILE, HEAD), lambda h: (0, 0, h))] * 6
        + [column, big, big, column, column, pl.BlockSpec((3, 2, HEAD), lambda h: (0, 0, h))],
        out_specs=pl.BlockSpec((2, 3, HEAD), lambda h: (0, 0, h)),
        out_shape=jax.ShapeDtypeStruct((2, 3, width), jnp.float32),
        scratch_shapes=[pltpu.VMEM((6 * TILE, 2 * HEAD), jnp.bfloat16)] * 2,
        compiler_params=pltpu.CompilerParams(vmem_limit_bytes=VMEM_LIMIT),
        cost_estimate=pl.CostEstimate(
            flops=2 * 4 * rows * span * width, bytes_accessed=22_000_000, transcendentals=0
        ),
        name="column_sums",
    )(*queries, *tqs, *tkvs, out_grad, e, ds, inv, gq, coef)


def neighbours(block):
    count = lax.axis_size("tm")
    up = [(i, i + 1) for i in range(count - 1)]
    down = [(i + 1, i) for i in range(count - 1)]
    return lax.ppermute(block, "tm", up), lax.ppermute(block, "tm", down)


def sum_over_tm(part):
    count = lax.axis_size("tm")
    step = 1
    while step < count:
        part = part + lax.ppermute(part, "tm", [(i, i ^ step) for i in range(count)])
        step *= 2
    return part


def body(tokens, w_qkv, gamma, beta, out_grad, tile_frame, tile_keep):
    clipped, masks, coef = prep(w_qkv, gamma, beta)
    queries, kvs, tqs, tkvs = [], [], [], []
    for tile in range(2):
        chunks = gather_chunks(tokens[tile * TILE : (tile + 1) * TILE])
        query, kv = project(chunks, clipped, False)
        kv_before, kv_after = neighbours(kv)
        tq, tkv = project(chunks, masks, True)
        tkv_before, tkv_after = neighbours(tkv)
        queries.append(query)
        kvs.append((kv_before, kv, kv_after))
        tqs.append(tq)
        tkvs.append((tkv_before, tkv, tkv_after))
    kv_all = [kvs[tile][place] for place in range(3) for tile in range(2)]
    tkv_all = [tkvs[tile][place] for place in range(3) for tile in range(2)]
    attended, e, ds, inv, gq = attend(tile_frame, tile_keep, queries, kv_all, out_grad)
    part = column_sums(queries, tqs, tkv_all, out_grad, e, ds, inv, gq, coef)
    totals = sum_over_tm(part)
    return attended, totals[0], totals[1]


def solution(mesh):
    return jax.shard_map(
        body,
        mesh=mesh,
        in_specs=(
            P("tm", "tensor"),
            P(None, None, "tensor"),
            P(None, "tensor"),
            P(None, "tensor"),
            P("tm", "tensor"),
            P(),
            P(),
        ),
        out_specs=(P("tm", "tensor"), P(None, "tensor"), P(None, "tensor")),
        check_vma=False,
    )
```

```python
import functools
import math

import jax
import jax.numpy as jnp
from jax import lax
from jax.experimental import pallas as pl
from jax.experimental.pallas import tpu as pltpu
from jax.sharding import PartitionSpec as P

HEAD = 128
TILE = 384
REACH = 2
WINDOW = 2 * REACH + 1
SCALE = HEAD**-0.5
LOG2E = math.log2(math.e)
NEG = -1e30
VMEM_LIMIT = 26 * 1024 * 1024
ATTEND_VMEM = 40 * 1024 * 1024

NT = (((1,), (1,)), ((), ()))


def dot(a, b):
    return jnp.dot(a, b, preferred_element_type=jnp.float32)


def dot_nt(a, b):
    return lax.dot_general(a, b, NT, preferred_element_type=jnp.float32)


def tensor_routes(z_count):
    def route(f):
        return [(z * 2 + y, f(z, y)) for z in range(z_count) for y in range(2)]

    up = route(lambda z, y: ((z + 1) % z_count) * 2 + y)
    down = route(lambda z, y: ((z - 1) % z_count) * 2 + y)
    swap = route(lambda z, y: z * 2 + 1 - y)
    return up, down, swap


def send(block, route):
    return lax.ppermute(block, "tensor", route)


def after(value, *others):
    return lax.optimization_barrier((value,) + others)[0]


def chunk_slots():
    me = lax.axis_index("tensor")
    z, y = me // 2, lax.rem(me, 2)
    below, above, far = lax.rem(z + 3, 4), lax.rem(z + 1, 4), lax.rem(z + 2, 4)
    return jnp.stack(
        [
            z * 2 + y,
            below * 2 + y,
            above * 2 + y,
            z * 2 + 1 - y,
            below * 2 + 1 - y,
            above * 2 + 1 - y,
            far * 2 + y,
            far * 2 + 1 - y,
        ]
    ).astype(jnp.int32)


def bounds_kernel(w_ref, gamma_ref, beta_ref, bound_ref, coef_ref):
    w = w_ref[0].astype(jnp.float32)
    col_max = jnp.max(w, axis=0, keepdims=True)
    col_min = jnp.min(w, axis=0, keepdims=True)
    member = pl.program_id(0)
    sig_gamma = jax.nn.sigmoid(gamma_ref[pl.ds(member, 1), :])
    sig_beta = jax.nn.sigmoid(beta_ref[pl.ds(member, 1), :])
    bound_ref[0, 0:1] = sig_gamma * col_max
    bound_ref[0, 1:2] = sig_beta * col_min
    coef_ref[0, 0:1] = sig_gamma * (1.0 - sig_gamma) * col_max
    coef_ref[0, 1:2] = sig_beta * (1.0 - sig_beta) * col_min


def bounds(w_qkv, gamma, beta):
    members, rows, width = w_qkv.shape
    whole = pl.BlockSpec((members, width), lambda p: (0, 0))
    two = pl.BlockSpec((1, 2, width), lambda p: (p, 0, 0))
    return pl.pallas_call(
        bounds_kernel,
        grid=(members,),
        in_specs=[pl.BlockSpec((1, rows, width), lambda p: (p, 0, 0)), whole, whole],
        out_specs=[two, two],
        out_shape=[jax.ShapeDtypeStruct((members, 2, width), jnp.float32)] * 2,
        compiler_params=pltpu.CompilerParams(vmem_limit_bytes=VMEM_LIMIT),
        cost_estimate=pl.CostEstimate(flops=0, bytes_accessed=7_000_000, transcendentals=0),
        name="clip_bounds",
    )(w_qkv, gamma, beta)


def load_rows(x_refs, x_scr, depth):
    col = row = 0
    for ref in x_refs:
        rows = ref.shape[0]
        x_scr[row : row + rows, col : col + depth] = ref[...]
        row += rows
        if row == x_scr.shape[0]:
            row, col = 0, col + depth


def clip_rows(w_refs, bound_ref, out_scr):
    upper, lower = bound_ref[0, 0:1], bound_ref[0, 1:2]
    depth, width = w_refs[0].shape[1:]
    for index, ref in enumerate(w_refs):
        block = ref[0].astype(jnp.float32)
        rows = slice(index * depth, (index + 1) * depth)
        out_scr[rows, 0:width] = jnp.minimum(jnp.maximum(block, lower), upper).astype(jnp.bfloat16)


def mask_rows(w_refs, bound_ref, out_scr, first):
    upper, lower = bound_ref[0, 0:1], bound_ref[0, 1:2]
    depth, width = w_refs[0].shape[1:]
    for index, ref in enumerate(w_refs):
        block = ref[0].astype(jnp.float32)
        rows = slice(index * depth, (index + 1) * depth)
        out_scr[rows, first : first + width] = jnp.where(block > upper, 1.0, 0.0).astype(
            jnp.bfloat16
        )
        out_scr[rows, first + width : first + 2 * width] = jnp.where(
            block < lower, 1.0, 0.0
        ).astype(jnp.bfloat16)


def early_kernel(slot_ref, *refs):
    x_refs, w_refs, bound_ref = refs[0:4], refs[4:8], refs[8]
    qkv_ref, mask_ref, x_scr, w_scr = refs[9:]
    depth, width = w_refs[0].shape[1:]

    @pl.when(pl.program_id(0) == 0)
    def _():
        load_rows(x_refs, x_scr, depth)

    clip_rows(w_refs, bound_ref, w_scr)
    mask_rows(w_refs, bound_ref, w_scr, width)
    result = dot(x_scr[...], w_scr[...])
    qkv_ref[0] = result[:, 0:width]
    mask_ref[0] = result[:, width:]


def late_qkv_kernel(slot_ref, *refs):
    x_refs, w_refs, bound_ref, sum_ref = refs[0:6], refs[6:10], refs[10], refs[11]
    q_ref, kv_ref, x_scr, w_scr = refs[12:]
    member = pl.program_id(0)

    @pl.when(member == 0)
    def _():
        load_rows(x_refs, x_scr, w_refs[0].shape[1])

    clip_rows(w_refs, bound_ref, w_scr)
    result = sum_ref[0] + dot(x_scr[...], w_scr[...])

    @pl.when(member == 0)
    def _():
        q_ref[...] = (result * (SCALE * LOG2E)).astype(jnp.bfloat16)

    @pl.when(member > 0)
    def _():
        kv_ref[0] = result.astype(jnp.bfloat16)


def late_mask_kernel(slot_ref, *refs):
    x_refs, w_refs, bound_ref, sum_ref = refs[0:6], refs[6:10], refs[10], refs[11]
    out_ref, x_scr, w_scr = refs[12:]

    @pl.when(pl.program_id(0) == 0)
    def _():
        load_rows(x_refs, x_scr, w_refs[0].shape[1])

    mask_rows(w_refs, bound_ref, w_scr, 0)
    out_ref[0] = (sum_ref[0] + dot(x_scr[...], w_scr[...])).astype(jnp.bfloat16)


def product_call(kernel, name, slots, first_slot, chunks, w_qkv, bound, sums, outs, columns):
    members, full, width = w_qkv.shape
    depth = full // 8
    rows = max(c.shape[0] for c in chunks)
    inner = sum(c.shape[0] for c in chunks) // rows * depth
    count = inner // depth
    w_specs = [
        pl.BlockSpec((1, depth, width), lambda p, s, i=first_slot + i: (p, s[i], 0))
        for i in range(count)
    ]
    return pl.pallas_call(
        kernel,
        grid_spec=pltpu.PrefetchScalarGridSpec(
            num_scalar_prefetch=1,
            grid=(members,),
            in_specs=[pl.BlockSpec(c.shape, lambda p, s: (0, 0)) for c in chunks]
            + w_specs
            + [pl.BlockSpec((1, 2, width), lambda p, s: (p, 0, 0))]
            + [pl.BlockSpec((1,) + a.shape[1:], lambda p, s: (p, 0, 0)) for a in sums],
            out_specs=[spec for spec, _ in outs],
            scratch_shapes=[
                pltpu.VMEM((rows, inner), jnp.bfloat16),
                pltpu.VMEM((inner, columns), jnp.bfloat16),
            ],
        ),
        out_shape=[shape for _, shape in outs],
        compiler_params=pltpu.CompilerParams(vmem_limit_bytes=VMEM_LIMIT),
        cost_estimate=pl.CostEstimate(
            flops=2 * rows * inner * columns * members,
            bytes_accessed=members * inner * width * 2,
            transcendentals=0,
        ),
        name=name,
    )(slots, *chunks, *([w_qkv] * count), bound, *sums)


def members_out(members, rows, columns, dtype):
    spec = pl.BlockSpec((1, rows, columns), lambda p, s: (p, 0, 0))
    return spec, jax.ShapeDtypeStruct((members, rows, columns), dtype)


def early_products(slots, chunks, w_qkv, bound):
    members, _, width = w_qkv.shape
    rows = chunks[0].shape[0]
    outs = [
        members_out(members, rows, width, jnp.float32),
        members_out(members, rows, 2 * width, jnp.float32),
    ]
    return product_call(
        early_kernel, "early_products", slots, 0, chunks, w_qkv, bound, [], outs, 3 * width
    )


def late_qkv(slots, chunks, w_qkv, bound, sums):
    members, _, width = w_qkv.shape
    rows = chunks[0].shape[0]
    outs = [
        (
            pl.BlockSpec((rows, width), lambda p, s: (0, 0)),
            jax.ShapeDtypeStruct((rows, width), jnp.bfloat16),
        ),
        (
            pl.BlockSpec((1, rows, width), lambda p, s: (jnp.maximum(p - 1, 0), 0, 0)),
            jax.ShapeDtypeStruct((2, rows, width), jnp.bfloat16),
        ),
    ]
    return product_call(
        late_qkv_kernel, "late_qkv", slots, 4, chunks, w_qkv, bound, [sums], outs, width
    )


def late_masks(slots, chunks, w_qkv, bound, sums):
    members, _, width = w_qkv.shape
    outs = [members_out(members, chunks[0].shape[0], 2 * width, jnp.bfloat16)]
    return product_call(
        late_mask_kernel, "late_masks", slots, 4, chunks, w_qkv, bound, [sums], outs, 2 * width
    )[0]


def attend_kernel(frame_ref, keep_ref, *refs):
    q_ref, kv_ref, near_ref, other_ref, grad_ref = refs[0:5]
    att_ref, gq_ref, own_ref, for_near_ref, for_other_ref, k_scr, v_scr, gk_scr, gv_scr = refs[5:]
    position = lax.axis_index("tm")
    count = 2 * TILE
    even = 1 - lax.rem(position, 2)
    near_at = pl.multiple_of(2 * count * even, count)
    other_at = pl.multiple_of(2 * count * (1 - even), count)
    for member, scr in enumerate((k_scr, v_scr)):
        scr[count : 2 * count] = kv_ref[member]
        scr[pl.ds(near_at, count), :] = near_ref[member]
        scr[pl.ds(other_at, count), :] = other_ref[member]
    first = position * 2
    tiles = frame_ref.shape[0]
    for i in range(2):
        a = first + i
        bias = []
        for t in range(WINDOW):
            b = a + (t - REACH)
            b_in = jnp.clip(b, 0, tiles - 1)
            ok = (
                (b >= 0)
                & (b < tiles)
                & (jnp.abs(frame_ref[a] - frame_ref[b_in]) <= 1)
                & (keep_ref[a, t] == 1)
            )
            bias.append(jnp.where(ok, 0.0, NEG))
        rows = slice(i * TILE, (i + 1) * TILE)
        keys = slice(i * TILE, i * TILE + WINDOW * TILE)
        q = q_ref[rows, :]
        grad = grad_ref[rows, :]
        k = k_scr[keys]
        v = v_scr[keys]
        scores = dot_nt(q, k)
        parts = [scores[:, t * TILE : (t + 1) * TILE] for t in range(WINDOW)]
        peak = functools.reduce(
            jnp.maximum,
            [jnp.max(p, axis=1, keepdims=True) + bias[t] for t, p in enumerate(parts)],
        )
        weights = [jnp.exp2(p - (peak - bias[t])) for t, p in enumerate(parts)]
        total = sum(jnp.sum(w, axis=1, keepdims=True) for w in weights)
        e = jnp.concatenate(weights, axis=1)
        e_low = e.astype(jnp.bfloat16)
        inv = 1.0 / total
        out = dot(e_low, v) * inv
        att_ref[rows, :] = out.astype(jnp.bfloat16)
        grad_wide = grad.astype(jnp.float32)
        delta = jnp.sum(out * grad_wide, axis=1, keepdims=True)
        dprobs = dot_nt(grad, v)
        ds = (e * (dprobs - delta)).astype(jnp.bfloat16)
        gq_ref[rows, :] = (dot(ds, k) * (inv * SCALE)).astype(jnp.bfloat16)
        q_scaled = (q.astype(jnp.float32) * (inv * (1.0 / LOG2E))).astype(jnp.bfloat16)
        grad_scaled = (grad_wide * inv).astype(jnp.bfloat16)
        gk = dot(q_scaled.T, ds)
        gv = dot(grad_scaled.T, e_low)
        if i == 0:
            gk_scr[:, keys] = gk
            gv_scr[:, keys] = gv
        else:
            span, head = WINDOW * TILE, slice(i * TILE, WINDOW * TILE)
            rest = slice(WINDOW * TILE, (WINDOW + 1) * TILE)
            gk_scr[:, head] += gk[:, 0 : span - TILE]
            gv_scr[:, head] += gv[:, 0 : span - TILE]
            gk_scr[:, rest] = gk[:, span - TILE :]
            gv_scr[:, rest] = gv[:, span - TILE :]
    for member, scr in enumerate((gk_scr, gv_scr)):
        own_ref[member] = scr[:, count : 2 * count].T.astype(jnp.bfloat16)
        for_near_ref[member] = scr[:, pl.ds(near_at, count)].T.astype(jnp.bfloat16)
        for_other_ref[member] = scr[:, pl.ds(other_at, count)].T.astype(jnp.bfloat16)


def attend(tile_frame, tile_keep, query, kv, kv_near, kv_other, out_grad):
    rows, width = out_grad.shape
    heads = width // HEAD
    span = WINDOW * TILE
    column = pl.BlockSpec((rows, HEAD), lambda h, *_: (0, h))
    pair = pl.BlockSpec((2, rows, HEAD), lambda h, *_: (0, 0, h))
    return pl.pallas_call(
        attend_kernel,
        grid_spec=pltpu.PrefetchScalarGridSpec(
            num_scalar_prefetch=2,
            grid=(heads,),
            in_specs=[column, pair, pair, pair, column],
            out_specs=[column, column, pair, pair, pair],
            scratch_shapes=[pltpu.VMEM((6 * TILE, HEAD), jnp.bfloat16)] * 2
            + [pltpu.VMEM((HEAD, 6 * TILE), jnp.float32)] * 2,
        ),
        out_shape=[
            jax.ShapeDtypeStruct((rows, width), jnp.bfloat16),
            jax.ShapeDtypeStruct((rows, width), jnp.bfloat16),
            jax.ShapeDtypeStruct((2, rows, width), jnp.bfloat16),
            jax.ShapeDtypeStruct((2, rows, width), jnp.bfloat16),
            jax.ShapeDtypeStruct((2, rows, width), jnp.bfloat16),
        ],
        compiler_params=pltpu.CompilerParams(vmem_limit_bytes=ATTEND_VMEM),
        cost_estimate=pl.CostEstimate(
            flops=2 * 6 * rows * span * width,
            bytes_accessed=15_000_000,
            transcendentals=rows * span * heads,
        ),
        name="attend",
    )(tile_frame, tile_keep, query, kv, kv_near, kv_other, out_grad)


def add_up(grad, t_ref, coef_ref, side):
    width = grad.shape[1]
    part = grad * t_ref[0, :, side * width : (side + 1) * width].astype(jnp.float32)
    return jnp.sum(part, axis=0, keepdims=True) * coef_ref[0, side : side + 1]


def own_sums_kernel(gq_ref, own_ref, t_ref, coef_ref, out_ref):
    member = pl.program_id(0)

    @pl.when(member == 0)
    def _():
        for side in range(2):
            grad = gq_ref[...].astype(jnp.float32)
            out_ref[0, side : side + 1] = add_up(grad, t_ref, coef_ref, side)

    @pl.when(member > 0)
    def _():
        for side in range(2):
            grad = own_ref[0].astype(jnp.float32)
            out_ref[0, side : side + 1] = add_up(grad, t_ref, coef_ref, side)


def own_sums(gq, own, products, coef):
    rows, width = gq.shape
    return pl.pallas_call(
        own_sums_kernel,
        grid=(3,),
        in_specs=[
            pl.BlockSpec((rows, width), lambda p: (0, 0)),
            pl.BlockSpec((1, rows, width), lambda p: (jnp.maximum(p - 1, 0), 0, 0)),
            pl.BlockSpec((1, rows, 2 * width), lambda p: (p, 0, 0)),
            pl.BlockSpec((1, 2, width), lambda p: (p, 0, 0)),
        ],
        out_specs=pl.BlockSpec((1, 2, width), lambda p: (p, 0, 0)),
        out_shape=jax.ShapeDtypeStruct((3, 2, width), jnp.float32),
        compiler_params=pltpu.CompilerParams(vmem_limit_bytes=VMEM_LIMIT),
        cost_estimate=pl.CostEstimate(flops=0, bytes_accessed=6_000_000, transcendentals=0),
        name="own_sums",
    )(gq, own, products, coef)


def all_sums_kernel(near_ref, other_ref, t_ref, coef_ref, own_ref, out_ref):
    member = pl.program_id(0)

    @pl.when(member == 0)
    def _():
        out_ref[0] = own_ref[0]

    @pl.when(member > 0)
    def _():
        for side in range(2):
            grad = near_ref[0].astype(jnp.float32) + other_ref[0].astype(jnp.float32)
            total = add_up(grad, t_ref, coef_ref, side)
            out_ref[0, side : side + 1] = total + own_ref[0, side : side + 1]


def all_sums(near, other, products, coef, own):
    _, rows, width = near.shape
    grads = pl.BlockSpec((1, rows, width), lambda p: (jnp.maximum(p - 1, 0), 0, 0))
    two = pl.BlockSpec((1, 2, width), lambda p: (p, 0, 0))
    return pl.pallas_call(
        all_sums_kernel,
        grid=(3,),
        in_specs=[
            grads,
            grads,
            pl.BlockSpec((1, rows, 2 * width), lambda p: (jnp.maximum(p, 1), 0, 0)),
            two,
            two,
        ],
        out_specs=two,
        out_shape=jax.ShapeDtypeStruct((3, 2, width), jnp.float32),
        compiler_params=pltpu.CompilerParams(vmem_limit_bytes=VMEM_LIMIT),
        cost_estimate=pl.CostEstimate(flops=0, bytes_accessed=5_000_000, transcendentals=0),
        name="all_sums",
    )(near, other, products, coef, own)


def swap_near(block):
    count = lax.axis_size("tm")
    return lax.ppermute(block, "tm", [(i, i ^ 1) for i in range(count)])


def swap_other(block):
    count = lax.axis_size("tm")
    pairs = [(i, i + 1) for i in range(1, count - 1, 2)]
    return lax.ppermute(block, "tm", pairs + [(b, a) for a, b in pairs])


def sum_over_tm(part):
    count = lax.axis_size("tm")
    step = 1
    while step < count:
        part = part + lax.ppermute(part, "tm", [(i, i ^ step) for i in range(count)])
        step *= 2
    return part


def body(tokens, w_qkv, gamma, beta, out_grad, tile_frame, tile_keep):
    up, down, swap = tensor_routes(4)
    half = tokens.shape[0] // 2
    slots = chunk_slots()
    bound, coef = bounds(w_qkv, gamma, beta)
    below, above, beside = send(tokens, up), send(tokens, down), send(tokens, swap)
    below, above, beside = (after(part, bound) for part in (below, above, beside))
    far = [send(below[:half], up), send(above[half:], down)]
    beside_below, beside_above = send(beside, up), send(beside, down)
    beside_far = [send(part, swap) for part in far]
    early = (after(tokens, *far), below, above, beside)
    qkv_sums, mask_sums = early_products(slots, early, w_qkv, bound)
    late = (after(beside_below, qkv_sums), beside_above, *far, *beside_far)
    query, kv = late_qkv(slots, late, w_qkv, bound, qkv_sums)
    kv_near, kv_other = swap_near(kv), swap_other(kv)
    late = (after(late[0], kv),) + late[1:]
    products = late_masks(slots, late, w_qkv, bound, mask_sums)
    out_grad = after(out_grad, products)
    attended, gq, own, for_near, for_other = attend(
        tile_frame, tile_keep, query, kv, kv_near, kv_other, out_grad
    )
    part = own_sums(gq, own, products, coef)
    part = all_sums(swap_near(for_near), swap_other(for_other), products, coef, part)
    totals = sum_over_tm(part)
    return attended, totals[:, 0], totals[:, 1]


def solution(mesh):
    return jax.shard_map(
        body,
        mesh=mesh,
        in_specs=(
            P("tm", "tensor"),
            P(None, None, "tensor"),
            P(None, "tensor"),
            P(None, "tensor"),
            P("tm", "tensor"),
            P(),
            P(),
        ),
        out_specs=(P("tm", "tensor"), P(None, "tensor"), P(None, "tensor")),
        check_vma=False,
    )
```

```python
import functools
import math

import jax
import jax.numpy as jnp
from jax import lax
from jax.experimental import pallas as pl
from jax.experimental.pallas import tpu as pltpu
from jax.sharding import PartitionSpec as P

HEAD = 128
TILE = 384
REACH = 2
WINDOW = 2 * REACH + 1
SCALE = HEAD**-0.5
LOG2E = math.log2(math.e)
NEG = -1e30
MIB = 1024 * 1024

NT = (((1,), (1,)), ((), ()))


def dot(a, b):
    return jnp.dot(a, b, preferred_element_type=jnp.float32)


def dot_nt(a, b):
    return lax.dot_general(a, b, NT, preferred_element_type=jnp.float32)


def tensor_routes(z_count):
    def route(f):
        return [(z * 2 + y, f(z, y)) for z in range(z_count) for y in range(2)]

    up = route(lambda z, y: ((z + 1) % z_count) * 2 + y)
    down = route(lambda z, y: ((z - 1) % z_count) * 2 + y)
    swap = route(lambda z, y: z * 2 + 1 - y)
    return up, down, swap


def send(block, route):
    return lax.ppermute(block, "tensor", route)


def after(value, *others):
    return lax.optimization_barrier((value,) + others)[0]


def chunk_slots():
    me = lax.axis_index("tensor")
    z, y = me // 2, lax.rem(me, 2)
    below, above, far = lax.rem(z + 3, 4), lax.rem(z + 1, 4), lax.rem(z + 2, 4)
    return jnp.stack(
        [
            z * 2 + y,
            below * 2 + y,
            above * 2 + y,
            z * 2 + 1 - y,
            below * 2 + 1 - y,
            above * 2 + 1 - y,
            far * 2 + y,
            far * 2 + 1 - y,
        ]
    ).astype(jnp.int32)


def bounds_kernel(w_ref, gamma_ref, beta_ref, bound_ref, coef_ref):
    w = w_ref[0].astype(jnp.float32)
    col_max = jnp.max(w, axis=0, keepdims=True)
    col_min = jnp.min(w, axis=0, keepdims=True)
    member = pl.program_id(0)
    sig_gamma = jax.nn.sigmoid(gamma_ref[pl.ds(member, 1), :])
    sig_beta = jax.nn.sigmoid(beta_ref[pl.ds(member, 1), :])
    bound_ref[0, 0:1] = sig_gamma * col_max
    bound_ref[0, 1:2] = sig_beta * col_min
    coef_ref[0, 0:1] = sig_gamma * (1.0 - sig_gamma) * col_max
    coef_ref[0, 1:2] = sig_beta * (1.0 - sig_beta) * col_min


def bounds(w_qkv, gamma, beta):
    members, rows, width = w_qkv.shape
    whole = pl.BlockSpec((members, width), lambda p: (0, 0))
    two = pl.BlockSpec((1, 2, width), lambda p: (p, 0, 0))
    return pl.pallas_call(
        bounds_kernel,
        grid=(members,),
        in_specs=[pl.BlockSpec((1, rows, width), lambda p: (p, 0, 0)), whole, whole],
        out_specs=[two, two],
        out_shape=[jax.ShapeDtypeStruct((members, 2, width), jnp.float32)] * 2,
        compiler_params=pltpu.CompilerParams(vmem_limit_bytes=8 * MIB),
        cost_estimate=pl.CostEstimate(flops=0, bytes_accessed=7_000_000, transcendentals=0),
        name="clip_bounds",
    )(w_qkv, gamma, beta)


def load_rows(x_refs, x_scr, depth):
    col = row = 0
    for ref in x_refs:
        rows = ref.shape[0]
        x_scr[row : row + rows, col : col + depth] = ref[...]
        row += rows
        if row == x_scr.shape[0]:
            row, col = 0, col + depth


def clip_rows(w_refs, bound_ref, out_scr):
    upper, lower = bound_ref[0, 0:1], bound_ref[0, 1:2]
    depth, width = w_refs[0].shape[1:]
    for index, ref in enumerate(w_refs):
        block = ref[0].astype(jnp.float32)
        rows = slice(index * depth, (index + 1) * depth)
        out_scr[rows, 0:width] = jnp.minimum(jnp.maximum(block, lower), upper).astype(jnp.bfloat16)


def mask_rows(w_refs, bound_ref, out_scr):
    upper, lower = bound_ref[0, 0:1], bound_ref[0, 1:2]
    depth, width = w_refs[0].shape[1:]
    for index, ref in enumerate(w_refs):
        block = ref[0].astype(jnp.float32)
        rows = slice(index * depth, (index + 1) * depth)
        out_scr[rows, 0:width] = jnp.where(block > upper, 1.0, 0.0).astype(
            jnp.bfloat16
        )
        out_scr[rows, width : 2 * width] = jnp.where(
            block < lower, 1.0, 0.0
        ).astype(jnp.bfloat16)


def early_kernel(fill, slot_ref, *refs):
    x_refs, w_refs, bound_ref = refs[0:4], refs[4:8], refs[8]
    out_ref, x_scr, w_scr = refs[9:]

    @pl.when(pl.program_id(0) == 0)
    def _():
        load_rows(x_refs, x_scr, w_refs[0].shape[1])

    fill(w_refs, bound_ref, w_scr)
    out_ref[0] = dot(x_scr[...], w_scr[...])


def late_qkv_kernel(slot_ref, *refs):
    x_refs, w_refs, bound_ref, sum_ref = refs[0:6], refs[6:10], refs[10], refs[11]
    q_ref, kv_ref, x_scr, w_scr = refs[12:]
    member = pl.program_id(0)

    @pl.when(member == 0)
    def _():
        load_rows(x_refs, x_scr, w_refs[0].shape[1])

    clip_rows(w_refs, bound_ref, w_scr)
    result = sum_ref[0] + dot(x_scr[...], w_scr[...])

    @pl.when(member == 0)
    def _():
        q_ref[...] = (result * (SCALE * LOG2E)).astype(jnp.bfloat16)

    @pl.when(member > 0)
    def _():
        kv_ref[0] = result.astype(jnp.bfloat16)


def late_mask_kernel(slot_ref, *refs):
    x_refs, w_refs, bound_ref, sum_ref = refs[0:6], refs[6:10], refs[10], refs[11]
    out_ref, last_ref, x_scr, w_scr = refs[12:]
    width = w_refs[0].shape[2]

    @pl.when(pl.program_id(0) == 0)
    def _():
        load_rows(x_refs, x_scr, w_refs[0].shape[1])

    mask_rows(w_refs, bound_ref, w_scr)
    result = (sum_ref[0] + dot(x_scr[...], w_scr[...])).astype(jnp.bfloat16)
    out_ref[0] = result
    last_ref[0, 0] = result[:, width - HEAD : width]
    last_ref[0, 1] = result[:, 2 * width - HEAD :]


def product_call(
    kernel, name, vmem, slots, first_slot, chunks, w_qkv, bound, sums, outs, columns
):
    members, full, width = w_qkv.shape
    depth = full // 8
    rows = max(c.shape[0] for c in chunks)
    inner = sum(c.shape[0] for c in chunks) // rows * depth
    count = inner // depth
    w_specs = [
        pl.BlockSpec((1, depth, width), lambda p, s, i=first_slot + i: (p, s[i], 0))
        for i in range(count)
    ]
    return pl.pallas_call(
        kernel,
        grid_spec=pltpu.PrefetchScalarGridSpec(
            num_scalar_prefetch=1,
            grid=(members,),
            in_specs=[pl.BlockSpec(c.shape, lambda p, s: (0, 0)) for c in chunks]
            + w_specs
            + [pl.BlockSpec((1, 2, width), lambda p, s: (p, 0, 0))]
            + [pl.BlockSpec((1,) + a.shape[1:], lambda p, s: (p, 0, 0)) for a in sums],
            out_specs=[spec for spec, _ in outs],
            scratch_shapes=[
                pltpu.VMEM((rows, inner), jnp.bfloat16),
                pltpu.VMEM((inner, columns), jnp.bfloat16),
            ],
        ),
        out_shape=[shape for _, shape in outs],
        compiler_params=pltpu.CompilerParams(vmem_limit_bytes=vmem * MIB),
        cost_estimate=pl.CostEstimate(
            flops=2 * rows * inner * columns * members,
            bytes_accessed=members * inner * width * 2,
            transcendentals=0,
        ),
        name=name,
    )(slots, *chunks, *([w_qkv] * count), bound, *sums)


def members_out(members, rows, columns, dtype):
    spec = pl.BlockSpec((1, rows, columns), lambda p, s: (p, 0, 0))
    return spec, jax.ShapeDtypeStruct((members, rows, columns), dtype)


def early_qkv(slots, chunks, w_qkv, bound):
    members, _, width = w_qkv.shape
    outs = [members_out(members, chunks[0].shape[0], width, jnp.float32)]
    kernel = functools.partial(early_kernel, clip_rows)
    return product_call(
        kernel, "early_qkv", 18, slots, 0, chunks, w_qkv, bound, [], outs, width
    )[0]


def early_masks(slots, chunks, w_qkv, bound):
    members, _, width = w_qkv.shape
    outs = [members_out(members, chunks[0].shape[0], 2 * width, jnp.float32)]
    kernel = functools.partial(early_kernel, mask_rows)
    return product_call(
        kernel, "early_masks", 58, slots, 0, chunks, w_qkv, bound, [], outs, 2 * width
    )[0]


def late_qkv(slots, chunks, w_qkv, bound, sums):
    members, _, width = w_qkv.shape
    rows = chunks[0].shape[0]
    outs = [
        (
            pl.BlockSpec((rows, width), lambda p, s: (0, 0)),
            jax.ShapeDtypeStruct((rows, width), jnp.bfloat16),
        ),
        (
            pl.BlockSpec((1, rows, width), lambda p, s: (jnp.maximum(p - 1, 0), 0, 0)),
            jax.ShapeDtypeStruct((2, rows, width), jnp.bfloat16),
        ),
    ]
    return product_call(
        late_qkv_kernel, "late_qkv", 18, slots, 4, chunks, w_qkv, bound, [sums], outs, width
    )


def late_masks(slots, chunks, w_qkv, bound, sums):
    members, _, width = w_qkv.shape
    rows = chunks[0].shape[0]
    outs = [
        members_out(members, rows, 2 * width, jnp.bfloat16),
        (
            pl.BlockSpec((1, 2, rows, HEAD), lambda p, s: (jnp.maximum(p - 1, 0), 0, 0, 0)),
            jax.ShapeDtypeStruct((2, 2, rows, HEAD), jnp.bfloat16),
        ),
    ]
    return product_call(
        late_mask_kernel, "late_masks", 58, slots, 4, chunks, w_qkv, bound, [sums], outs, 2 * width
    )


def tile_bias(frame_ref, keep_ref, a):
    tiles = frame_ref.shape[0]
    bias = []
    for t in range(WINDOW):
        b = a + (t - REACH)
        b_in = jnp.clip(b, 0, tiles - 1)
        ok = (
            (b >= 0)
            & (b < tiles)
            & (jnp.abs(frame_ref[a] - frame_ref[b_in]) <= 1)
            & (keep_ref[a, t] == 1)
        )
        bias.append(jnp.where(ok, 0.0, NEG))
    return bias


def attend_kernel(returns, frame_ref, keep_ref, *refs):
    q_ref, kv_ref, near_ref, other_ref, grad_ref, high_ref, low_ref, coef_ref = refs[0:8]
    if returns:
        att_ref, sum_ref, for_near_ref, for_other_ref, k_scr, v_scr, gk_scr, gv_scr = refs[8:]
    else:
        t_near_ref, t_other_ref, _, att_ref, sum_ref, k_scr, v_scr, gk_scr, gv_scr = refs[8:]
    position = lax.axis_index("tm")
    count = 2 * TILE
    even = 1 - lax.rem(position, 2)
    near_at = pl.multiple_of(2 * count * even, count)
    other_at = pl.multiple_of(2 * count * (1 - even), count)
    for member, scr in enumerate((k_scr, v_scr)):
        scr[count : 2 * count] = kv_ref[member]
        scr[pl.ds(near_at, count), :] = near_ref[member]
        scr[pl.ds(other_at, count), :] = other_ref[member]
    sums = [[0.0, 0.0] for _ in range(3)]

    def add(member, grad, high, low):
        for side, t in enumerate((high, low)):
            part = grad * t.astype(jnp.float32)
            sums[member][side] += jnp.sum(part, axis=0, keepdims=True)

    for i in range(2):
        bias = tile_bias(frame_ref, keep_ref, position * 2 + i)
        rows = slice(i * TILE, (i + 1) * TILE)
        keys = slice(i * TILE, i * TILE + WINDOW * TILE)
        q = q_ref[rows, :]
        grad = grad_ref[rows, :]
        k = k_scr[keys]
        v = v_scr[keys]
        scores = dot_nt(q, k)
        parts = [scores[:, t * TILE : (t + 1) * TILE] for t in range(WINDOW)]
        peak = functools.reduce(
            jnp.maximum,
            [jnp.max(p, axis=1, keepdims=True) + bias[t] for t, p in enumerate(parts)],
        )
        weights = [jnp.exp2(p - (peak - bias[t])) for t, p in enumerate(parts)]
        total = sum(jnp.sum(w, axis=1, keepdims=True) for w in weights)
        e = jnp.concatenate(weights, axis=1)
        e_low = e.astype(jnp.bfloat16)
        inv = 1.0 / total
        out = dot(e_low, v) * inv
        att_ref[rows, :] = out.astype(jnp.bfloat16)
        grad_wide = grad.astype(jnp.float32)
        delta = jnp.sum(out * grad_wide, axis=1, keepdims=True)
        dprobs = dot_nt(grad, v)
        ds = (e * (dprobs - delta)).astype(jnp.bfloat16)
        gq = dot(ds, k) * (inv * SCALE)
        add(0, gq, high_ref[0, rows, :], low_ref[0, rows, :])
        q_scaled = (q.astype(jnp.float32) * (inv * (1.0 / LOG2E))).astype(jnp.bfloat16)
        grad_scaled = (grad_wide * inv).astype(jnp.bfloat16)
        gk = dot(q_scaled.T, ds)
        gv = dot(grad_scaled.T, e_low)
        if i == 0:
            gk_scr[:, keys] = gk
            gv_scr[:, keys] = gv
        else:
            span, head = WINDOW * TILE, slice(i * TILE, WINDOW * TILE)
            rest = slice(WINDOW * TILE, (WINDOW + 1) * TILE)
            gk_scr[:, head] += gk[:, 0 : span - TILE]
            gv_scr[:, head] += gv[:, 0 : span - TILE]
            gk_scr[:, rest] = gk[:, span - TILE :]
            gv_scr[:, rest] = gv[:, span - TILE :]
    for member, scr in enumerate((gk_scr, gv_scr)):
        own = scr[:, count : 2 * count].T
        for_near = scr[:, pl.ds(near_at, count)].T
        for_other = scr[:, pl.ds(other_at, count)].T
        add(member + 1, own, high_ref[member + 1], low_ref[member + 1])
        if returns:
            for_near_ref[member] = for_near.astype(jnp.bfloat16)
            for_other_ref[member] = for_other.astype(jnp.bfloat16)
        else:
            add(member + 1, for_near, t_near_ref[member, 0], t_near_ref[member, 1])
            add(member + 1, for_other, t_other_ref[member, 0], t_other_ref[member, 1])
    for member in range(3):
        for side in range(2):
            sum_ref[member, side : side + 1] = (
                sums[member][side] * coef_ref[member, side : side + 1]
            )


def attend(tile_frame, tile_keep, first, count, query, kvs, out_grad, products, coef, last=None):
    rows, width = out_grad.shape
    heads = width // HEAD
    span = WINDOW * TILE
    column = pl.BlockSpec((rows, HEAD), lambda h, *_: (0, h + first))
    pair = pl.BlockSpec((2, rows, HEAD), lambda h, *_: (0, 0, h + first))
    halo = pl.BlockSpec((2, rows, HEAD), lambda h, *_: (0, 0, h))
    high = pl.BlockSpec((3, rows, HEAD), lambda h, *_: (0, 0, h + first))
    low = pl.BlockSpec((3, rows, HEAD), lambda h, *_: (0, 0, h + first + heads))
    in_specs = [column, pair, pair, pair, column, high, low]
    in_specs += [pl.BlockSpec((3, 2, HEAD), lambda h, *_: (0, 0, h + first))]
    operands = [tile_frame, tile_keep, query, *kvs, out_grad, products, products, coef]
    out_specs = [column, pl.BlockSpec((3, 2, HEAD), lambda h, *_: (0, 0, h))]
    out_shape = [
        jax.ShapeDtypeStruct((rows, width), jnp.bfloat16),
        jax.ShapeDtypeStruct((3, 2, count * HEAD), jnp.float32),
    ]
    aliases = {}
    if last is None:
        out_specs += [halo, halo]
        out_shape += [jax.ShapeDtypeStruct((2, rows, count * HEAD), jnp.bfloat16)] * 2
    else:
        near, other, attended = last
        in_specs += [pl.BlockSpec((2, 2, rows, HEAD), lambda h, *_: (0, 0, 0, 0))] * 2
        in_specs += [pl.BlockSpec(memory_space=pl.ANY)]
        operands += [near, other, attended]
        aliases = {len(operands) - 1: 0}
    return pl.pallas_call(
        functools.partial(attend_kernel, last is None),
        grid_spec=pltpu.PrefetchScalarGridSpec(
            num_scalar_prefetch=2,
            grid=(count,),
            in_specs=in_specs,
            out_specs=out_specs,
            scratch_shapes=[pltpu.VMEM((6 * TILE, HEAD), jnp.bfloat16)] * 2
            + [pltpu.VMEM((HEAD, 6 * TILE), jnp.float32)] * 2,
        ),
        out_shape=out_shape,
        input_output_aliases=aliases,
        compiler_params=pltpu.CompilerParams(vmem_limit_bytes=34 * MIB),
        cost_estimate=pl.CostEstimate(
            flops=2 * 6 * rows * span * HEAD * count,
            bytes_accessed=5_000_000 * count,
            transcendentals=rows * span * count,
        ),
        name="attend",
    )(*operands)


def all_sums_kernel(near_ref, other_ref, high_ref, low_ref, coef_ref, first_ref, last_ref, out_ref):
    member = pl.program_id(0)
    width = near_ref.shape[2]
    out_ref[0, :, width:] = last_ref[0]

    @pl.when(member == 0)
    def _():
        out_ref[0, :, 0:width] = first_ref[0]

    @pl.when(member > 0)
    def _():
        grad = near_ref[0].astype(jnp.float32) + other_ref[0].astype(jnp.float32)
        for side, t_ref in enumerate((high_ref, low_ref)):
            part = grad * t_ref[0, :, 0:width].astype(jnp.float32)
            total = jnp.sum(part, axis=0, keepdims=True) * coef_ref[0, side : side + 1, 0:width]
            out_ref[0, side : side + 1, 0:width] = total + first_ref[0, side : side + 1]


def all_sums(near, other, products, coef, first, last):
    _, rows, narrow = near.shape
    width = products.shape[2] // 2
    grads = pl.BlockSpec((1, rows, narrow), lambda p: (jnp.maximum(p - 1, 0), 0, 0))
    two = lambda a: pl.BlockSpec((1, 2, a.shape[2]), lambda p: (p, 0, 0))
    return pl.pallas_call(
        all_sums_kernel,
        grid=(3,),
        in_specs=[
            grads,
            grads,
            pl.BlockSpec((1, rows, width), lambda p: (jnp.maximum(p, 1), 0, 0)),
            pl.BlockSpec((1, rows, width), lambda p: (jnp.maximum(p, 1), 0, 1)),
            two(coef),
            two(first),
            two(last),
        ],
        out_specs=two(coef),
        out_shape=jax.ShapeDtypeStruct((3, 2, width), jnp.float32),
        compiler_params=pltpu.CompilerParams(vmem_limit_bytes=16 * MIB),
        cost_estimate=pl.CostEstimate(flops=0, bytes_accessed=5_000_000, transcendentals=0),
        name="all_sums",
    )(near, other, products, products, coef, first, last)


def swap_near(block):
    count = lax.axis_size("tm")
    return lax.ppermute(block, "tm", [(i, i ^ 1) for i in range(count)])


def swap_other(block):
    count = lax.axis_size("tm")
    pairs = [(i, i + 1) for i in range(1, count - 1, 2)]
    return lax.ppermute(block, "tm", pairs + [(b, a) for a, b in pairs])


def sum_over_tm(part):
    count = lax.axis_size("tm")
    step = 1
    while step < count:
        part = part + lax.ppermute(part, "tm", [(i, i ^ step) for i in range(count)])
        step *= 2
    return part


def body(tokens, w_qkv, gamma, beta, out_grad, tile_frame, tile_keep):
    up, down, swap = tensor_routes(4)
    half = tokens.shape[0] // 2
    slots = chunk_slots()
    bound, coef = bounds(w_qkv, gamma, beta)
    below, above, beside = send(tokens, up), send(tokens, down), send(tokens, swap)
    below, above, beside = (after(part, bound) for part in (below, above, beside))
    far = [send(below[:half], up), send(above[half:], down)]
    early = (tokens, below, above, beside)
    qkv_sums = early_qkv(slots, early, w_qkv, bound)
    beside = after(beside, qkv_sums)
    beside_below, beside_above = send(beside, up), send(beside, down)
    beside_far = [send(part, swap) for part in far]
    early = (after(tokens, *far),) + early[1:]
    mask_sums = early_masks(slots, early, w_qkv, bound)
    late = (after(beside_below, mask_sums), beside_above, *far, *beside_far)
    query, kv = late_qkv(slots, late, w_qkv, bound, qkv_sums)
    kvs = (kv, swap_near(kv), swap_other(kv))
    late = (after(late[0], kv),) + late[1:]
    products, last_products = late_masks(slots, late, w_qkv, bound, mask_sums)
    t_other, t_near = swap_other(last_products), swap_near(last_products)
    attended, first, for_near, for_other = attend(
        tile_frame, tile_keep, 0, 2, query, kvs, out_grad, products, coef
    )
    from_other, from_near = swap_other(for_other), swap_near(for_near)
    attended, last = attend(
        tile_frame,
        tile_keep,
        2,
        1,
        query,
        kvs,
        out_grad,
        products,
        coef,
        (t_near, t_other, attended),
    )
    totals = sum_over_tm(all_sums(from_near, from_other, products, coef, first, last))
    return attended, totals[:, 0], totals[:, 1]


def solution(mesh):
    return jax.shard_map(
        body,
        mesh=mesh,
        in_specs=(
            P("tm", "tensor"),
            P(None, None, "tensor"),
            P(None, "tensor"),
            P(None, "tensor"),
            P("tm", "tensor"),
            P(),
            P(),
        ),
        out_specs=(P("tm", "tensor"), P(None, "tensor"), P(None, "tensor")),
        check_vma=False,
    )
```

```python
import functools
import math

import jax
import jax.numpy as jnp
from jax import lax
from jax.experimental import pallas as pl
from jax.experimental.pallas import tpu as pltpu
from jax.sharding import PartitionSpec as P

HEAD = 128
TILE = 384
REACH = 2
WINDOW = 2 * REACH + 1
SCALE = HEAD**-0.5
LOG2E = math.log2(math.e)
NEG = -1e30
MIB = 1024 * 1024
EARLY_COST = 1.0
MASK_COST = 1.0

NT = (((1,), (1,)), ((), ()))


def dot(a, b):
    return jnp.dot(a, b, preferred_element_type=jnp.float32)


def dot_nt(a, b):
    return lax.dot_general(a, b, NT, preferred_element_type=jnp.float32)


def tensor_routes(z_count):
    def route(f):
        return [(z * 2 + y, f(z, y)) for z in range(z_count) for y in range(2)]

    up = route(lambda z, y: ((z + 1) % z_count) * 2 + y)
    down = route(lambda z, y: ((z - 1) % z_count) * 2 + y)
    swap = route(lambda z, y: z * 2 + 1 - y)
    return up, down, swap


def send(block, route):
    return lax.ppermute(block, "tensor", route)


def after(value, *others):
    return lax.optimization_barrier((value,) + others)[0]


def chunk_slots():
    me = lax.axis_index("tensor")
    z, y = me // 2, lax.rem(me, 2)
    below, above, far = lax.rem(z + 3, 4), lax.rem(z + 1, 4), lax.rem(z + 2, 4)
    return jnp.stack(
        [
            z * 2 + y,
            below * 2 + y,
            above * 2 + y,
            z * 2 + 1 - y,
            below * 2 + 1 - y,
            above * 2 + 1 - y,
            far * 2 + y,
            far * 2 + 1 - y,
        ]
    ).astype(jnp.int32)


def bounds_kernel(w_ref, gamma_ref, beta_ref, bound_ref, coef_ref):
    w = w_ref[0].astype(jnp.float32)
    col_max = jnp.max(w, axis=0, keepdims=True)
    col_min = jnp.min(w, axis=0, keepdims=True)
    member = pl.program_id(0)
    sig_gamma = jax.nn.sigmoid(gamma_ref[pl.ds(member, 1), :])
    sig_beta = jax.nn.sigmoid(beta_ref[pl.ds(member, 1), :])
    bound_ref[0, 0:1] = sig_gamma * col_max
    bound_ref[0, 1:2] = sig_beta * col_min
    coef_ref[0, 0:1] = sig_gamma * (1.0 - sig_gamma) * col_max
    coef_ref[0, 1:2] = sig_beta * (1.0 - sig_beta) * col_min


def bounds(w_qkv, gamma, beta):
    members, rows, width = w_qkv.shape
    whole = pl.BlockSpec((members, width), lambda p: (0, 0))
    two = pl.BlockSpec((1, 2, width), lambda p: (p, 0, 0))
    return pl.pallas_call(
        bounds_kernel,
        grid=(members,),
        in_specs=[pl.BlockSpec((1, rows, width), lambda p: (p, 0, 0)), whole, whole],
        out_specs=[two, two],
        out_shape=[jax.ShapeDtypeStruct((members, 2, width), jnp.float32)] * 2,
        compiler_params=pltpu.CompilerParams(vmem_limit_bytes=8 * MIB),
        cost_estimate=pl.CostEstimate(flops=0, bytes_accessed=7_000_000, transcendentals=0),
        name="clip_bounds",
    )(in_hbm(w_qkv), gamma, beta)


def load_rows(x_refs, x_scr, depth):
    col = row = 0
    for ref in x_refs:
        rows = ref.shape[0]
        x_scr[row : row + rows, col : col + depth] = ref[...]
        row += rows
        if row == x_scr.shape[0]:
            row, col = 0, col + depth


def fetch_rows(first_slot, first_member, slot_ref, w_ref, w_buf, w_sem):
    steps, count, depth, _ = w_buf.shape

    def copy(step, index):
        row = pl.multiple_of(slot_ref[first_slot + index] * depth, depth)
        return pltpu.make_async_copy(
            w_ref.at[step + first_member, pl.ds(row, depth), :],
            w_buf.at[step, index],
            w_sem.at[step, index],
        )

    step = pl.program_id(0)

    @pl.when(step == 0)
    def _():
        for other in range(steps):
            for index in range(count):
                copy(other, index).start()

    for index in range(count):
        copy(step, index).wait()


def clip_rows(w_buf, step, bound_ref, out_scr):
    upper, lower = bound_ref[0, 0:1], bound_ref[0, 1:2]
    _, count, depth, _ = w_buf.shape
    for index in range(count):
        block = w_buf[step, index].astype(jnp.float32)
        rows = slice(index * depth, (index + 1) * depth)
        out_scr[rows, :] = jnp.minimum(jnp.maximum(block, lower), upper).astype(jnp.bfloat16)


def mask_rows(w_buf, step, bound_ref, out_scr):
    upper, lower = bound_ref[0, 0:1], bound_ref[0, 1:2]
    _, count, depth, width = w_buf.shape
    for index in range(count):
        block = w_buf[step, index].astype(jnp.float32)
        rows = slice(index * depth, (index + 1) * depth)
        out_scr[rows, 0:width] = jnp.where(block > upper, 1.0, 0.0).astype(jnp.bfloat16)
        out_scr[rows, width : 2 * width] = jnp.where(block < lower, 1.0, 0.0).astype(jnp.bfloat16)


def early_qkv_kernel(slot_ref, *refs):
    x_refs, rest = refs[:-10], refs[-10:]
    w_ref, bound_ref, q_ref, out_ref, x_scr, w_scr, w_buf, w_sem, q_buf, q_sem = rest
    step, steps = pl.program_id(0), w_buf.shape[0]
    fetch_rows(0, 0, slot_ref, w_ref, w_buf, w_sem)

    @pl.when(step == 0)
    def _():
        load_rows(x_refs, x_scr, w_buf.shape[2])

    clip_rows(w_buf, step, bound_ref, w_scr)
    result = dot(x_scr[...], w_scr[...])
    copy = pltpu.make_async_copy(q_buf, q_ref, q_sem)

    @pl.when(step == 0)
    def _():
        q_buf[...] = result
        copy.start()

    @pl.when(step > 0)
    def _():
        out_ref[0] = result

    @pl.when(step == steps - 1)
    def _():
        copy.wait()


def early_mask_kernel(slot_ref, *refs):
    x_refs, rest = refs[:-9], refs[-9:]
    w_ref, bound_ref, out_ref, x_scr, w_scr, w_buf, w_sem, out_buf, out_sem = rest
    step, steps = pl.program_id(0), w_buf.shape[0]
    fetch_rows(0, 0, slot_ref, w_ref, w_buf, w_sem)

    @pl.when(step == 0)
    def _():
        load_rows(x_refs, x_scr, w_buf.shape[2])

    mask_rows(w_buf, step, bound_ref, w_scr)
    out_buf[step] = dot(x_scr[...], w_scr[...])

    def copy(index):
        return pltpu.make_async_copy(out_buf.at[index], out_ref.at[index], out_sem.at[index])

    copy(step).start()

    @pl.when(step == steps - 1)
    def _():
        for index in range(steps):
            copy(index).wait()


def late_kv_kernel(slot_ref, *refs):
    x_refs, rest = refs[:-10], refs[-10:]
    w_ref, bound_ref, sum_ref, kv_ref, x_ref, x_scr, w_scr, w_buf, w_sem, x_sem = rest
    step, steps = pl.program_id(0), w_buf.shape[0]
    fetch_rows(4, 1, slot_ref, w_ref, w_buf, w_sem)
    copy = pltpu.make_async_copy(x_scr, x_ref, x_sem)

    @pl.when(step == 0)
    def _():
        load_rows(x_refs, x_scr, w_buf.shape[2])
        copy.start()

    clip_rows(w_buf, step, bound_ref, w_scr)
    kv_ref[0] = (sum_ref[0] + dot(x_scr[...], w_scr[...])).astype(jnp.bfloat16)

    @pl.when(step == steps - 1)
    def _():
        copy.wait()


def late_rest_kernel(slot_ref, *refs):
    x_ref, w_ref, bound_ref, q_sum_ref, sum_ref, q_ref, out_ref, last_ref = refs[:8]
    x_scr, w_scr, w_buf, w_sem, q_scr, sum_buf, sum_sem, x_sem = refs[8:]
    step, steps = pl.program_id(0), w_buf.shape[0]
    width = w_buf.shape[3]

    def copy(index):
        return pltpu.make_async_copy(sum_ref.at[index], sum_buf.at[index], sum_sem.at[index])

    x_copy = pltpu.make_async_copy(x_ref, x_scr, x_sem)

    @pl.when(step == 0)
    def _():
        x_copy.start()

    fetch_rows(4, 0, slot_ref, w_ref, w_buf, w_sem)

    @pl.when(step == 0)
    def _():
        for index in range(steps):
            copy(index).start()
        clip_rows(w_buf, 0, bound_ref, q_scr)
        x_copy.wait()
        result = q_sum_ref[...] + dot(x_scr[...], q_scr[...])
        q_ref[...] = (result * (SCALE * LOG2E)).astype(jnp.bfloat16)

    mask_rows(w_buf, step, bound_ref, w_scr)
    product = dot(x_scr[...], w_scr[...])
    copy(step).wait()
    result = (sum_buf[step] + product).astype(jnp.bfloat16)
    out_ref[0] = result
    last_ref[0, 0] = result[:, width - HEAD : width]
    last_ref[0, 1] = result[:, 2 * width - HEAD :]


def in_hbm(array):
    return pltpu.with_memory_space_constraint(array, pltpu.HBM)


def product_call(
    kernel, name, vmem, members, columns, slots, chunks, w_qkv, bound, sums, outs, scratch, cost
):
    first, count = members
    _, full, width = w_qkv.shape
    depth = full // 8
    rows = max(c.shape[0] for c in chunks)
    inner = sum(c.shape[0] * c.shape[1] for c in chunks) // rows
    block = lambda a: pl.BlockSpec((1,) + a.shape[1:], lambda p, s: (p + first, 0, 0))
    stays = pl.BlockSpec(memory_space=pltpu.HBM)
    return pl.pallas_call(
        kernel,
        grid_spec=pltpu.PrefetchScalarGridSpec(
            num_scalar_prefetch=1,
            grid=(count,),
            in_specs=[
                stays if len(chunks) == 1 else pl.BlockSpec(c.shape, lambda p, s: (0, 0))
                for c in chunks
            ]
            + [stays, block(bound)]
            + [stays if spec is None else spec for _, spec in sums],
            out_specs=[stays if spec is None else spec for spec, _ in outs],
            scratch_shapes=[
                pltpu.VMEM((rows, inner), jnp.bfloat16),
                pltpu.VMEM((inner, columns), jnp.bfloat16),
                pltpu.VMEM((count, inner // depth, depth, width), jnp.bfloat16),
                pltpu.SemaphoreType.DMA((count, inner // depth)),
            ]
            + scratch,
        ),
        out_shape=[shape for _, shape in outs],
        compiler_params=pltpu.CompilerParams(vmem_limit_bytes=vmem * MIB),
        cost_estimate=pl.CostEstimate(
            flops=int(2 * rows * inner * columns * count * cost),
            bytes_accessed=int(count * inner * width * 2 * cost),
            transcendentals=0,
        ),
        name=name,
    )(slots, *chunks, in_hbm(w_qkv), bound, *[a for a, _ in sums])


def rows_of(chunks):
    return max(c.shape[0] for c in chunks)


def members_out(members, rows, columns, dtype):
    spec = pl.BlockSpec((1, rows, columns), lambda p, s: (p, 0, 0))
    return spec, jax.ShapeDtypeStruct((members, rows, columns), dtype)


def early_qkv(slots, chunks, w_qkv, bound):
    members, _, width = w_qkv.shape
    rows = rows_of(chunks)
    outs = [
        (None, pltpu.HBM((rows, width), jnp.float32)),
        (
            pl.BlockSpec((1, rows, width), lambda p, s: (jnp.maximum(p - 1, 0), 0, 0)),
            jax.ShapeDtypeStruct((members - 1, rows, width), jnp.float32),
        ),
    ]
    scratch = [pltpu.VMEM((rows, width), jnp.float32), pltpu.SemaphoreType.DMA(())]
    return product_call(
        early_qkv_kernel,
        "early_qkv",
        19,
        (0, members),
        width,
        slots,
        chunks,
        w_qkv,
        bound,
        [],
        outs,
        scratch,
        EARLY_COST,
    )


def early_masks(slots, chunks, w_qkv, bound):
    members, _, width = w_qkv.shape
    shape = (members, rows_of(chunks), 2 * width)
    outs = [(None, pltpu.HBM(shape, jnp.float32))]
    scratch = [pltpu.VMEM(shape, jnp.float32), pltpu.SemaphoreType.DMA((members,))]
    return product_call(
        early_mask_kernel,
        "early_masks",
        25,
        (0, members),
        2 * width,
        slots,
        chunks,
        w_qkv,
        bound,
        [],
        outs,
        scratch,
        MASK_COST,
    )[0]


def late_kv(slots, chunks, w_qkv, bound, sums):
    members, full, width = w_qkv.shape
    rows = rows_of(chunks)
    spec = pl.BlockSpec((1, rows, width), lambda p, s: (p, 0, 0))
    outs = [
        members_out(members - 1, rows, width, jnp.bfloat16),
        (None, pltpu.HBM((rows, full // 2), jnp.bfloat16)),
    ]
    return product_call(
        late_kv_kernel,
        "late_kv",
        19,
        (1, members - 1),
        width,
        slots,
        chunks,
        w_qkv,
        bound,
        [(sums, spec)],
        outs,
        [pltpu.SemaphoreType.DMA(())],
        1,
    )


def late_rest(slots, chunks, w_qkv, bound, q_sums, sums):
    members, _, width = w_qkv.shape
    rows = rows_of(chunks)
    outs = [
        (
            pl.BlockSpec((rows, width), lambda p, s: (0, 0)),
            jax.ShapeDtypeStruct((rows, width), jnp.bfloat16),
        ),
        members_out(members, rows, 2 * width, jnp.bfloat16),
        (
            pl.BlockSpec((1, 2, rows, HEAD), lambda p, s: (jnp.maximum(p - 1, 0), 0, 0, 0)),
            jax.ShapeDtypeStruct((2, 2, rows, HEAD), jnp.bfloat16),
        ),
    ]
    scratch = [
        pltpu.VMEM((4 * (w_qkv.shape[1] // 8), width), jnp.bfloat16),
        pltpu.VMEM(sums.shape, jnp.float32),
        pltpu.SemaphoreType.DMA((members,)),
        pltpu.SemaphoreType.DMA(()),
    ]
    q_spec = pl.BlockSpec((rows, width), lambda p, s: (0, 0))
    return product_call(
        late_rest_kernel,
        "late_rest",
        30,
        (0, members),
        2 * width,
        slots,
        chunks,
        w_qkv,
        bound,
        [(in_hbm(q_sums), q_spec), (in_hbm(sums), None)],
        outs,
        scratch,
        1,
    )


def tile_bias(frame_ref, keep_ref, a):
    tiles = frame_ref.shape[0]
    bias = []
    for t in range(WINDOW):
        b = a + (t - REACH)
        b_in = jnp.clip(b, 0, tiles - 1)
        ok = (
            (b >= 0)
            & (b < tiles)
            & (jnp.abs(frame_ref[a] - frame_ref[b_in]) <= 1)
            & (keep_ref[a, t] == 1)
        )
        bias.append(jnp.where(ok, 0.0, NEG))
    return bias


def attend_kernel(returns, frame_ref, keep_ref, *refs):
    q_ref, kv_ref, near_ref, other_ref, grad_ref, high_ref, low_ref, coef_ref = refs[0:8]
    if returns:
        att_ref, sum_ref, for_near_ref, for_other_ref, k_scr, v_scr, gk_scr, gv_scr = refs[8:]
    else:
        t_near_ref, t_other_ref, _, att_ref, sum_ref, k_scr, v_scr, gk_scr, gv_scr = refs[8:]
    position = lax.axis_index("tm")
    count = 2 * TILE
    even = 1 - lax.rem(position, 2)
    near_at = pl.multiple_of(2 * count * even, count)
    other_at = pl.multiple_of(2 * count * (1 - even), count)
    for member, scr in enumerate((k_scr, v_scr)):
        scr[count : 2 * count] = kv_ref[member]
        scr[pl.ds(near_at, count), :] = near_ref[member]
        scr[pl.ds(other_at, count), :] = other_ref[member]
    sums = [[0.0, 0.0] for _ in range(3)]

    def add(member, grad, high, low):
        for side, t in enumerate((high, low)):
            part = grad * t.astype(jnp.float32)
            sums[member][side] += jnp.sum(part, axis=0, keepdims=True)

    for i in range(2):
        bias = tile_bias(frame_ref, keep_ref, position * 2 + i)
        rows = slice(i * TILE, (i + 1) * TILE)
        keys = slice(i * TILE, i * TILE + WINDOW * TILE)
        q = q_ref[rows, :]
        grad = grad_ref[rows, :]
        k = k_scr[keys]
        v = v_scr[keys]
        scores = dot_nt(q, k)
        parts = [scores[:, t * TILE : (t + 1) * TILE] for t in range(WINDOW)]
        peak = functools.reduce(
            jnp.maximum,
            [jnp.max(p, axis=1, keepdims=True) + bias[t] for t, p in enumerate(parts)],
        )
        weights = [jnp.exp2(p - (peak - bias[t])) for t, p in enumerate(parts)]
        total = sum(jnp.sum(w, axis=1, keepdims=True) for w in weights)
        e = jnp.concatenate(weights, axis=1)
        e_low = e.astype(jnp.bfloat16)
        inv = 1.0 / total
        out = dot(e_low, v) * inv
        att_ref[rows, :] = out.astype(jnp.bfloat16)
        grad_wide = grad.astype(jnp.float32)
        delta = jnp.sum(out * grad_wide, axis=1, keepdims=True)
        dprobs = dot_nt(grad, v)
        ds = (e * (dprobs - delta)).astype(jnp.bfloat16)
        gq = dot(ds, k) * (inv * SCALE)
        add(0, gq, high_ref[0, rows, :], low_ref[0, rows, :])
        q_scaled = (q.astype(jnp.float32) * (inv * (1.0 / LOG2E))).astype(jnp.bfloat16)
        grad_scaled = (grad_wide * inv).astype(jnp.bfloat16)
        gk = dot(q_scaled.T, ds)
        gv = dot(grad_scaled.T, e_low)
        if i == 0:
            gk_scr[:, keys] = gk
            gv_scr[:, keys] = gv
        else:
            span, head = WINDOW * TILE, slice(i * TILE, WINDOW * TILE)
            rest = slice(WINDOW * TILE, (WINDOW + 1) * TILE)
            gk_scr[:, head] += gk[:, 0 : span - TILE]
            gv_scr[:, head] += gv[:, 0 : span - TILE]
            gk_scr[:, rest] = gk[:, span - TILE :]
            gv_scr[:, rest] = gv[:, span - TILE :]
    for member, scr in enumerate((gk_scr, gv_scr)):
        own = scr[:, count : 2 * count].T
        for_near = scr[:, pl.ds(near_at, count)].T
        for_other = scr[:, pl.ds(other_at, count)].T
        add(member + 1, own, high_ref[member + 1], low_ref[member + 1])
        if returns:
            for_near_ref[member] = for_near.astype(jnp.bfloat16)
            for_other_ref[member] = for_other.astype(jnp.bfloat16)
        else:
            add(member + 1, for_near, t_near_ref[member, 0], t_near_ref[member, 1])
            add(member + 1, for_other, t_other_ref[member, 0], t_other_ref[member, 1])
    for member in range(3):
        for side in range(2):
            sum_ref[member, side : side + 1] = (
                sums[member][side] * coef_ref[member, side : side + 1]
            )


def attend(tile_frame, tile_keep, first, count, query, kvs, out_grad, products, coef, last=None):
    rows, width = out_grad.shape
    heads = width // HEAD
    span = WINDOW * TILE
    column = pl.BlockSpec((rows, HEAD), lambda h, *_: (0, h + first))
    pair = pl.BlockSpec((2, rows, HEAD), lambda h, *_: (0, 0, h + first))
    halo = pl.BlockSpec((2, rows, HEAD), lambda h, *_: (0, 0, h))
    high = pl.BlockSpec((3, rows, HEAD), lambda h, *_: (0, 0, h + first))
    low = pl.BlockSpec((3, rows, HEAD), lambda h, *_: (0, 0, h + first + heads))
    in_specs = [column, pair, pair, pair, column, high, low]
    in_specs += [pl.BlockSpec((3, 2, HEAD), lambda h, *_: (0, 0, h + first))]
    operands = [tile_frame, tile_keep, query, *kvs, out_grad, products, products, coef]
    out_specs = [column, pl.BlockSpec((3, 2, HEAD), lambda h, *_: (0, 0, h))]
    out_shape = [
        jax.ShapeDtypeStruct((rows, width), jnp.bfloat16),
        jax.ShapeDtypeStruct((3, 2, count * HEAD), jnp.float32),
    ]
    aliases = {}
    if last is None:
        out_specs += [halo, halo]
        out_shape += [jax.ShapeDtypeStruct((2, rows, count * HEAD), jnp.bfloat16)] * 2
    else:
        near, other, attended = last
        in_specs += [pl.BlockSpec((2, 2, rows, HEAD), lambda h, *_: (0, 0, 0, 0))] * 2
        in_specs += [pl.BlockSpec(memory_space=pl.ANY)]
        operands += [near, other, attended]
        aliases = {len(operands) - 1: 0}
    return pl.pallas_call(
        functools.partial(attend_kernel, last is None),
        grid_spec=pltpu.PrefetchScalarGridSpec(
            num_scalar_prefetch=2,
            grid=(count,),
            in_specs=in_specs,
            out_specs=out_specs,
            scratch_shapes=[pltpu.VMEM((6 * TILE, HEAD), jnp.bfloat16)] * 2
            + [pltpu.VMEM((HEAD, 6 * TILE), jnp.float32)] * 2,
        ),
        out_shape=out_shape,
        input_output_aliases=aliases,
        compiler_params=pltpu.CompilerParams(vmem_limit_bytes=34 * MIB),
        cost_estimate=pl.CostEstimate(
            flops=2 * 6 * rows * span * HEAD * count,
            bytes_accessed=5_000_000 * count,
            transcendentals=rows * span * count,
        ),
        name="attend",
    )(*operands)


def all_sums_kernel(near_ref, other_ref, high_ref, low_ref, coef_ref, first_ref, last_ref, out_ref):
    member = pl.program_id(0)
    width = near_ref.shape[2]
    out_ref[0, :, width:] = last_ref[0]

    @pl.when(member == 0)
    def _():
        out_ref[0, :, 0:width] = first_ref[0]

    @pl.when(member > 0)
    def _():
        grad = near_ref[0].astype(jnp.float32) + other_ref[0].astype(jnp.float32)
        for side, t_ref in enumerate((high_ref, low_ref)):
            part = grad * t_ref[0, :, 0:width].astype(jnp.float32)
            total = jnp.sum(part, axis=0, keepdims=True) * coef_ref[0, side : side + 1, 0:width]
            out_ref[0, side : side + 1, 0:width] = total + first_ref[0, side : side + 1]


def all_sums(near, other, products, coef, first, last):
    _, rows, narrow = near.shape
    width = products.shape[2] // 2
    grads = pl.BlockSpec((1, rows, narrow), lambda p: (jnp.maximum(p - 1, 0), 0, 0))
    two = lambda a: pl.BlockSpec((1, 2, a.shape[2]), lambda p: (p, 0, 0))
    return pl.pallas_call(
        all_sums_kernel,
        grid=(3,),
        in_specs=[
            grads,
            grads,
            pl.BlockSpec((1, rows, width), lambda p: (jnp.maximum(p, 1), 0, 0)),
            pl.BlockSpec((1, rows, width), lambda p: (jnp.maximum(p, 1), 0, 1)),
            two(coef),
            two(first),
            two(last),
        ],
        out_specs=two(coef),
        out_shape=jax.ShapeDtypeStruct((3, 2, width), jnp.float32),
        compiler_params=pltpu.CompilerParams(vmem_limit_bytes=16 * MIB),
        cost_estimate=pl.CostEstimate(flops=0, bytes_accessed=5_000_000, transcendentals=0),
        name="all_sums",
    )(near, other, products, products, coef, first, last)


def swap_near(block):
    count = lax.axis_size("tm")
    return lax.ppermute(block, "tm", [(i, i ^ 1) for i in range(count)])


def swap_other(block):
    count = lax.axis_size("tm")
    pairs = [(i, i + 1) for i in range(1, count - 1, 2)]
    return lax.ppermute(block, "tm", pairs + [(b, a) for a, b in pairs])


def sum_over_tm(part):
    count = lax.axis_size("tm")
    swapped = lambda step: lax.ppermute(part, "tm", [(i, i ^ step) for i in range(count)])
    part = part + swapped(1)
    part = part + swapped(8)
    return (part + swapped(2)) + (swapped(4) + swapped(6))


def body(tokens, w_qkv, gamma, beta, out_grad, tile_frame, tile_keep):
    up, down, swap = tensor_routes(4)
    half = tokens.shape[0] // 2
    slots = chunk_slots()
    bound, coef = bounds(w_qkv, gamma, beta)
    below, above, beside = send(tokens, up), send(tokens, down), send(tokens, swap)
    below, above, beside = (after(part, bound) for part in (below, above, beside))
    far = [send(below[:half], up), send(above[half:], down)]
    early = (in_hbm(tokens), below, above, beside)
    q_sums, kv_sums = early_qkv(slots, early, w_qkv, bound)
    beside = after(beside, kv_sums)
    beside_below, beside_above = send(beside, up), send(beside, down)
    beside_far = [send(part, swap) for part in far]
    early = (in_hbm(after(tokens, *far)),) + early[1:]
    mask_sums = early_masks(slots, early, w_qkv, bound)
    late = (after(beside_below, mask_sums), beside_above, *far, *beside_far)
    kv, late = late_kv(slots, late, w_qkv, bound, kv_sums)
    kvs = (kv, swap_near(kv), swap_other(kv))
    query, products, last_products = late_rest(slots, (in_hbm(late),), w_qkv, bound, q_sums, mask_sums)
    t_other, t_near = swap_other(last_products), swap_near(last_products)
    attended, first, for_near, for_other = attend(
        tile_frame, tile_keep, 0, 2, query, kvs, out_grad, products, coef
    )
    from_other, from_near = swap_other(for_other), swap_near(for_near)
    attended, last = attend(
        tile_frame,
        tile_keep,
        2,
        1,
        query,
        kvs,
        out_grad,
        products,
        coef,
        (t_near, t_other, attended),
    )
    totals = sum_over_tm(all_sums(from_near, from_other, products, coef, first, last))
    return attended, totals[:, 0], totals[:, 1]


def solution(mesh):
    return jax.shard_map(
        body,
        mesh=mesh,
        in_specs=(
            P("tm", "tensor"),
            P(None, None, "tensor"),
            P(None, "tensor"),
            P(None, "tensor"),
            P("tm", "tensor"),
            P(),
            P(),
        ),
        out_specs=(P("tm", "tensor"), P(None, "tensor"), P(None, "tensor")),
        check_vma=False,
    )
```

```python
import functools
import math

import jax
import jax.numpy as jnp
from jax import lax
from jax.experimental import pallas as pl
from jax.experimental.pallas import tpu as pltpu
from jax.sharding import PartitionSpec as P

HEAD = 128
TILE = 384
REACH = 2
WINDOW = 2 * REACH + 1
SCALE = HEAD**-0.5
LOG2E = math.log2(math.e)
NEG = -1e30
MIB = 1024 * 1024
EARLY_COST = 1.0
MASK_COST = 1.0

NT = (((1,), (1,)), ((), ()))


def dot(a, b):
    return jnp.dot(a, b, preferred_element_type=jnp.float32)


def dot_nt(a, b):
    return lax.dot_general(a, b, NT, preferred_element_type=jnp.float32)


def tensor_routes(z_count):
    def route(f):
        return [(z * 2 + y, f(z, y)) for z in range(z_count) for y in range(2)]

    up = route(lambda z, y: ((z + 1) % z_count) * 2 + y)
    down = route(lambda z, y: ((z - 1) % z_count) * 2 + y)
    swap = route(lambda z, y: z * 2 + 1 - y)
    return up, down, swap


def send(block, route):
    return lax.ppermute(block, "tensor", route)


def after(value, *others):
    return lax.optimization_barrier((value,) + others)[0]


def chunk_slots():
    me = lax.axis_index("tensor")
    z, y = me // 2, lax.rem(me, 2)
    below, above, far = lax.rem(z + 3, 4), lax.rem(z + 1, 4), lax.rem(z + 2, 4)
    return jnp.stack(
        [
            z * 2 + y,
            below * 2 + y,
            above * 2 + y,
            z * 2 + 1 - y,
            below * 2 + 1 - y,
            above * 2 + 1 - y,
            far * 2 + y,
            far * 2 + 1 - y,
        ]
    ).astype(jnp.int32)


def tile_bias(frame_ref, keep_ref, a):
    tiles = frame_ref.shape[0]
    bias = []
    for t in range(WINDOW):
        b = a + (t - REACH)
        b_in = jnp.clip(b, 0, tiles - 1)
        ok = (
            (b >= 0)
            & (b < tiles)
            & (jnp.abs(frame_ref[a] - frame_ref[b_in]) <= 1)
            & (keep_ref[a, t] == 1)
        )
        bias.append(jnp.where(ok, 0.0, NEG))
    return bias


def bounds_kernel(frame_ref, keep_ref, w_ref, gamma_ref, beta_ref, bound_ref, coef_ref, bias_ref):
    w = w_ref[0].astype(jnp.float32)
    col_max = jnp.max(w, axis=0, keepdims=True)
    col_min = jnp.min(w, axis=0, keepdims=True)
    member = pl.program_id(0)
    sig_gamma = jax.nn.sigmoid(gamma_ref[pl.ds(member, 1), :])
    sig_beta = jax.nn.sigmoid(beta_ref[pl.ds(member, 1), :])
    bound_ref[0, 0:1] = sig_gamma * col_max
    bound_ref[0, 1:2] = sig_beta * col_min
    coef_ref[0, 0:1] = sig_gamma * (1.0 - sig_gamma) * col_max
    coef_ref[0, 1:2] = sig_beta * (1.0 - sig_beta) * col_min
    first = lax.axis_index("tm") * 2
    for i in range(2):
        for t, bias in enumerate(tile_bias(frame_ref, keep_ref, first + i)):
            bias_ref[i, t : t + 1] = jnp.full((1, HEAD), bias, jnp.float32)
        bias_ref[i, WINDOW:] = jnp.zeros((8 - WINDOW, HEAD), jnp.float32)


def bounds(w_qkv, gamma, beta, tile_frame, tile_keep):
    members, rows, width = w_qkv.shape
    whole = pl.BlockSpec((members, width), lambda p, *_: (0, 0))
    two = pl.BlockSpec((1, 2, width), lambda p, *_: (p, 0, 0))
    return pl.pallas_call(
        bounds_kernel,
        grid_spec=pltpu.PrefetchScalarGridSpec(
            num_scalar_prefetch=2,
            grid=(members,),
            in_specs=[pl.BlockSpec((1, rows, width), lambda p, *_: (p, 0, 0)), whole, whole],
            out_specs=[two, two, pl.BlockSpec((2, 8, HEAD), lambda p, *_: (0, 0, 0))],
        ),
        out_shape=[pltpu.HBM((members, 2, width), jnp.float32)] * 2
        + [pltpu.HBM((2, 8, HEAD), jnp.float32)],
        compiler_params=pltpu.CompilerParams(vmem_limit_bytes=8 * MIB),
        cost_estimate=pl.CostEstimate(flops=0, bytes_accessed=7_000_000, transcendentals=0),
        name="clip_bounds",
    )(tile_frame, tile_keep, in_hbm(w_qkv), gamma, beta)


def load_rows(x_refs, x_scr, depth):
    col = row = 0
    for ref in x_refs:
        rows = ref.shape[0]
        x_scr[row : row + rows, col : col + depth] = ref[...]
        row += rows
        if row == x_scr.shape[0]:
            row, col = 0, col + depth


def fetch_rows(first_slot, first_member, load, slot_ref, w_ref, bound_ref, w_buf, w_sem, *bound):
    steps, count, depth, _ = w_buf.shape
    bound_copy = pltpu.make_async_copy(bound_ref, *bound)

    def copy(step, index):
        row = pl.multiple_of(slot_ref[first_slot + index] * depth, depth)
        return pltpu.make_async_copy(
            w_ref.at[step + first_member, pl.ds(row, depth), :],
            w_buf.at[step, index],
            w_sem.at[step, index],
        )

    step = pl.program_id(0)

    @pl.when(step == 0)
    def _():
        bound_copy.start()
        for index in range(count):
            copy(0, index).start()
        load()
        bound_copy.wait()

    for index in range(count):
        copy(step, index).wait()

    @pl.when(step == 0)
    def _():
        for other in range(1, steps):
            for index in range(count):
                copy(other, index).start()


def clip_rows(w_buf, step, member, bound_buf, out_scr):
    upper, lower = bound_buf[member, 0:1], bound_buf[member, 1:2]
    _, count, depth, _ = w_buf.shape
    for index in range(count):
        block = w_buf[step, index].astype(jnp.float32)
        rows = slice(index * depth, (index + 1) * depth)
        out_scr[rows, :] = jnp.minimum(jnp.maximum(block, lower), upper).astype(jnp.bfloat16)


def mask_rows(w_buf, step, member, bound_buf, out_scr):
    upper, lower = bound_buf[member, 0:1], bound_buf[member, 1:2]
    _, count, depth, width = w_buf.shape
    for index in range(count):
        block = w_buf[step, index].astype(jnp.float32)
        rows = slice(index * depth, (index + 1) * depth)
        out_scr[rows, 0:width] = jnp.where(block > upper, 1.0, 0.0).astype(jnp.bfloat16)
        out_scr[rows, width : 2 * width] = jnp.where(block < lower, 1.0, 0.0).astype(jnp.bfloat16)


def early_qkv_kernel(slot_ref, *refs):
    x_refs, rest = refs[:-12], refs[-12:]
    w_ref, bound_ref, q_ref, out_ref, x_scr, w_scr = rest[:6]
    w_buf, w_sem, bound_buf, bound_sem, q_buf, q_sem = rest[6:]
    step, steps = pl.program_id(0), w_buf.shape[0]
    load = lambda: load_rows(x_refs, x_scr, w_buf.shape[2])
    fetch_rows(0, 0, load, slot_ref, w_ref, bound_ref, w_buf, w_sem, bound_buf, bound_sem)
    clip_rows(w_buf, step, step, bound_buf, w_scr)
    result = dot(x_scr[...], w_scr[...])
    copy = pltpu.make_async_copy(q_buf, q_ref, q_sem)

    @pl.when(step == 0)
    def _():
        q_buf[...] = result
        copy.start()

    @pl.when(step > 0)
    def _():
        out_ref[0] = result

    @pl.when(step == steps - 1)
    def _():
        copy.wait()


def early_mask_kernel(slot_ref, *refs):
    x_refs, rest = refs[:-11], refs[-11:]
    w_ref, bound_ref, out_ref, x_scr, w_scr, w_buf, w_sem = rest[:7]
    bound_buf, bound_sem, out_buf, out_sem = rest[7:]
    step, steps = pl.program_id(0), w_buf.shape[0]
    load = lambda: load_rows(x_refs, x_scr, w_buf.shape[2])
    fetch_rows(0, 0, load, slot_ref, w_ref, bound_ref, w_buf, w_sem, bound_buf, bound_sem)
    mask_rows(w_buf, step, step, bound_buf, w_scr)
    out_buf[step] = dot(x_scr[...], w_scr[...]).astype(jnp.bfloat16)

    def copy(index):
        return pltpu.make_async_copy(out_buf.at[index], out_ref.at[index], out_sem.at[index])

    copy(step).start()

    @pl.when(step == steps - 1)
    def _():
        for index in range(steps):
            copy(index).wait()


def late_kv_kernel(slot_ref, *refs):
    x_refs, rest = refs[:-12], refs[-12:]
    w_ref, bound_ref, sum_ref, kv_ref, x_ref, x_scr, w_scr = rest[:7]
    w_buf, w_sem, bound_buf, bound_sem, x_sem = rest[7:]
    step, steps = pl.program_id(0), w_buf.shape[0]
    load = lambda: load_rows(x_refs, x_scr, w_buf.shape[2])
    fetch_rows(4, 1, load, slot_ref, w_ref, bound_ref, w_buf, w_sem, bound_buf, bound_sem)
    copy = pltpu.make_async_copy(x_scr, x_ref, x_sem)

    @pl.when(step == 0)
    def _():
        copy.start()

    clip_rows(w_buf, step, step + 1, bound_buf, w_scr)
    kv_ref[0] = (sum_ref[0] + dot(x_scr[...], w_scr[...])).astype(jnp.bfloat16)

    @pl.when(step == steps - 1)
    def _():
        copy.wait()


def late_rest_kernel(slot_ref, *refs):
    x_ref, w_ref, bound_ref, q_sum_ref, sum_ref, q_ref, out_ref, last_ref = refs[:8]
    x_scr, w_scr, w_buf, w_sem, bound_buf, bound_sem = refs[8:14]
    q_scr, q_buf, q_sem, sum_buf, sum_sem, x_sem = refs[14:]
    step, steps = pl.program_id(0), w_buf.shape[0]
    width = w_buf.shape[3]

    def copy(index):
        return pltpu.make_async_copy(sum_ref.at[index], sum_buf.at[index], sum_sem.at[index])

    x_copy = pltpu.make_async_copy(x_ref, x_scr, x_sem)
    q_copy = pltpu.make_async_copy(q_sum_ref, q_buf, q_sem)
    load = lambda: x_copy.start()
    fetch_rows(4, 0, load, slot_ref, w_ref, bound_ref, w_buf, w_sem, bound_buf, bound_sem)

    @pl.when(step == 0)
    def _():
        q_copy.start()
        for index in range(steps):
            copy(index).start()
        clip_rows(w_buf, 0, 0, bound_buf, q_scr)
        x_copy.wait()
        product = dot(x_scr[...], q_scr[...])
        q_copy.wait()
        q_ref[...] = ((q_buf[...] + product) * (SCALE * LOG2E)).astype(jnp.bfloat16)

    mask_rows(w_buf, step, step, bound_buf, w_scr)
    product = dot(x_scr[...], w_scr[...])
    copy(step).wait()
    result = (sum_buf[step].astype(jnp.float32) + product).astype(jnp.bfloat16)
    out_ref[0] = result
    last_ref[0, 0] = result[:, width - HEAD : width]
    last_ref[0, 1] = result[:, 2 * width - HEAD :]


def in_hbm(array):
    return pltpu.with_memory_space_constraint(array, pltpu.HBM)


def product_call(
    kernel, name, vmem, members, columns, slots, chunks, w_qkv, bound, sums, outs, scratch, cost
):
    _, count = members
    _, full, width = w_qkv.shape
    depth = full // 8
    rows = max(c.shape[0] for c in chunks)
    inner = sum(c.shape[0] * c.shape[1] for c in chunks) // rows
    stays = pl.BlockSpec(memory_space=pltpu.HBM)
    return pl.pallas_call(
        kernel,
        grid_spec=pltpu.PrefetchScalarGridSpec(
            num_scalar_prefetch=1,
            grid=(count,),
            in_specs=[
                stays if len(chunks) == 1 else pl.BlockSpec(c.shape, lambda p, s: (0, 0))
                for c in chunks
            ]
            + [stays, stays]
            + [stays if spec is None else spec for _, spec in sums],
            out_specs=[stays if spec is None else spec for spec, _ in outs],
            scratch_shapes=[
                pltpu.VMEM((rows, inner), jnp.bfloat16),
                pltpu.VMEM((inner, columns), jnp.bfloat16),
                pltpu.VMEM((count, inner // depth, depth, width), jnp.bfloat16),
                pltpu.SemaphoreType.DMA((count, inner // depth)),
                pltpu.VMEM(bound.shape, jnp.float32),
                pltpu.SemaphoreType.DMA(()),
            ]
            + scratch,
        ),
        out_shape=[shape for _, shape in outs],
        compiler_params=pltpu.CompilerParams(vmem_limit_bytes=vmem * MIB),
        cost_estimate=pl.CostEstimate(
            flops=int(2 * rows * inner * columns * count * cost),
            bytes_accessed=int(count * inner * width * 2 * cost),
            transcendentals=0,
        ),
        name=name,
    )(slots, *chunks, in_hbm(w_qkv), in_hbm(bound), *[a for a, _ in sums])


def rows_of(chunks):
    return max(c.shape[0] for c in chunks)


def members_out(members, rows, columns, dtype):
    spec = pl.BlockSpec((1, rows, columns), lambda p, s: (p, 0, 0))
    return spec, jax.ShapeDtypeStruct((members, rows, columns), dtype)


def early_qkv(slots, chunks, w_qkv, bound):
    members, _, width = w_qkv.shape
    rows = rows_of(chunks)
    outs = [
        (None, pltpu.HBM((rows, width), jnp.float32)),
        (
            pl.BlockSpec((1, rows, width), lambda p, s: (jnp.maximum(p - 1, 0), 0, 0)),
            jax.ShapeDtypeStruct((members - 1, rows, width), jnp.float32),
        ),
    ]
    scratch = [pltpu.VMEM((rows, width), jnp.float32), pltpu.SemaphoreType.DMA(())]
    return product_call(
        early_qkv_kernel,
        "early_qkv",
        19,
        (0, members),
        width,
        slots,
        chunks,
        w_qkv,
        bound,
        [],
        outs,
        scratch,
        EARLY_COST,
    )


def early_masks(slots, chunks, w_qkv, bound):
    members, _, width = w_qkv.shape
    shape = (members, rows_of(chunks), 2 * width)
    outs = [(None, pltpu.HBM(shape, jnp.bfloat16))]
    scratch = [pltpu.VMEM(shape, jnp.bfloat16), pltpu.SemaphoreType.DMA((members,))]
    return product_call(
        early_mask_kernel,
        "early_masks",
        25,
        (0, members),
        2 * width,
        slots,
        chunks,
        w_qkv,
        bound,
        [],
        outs,
        scratch,
        MASK_COST,
    )[0]


def late_kv(slots, chunks, w_qkv, bound, sums):
    members, full, width = w_qkv.shape
    rows = rows_of(chunks)
    spec = pl.BlockSpec((1, rows, width), lambda p, s: (p, 0, 0))
    outs = [
        members_out(members - 1, rows, width, jnp.bfloat16),
        (None, pltpu.HBM((rows, full // 2), jnp.bfloat16)),
    ]
    return product_call(
        late_kv_kernel,
        "late_kv",
        19,
        (1, members - 1),
        width,
        slots,
        chunks,
        w_qkv,
        bound,
        [(sums, spec)],
        outs,
        [pltpu.SemaphoreType.DMA(())],
        1,
    )


def late_rest(slots, chunks, w_qkv, bound, q_sums, sums):
    members, _, width = w_qkv.shape
    rows = rows_of(chunks)
    outs = [
        (
            pl.BlockSpec((rows, width), lambda p, s: (0, 0)),
            jax.ShapeDtypeStruct((rows, width), jnp.bfloat16),
        ),
        members_out(members, rows, 2 * width, jnp.bfloat16),
        (
            pl.BlockSpec((1, 2, rows, HEAD), lambda p, s: (jnp.maximum(p - 1, 0), 0, 0, 0)),
            jax.ShapeDtypeStruct((2, 2, rows, HEAD), jnp.bfloat16),
        ),
    ]
    scratch = [
        pltpu.VMEM((4 * (w_qkv.shape[1] // 8), width), jnp.bfloat16),
        pltpu.VMEM((rows, width), jnp.float32),
        pltpu.SemaphoreType.DMA(()),
        pltpu.VMEM(sums.shape, sums.dtype),
        pltpu.SemaphoreType.DMA((members,)),
        pltpu.SemaphoreType.DMA(()),
    ]
    return product_call(
        late_rest_kernel,
        "late_rest",
        30,
        (0, members),
        2 * width,
        slots,
        chunks,
        w_qkv,
        bound,
        [(in_hbm(q_sums), None), (in_hbm(sums), None)],
        outs,
        scratch,
        1,
    )


def attend_kernel(returns, *refs):
    bias_ref, q_ref, kv_ref, near_ref, other_ref, grad_ref, high_ref, low_ref, coef_ref = refs[0:9]
    if returns:
        att_ref, sum_ref, for_near_ref, for_other_ref, k_scr, v_scr, gk_scr, gv_scr = refs[9:]
    else:
        t_near_ref, t_other_ref, _, att_ref, sum_ref, k_scr, v_scr, gk_scr, gv_scr = refs[9:]
    position = lax.axis_index("tm")
    count = 2 * TILE
    even = 1 - lax.rem(position, 2)
    near_at = pl.multiple_of(2 * count * even, count)
    other_at = pl.multiple_of(2 * count * (1 - even), count)
    for member, scr in enumerate((k_scr, v_scr)):
        scr[count : 2 * count] = kv_ref[member]
        scr[pl.ds(near_at, count), :] = near_ref[member]
        scr[pl.ds(other_at, count), :] = other_ref[member]
    sums = [[0.0, 0.0] for _ in range(3)]

    def add(member, grad, high, low):
        for side, t in enumerate((high, low)):
            part = grad * t.astype(jnp.float32)
            sums[member][side] += jnp.sum(part, axis=0, keepdims=True)

    for i in range(2):
        bias = [bias_ref[i, t : t + 1, 0:1] for t in range(WINDOW)]
        rows = slice(i * TILE, (i + 1) * TILE)
        keys = slice(i * TILE, i * TILE + WINDOW * TILE)
        q = q_ref[rows, :]
        grad = grad_ref[rows, :]
        k = k_scr[keys]
        v = v_scr[keys]
        scores = dot_nt(q, k)
        parts = [scores[:, t * TILE : (t + 1) * TILE] for t in range(WINDOW)]
        peak = functools.reduce(
            jnp.maximum,
            [jnp.max(p, axis=1, keepdims=True) + bias[t] for t, p in enumerate(parts)],
        )
        weights = [jnp.exp2(p - (peak - bias[t])) for t, p in enumerate(parts)]
        total = sum(jnp.sum(w, axis=1, keepdims=True) for w in weights)
        e = jnp.concatenate(weights, axis=1)
        e_low = e.astype(jnp.bfloat16)
        inv = 1.0 / total
        out = dot(e_low, v) * inv
        att_ref[rows, :] = out.astype(jnp.bfloat16)
        grad_wide = grad.astype(jnp.float32)
        delta = jnp.sum(out * grad_wide, axis=1, keepdims=True)
        dprobs = dot_nt(grad, v)
        ds = (e * (dprobs - delta)).astype(jnp.bfloat16)
        gq = dot(ds, k) * (inv * SCALE)
        add(0, gq, high_ref[0, rows, :], low_ref[0, rows, :])
        q_scaled = (q.astype(jnp.float32) * (inv * (1.0 / LOG2E))).astype(jnp.bfloat16)
        grad_scaled = (grad_wide * inv).astype(jnp.bfloat16)
        gk = dot(q_scaled.T, ds)
        gv = dot(grad_scaled.T, e_low)
        if i == 0:
            gk_scr[:, keys] = gk
            gv_scr[:, keys] = gv
        else:
            span, head = WINDOW * TILE, slice(i * TILE, WINDOW * TILE)
            rest = slice(WINDOW * TILE, (WINDOW + 1) * TILE)
            gk_scr[:, head] += gk[:, 0 : span - TILE]
            gv_scr[:, head] += gv[:, 0 : span - TILE]
            gk_scr[:, rest] = gk[:, span - TILE :]
            gv_scr[:, rest] = gv[:, span - TILE :]
    for member, scr in enumerate((gk_scr, gv_scr)):
        own = scr[:, count : 2 * count].T
        for_near = scr[:, pl.ds(near_at, count)].T
        for_other = scr[:, pl.ds(other_at, count)].T
        add(member + 1, own, high_ref[member + 1], low_ref[member + 1])
        if returns:
            for_near_ref[member] = for_near.astype(jnp.bfloat16)
            for_other_ref[member] = for_other.astype(jnp.bfloat16)
        else:
            add(member + 1, for_near, t_near_ref[member, 0], t_near_ref[member, 1])
            add(member + 1, for_other, t_other_ref[member, 0], t_other_ref[member, 1])
    for member in range(3):
        for side in range(2):
            sum_ref[member, side : side + 1] = (
                sums[member][side] * coef_ref[member, side : side + 1]
            )


def attend(bias, first, count, query, kvs, out_grad, products, coef, last=None):
    rows, width = out_grad.shape
    heads = width // HEAD
    span = WINDOW * TILE
    column = pl.BlockSpec((rows, HEAD), lambda h: (0, h + first))
    pair = pl.BlockSpec((2, rows, HEAD), lambda h: (0, 0, h + first))
    halo = pl.BlockSpec((2, rows, HEAD), lambda h: (0, 0, h))
    high = pl.BlockSpec((3, rows, HEAD), lambda h: (0, 0, h + first))
    low = pl.BlockSpec((3, rows, HEAD), lambda h: (0, 0, h + first + heads))
    in_specs = [pl.BlockSpec((2, 8, HEAD), lambda h: (0, 0, 0))]
    in_specs += [column, pair, pair, pair, column, high, low]
    in_specs += [pl.BlockSpec((3, 2, HEAD), lambda h: (0, 0, h + first))]
    operands = [in_hbm(bias), query, *kvs, out_grad, products, products, in_hbm(coef)]
    out_specs = [column, pl.BlockSpec((3, 2, HEAD), lambda h: (0, 0, h))]
    out_shape = [
        jax.ShapeDtypeStruct((rows, width), jnp.bfloat16),
        jax.ShapeDtypeStruct((3, 2, count * HEAD), jnp.float32),
    ]
    aliases = {}
    if last is None:
        out_specs += [halo, halo]
        out_shape += [jax.ShapeDtypeStruct((2, rows, count * HEAD), jnp.bfloat16)] * 2
    else:
        near, other, attended = last
        in_specs += [pl.BlockSpec((2, 2, rows, HEAD), lambda h: (0, 0, 0, 0))] * 2
        in_specs += [pl.BlockSpec(memory_space=pl.ANY)]
        operands += [near, other, attended]
        aliases = {len(operands) - 1: 0}
    return pl.pallas_call(
        functools.partial(attend_kernel, last is None),
        grid=(count,),
        in_specs=in_specs,
        out_specs=out_specs,
        scratch_shapes=[pltpu.VMEM((6 * TILE, HEAD), jnp.bfloat16)] * 2
        + [pltpu.VMEM((HEAD, 6 * TILE), jnp.float32)] * 2,
        out_shape=out_shape,
        input_output_aliases=aliases,
        compiler_params=pltpu.CompilerParams(vmem_limit_bytes=34 * MIB),
        cost_estimate=pl.CostEstimate(
            flops=2 * 6 * rows * span * HEAD * count,
            bytes_accessed=5_000_000 * count,
            transcendentals=rows * span * count,
        ),
        name="attend",
    )(*operands)


def all_sums_kernel(near_ref, other_ref, high_ref, low_ref, coef_ref, first_ref, last_ref, out_ref):
    member = pl.program_id(0)
    width = near_ref.shape[2]
    out_ref[0, :, width:] = last_ref[0]

    @pl.when(member == 0)
    def _():
        out_ref[0, :, 0:width] = first_ref[0]

    @pl.when(member > 0)
    def _():
        grad = near_ref[0].astype(jnp.float32) + other_ref[0].astype(jnp.float32)
        for side, t_ref in enumerate((high_ref, low_ref)):
            part = grad * t_ref[0, :, 0:width].astype(jnp.float32)
            total = jnp.sum(part, axis=0, keepdims=True) * coef_ref[0, side : side + 1, 0:width]
            out_ref[0, side : side + 1, 0:width] = total + first_ref[0, side : side + 1]


def all_sums(near, other, products, coef, first, last):
    _, rows, narrow = near.shape
    width = products.shape[2] // 2
    grads = pl.BlockSpec((1, rows, narrow), lambda p: (jnp.maximum(p - 1, 0), 0, 0))
    two = lambda a: pl.BlockSpec((1, 2, a.shape[2]), lambda p: (p, 0, 0))
    return pl.pallas_call(
        all_sums_kernel,
        grid=(3,),
        in_specs=[
            grads,
            grads,
            pl.BlockSpec((1, rows, width), lambda p: (jnp.maximum(p, 1), 0, 0)),
            pl.BlockSpec((1, rows, width), lambda p: (jnp.maximum(p, 1), 0, 1)),
            two(coef),
            two(first),
            two(last),
        ],
        out_specs=two(coef),
        out_shape=jax.ShapeDtypeStruct((3, 2, width), jnp.float32),
        compiler_params=pltpu.CompilerParams(vmem_limit_bytes=16 * MIB),
        cost_estimate=pl.CostEstimate(flops=0, bytes_accessed=5_000_000, transcendentals=0),
        name="all_sums",
    )(near, other, products, products, coef, first, last)


def swap_near(block):
    count = lax.axis_size("tm")
    return lax.ppermute(block, "tm", [(i, i ^ 1) for i in range(count)])


def swap_other(block):
    count = lax.axis_size("tm")
    pairs = [(i, i + 1) for i in range(1, count - 1, 2)]
    return lax.ppermute(block, "tm", pairs + [(b, a) for a, b in pairs])


def sum_over_tm(part):
    count = lax.axis_size("tm")
    swapped = lambda step: lax.ppermute(part, "tm", [(i, i ^ step) for i in range(count)])
    part = part + swapped(1)
    part = part + swapped(8)
    return (part + swapped(2)) + (swapped(4) + swapped(6))


def body(tokens, w_qkv, gamma, beta, out_grad, tile_frame, tile_keep):
    up, down, swap = tensor_routes(4)
    half = tokens.shape[0] // 2
    slots = chunk_slots()
    bound, coef, bias = bounds(w_qkv, gamma, beta, tile_frame, tile_keep)
    below, above, beside = send(tokens, up), send(tokens, down), send(tokens, swap)
    below, above, beside = (after(part, bound) for part in (below, above, beside))
    far = [send(below[:half], up), send(above[half:], down)]
    early = (in_hbm(tokens), below, above, beside)
    q_sums, kv_sums = early_qkv(slots, early, w_qkv, bound)
    beside = after(beside, kv_sums)
    beside_below, beside_above = send(beside, up), send(beside, down)
    beside_far = [send(part, swap) for part in far]
    early = (in_hbm(after(tokens, *far)),) + early[1:]
    mask_sums = early_masks(slots, early, w_qkv, bound)
    late = (after(beside_below, mask_sums), beside_above, *far, *beside_far)
    kv, late = late_kv(slots, late, w_qkv, bound, kv_sums)
    kvs = (kv, swap_near(kv), swap_other(kv))
    query, products, last_products = late_rest(slots, (in_hbm(late),), w_qkv, bound, q_sums, mask_sums)
    t_other, t_near = swap_other(last_products), swap_near(last_products)
    attended, first, for_near, for_other = attend(
        bias, 0, 2, query, kvs, out_grad, products, coef
    )
    from_other, from_near = swap_other(for_other), swap_near(for_near)
    attended, last = attend(
        bias,
        2,
        1,
        query,
        kvs,
        out_grad,
        products,
        coef,
        (t_near, t_other, attended),
    )
    totals = sum_over_tm(all_sums(from_near, from_other, products, coef, first, last))
    return attended, totals[:, 0], totals[:, 1]


def solution(mesh):
    return jax.shard_map(
        body,
        mesh=mesh,
        in_specs=(
            P("tm", "tensor"),
            P(None, None, "tensor"),
            P(None, "tensor"),
            P(None, "tensor"),
            P("tm", "tensor"),
            P(),
            P(),
        ),
        out_specs=(P("tm", "tensor"), P(None, "tensor"), P(None, "tensor")),
        check_vma=False,
    )
```

```python
import functools
import math

import jax
import jax.numpy as jnp
from jax import lax
from jax.experimental import pallas as pl
from jax.experimental.pallas import tpu as pltpu
from jax.sharding import PartitionSpec as P

HEAD = 128
TILE = 384
REACH = 2
WINDOW = 2 * REACH + 1
SCALE = HEAD**-0.5
LOG2E = math.log2(math.e)
NEG = -1e30
MIB = 1024 * 1024

NT = (((1,), (1,)), ((), ()))


def dot(a, b):
    return jnp.dot(a, b, preferred_element_type=jnp.float32)


def dot_nt(a, b):
    return lax.dot_general(a, b, NT, preferred_element_type=jnp.float32)


def tensor_routes(z_count):
    def route(f):
        return [(z * 2 + y, f(z, y)) for z in range(z_count) for y in range(2)]

    up = route(lambda z, y: ((z + 1) % z_count) * 2 + y)
    down = route(lambda z, y: ((z - 1) % z_count) * 2 + y)
    swap = route(lambda z, y: z * 2 + 1 - y)
    return up, down, swap


def send(block, route):
    return lax.ppermute(block, "tensor", route)


def after(value, *others):
    return lax.optimization_barrier((value,) + others)[0]


def chunk_slots():
    me = lax.axis_index("tensor")
    z, y = me // 2, lax.rem(me, 2)
    below, above, far = lax.rem(z + 3, 4), lax.rem(z + 1, 4), lax.rem(z + 2, 4)
    return jnp.stack(
        [
            z * 2 + y,
            below * 2 + y,
            above * 2 + y,
            z * 2 + 1 - y,
            below * 2 + 1 - y,
            above * 2 + 1 - y,
            far * 2 + y,
            far * 2 + 1 - y,
        ]
    ).astype(jnp.int32)


def tile_bias(frame_ref, keep_ref, a):
    tiles = frame_ref.shape[0]
    bias = []
    for t in range(WINDOW):
        b = a + (t - REACH)
        b_in = jnp.clip(b, 0, tiles - 1)
        ok = (
            (b >= 0)
            & (b < tiles)
            & (jnp.abs(frame_ref[a] - frame_ref[b_in]) <= 1)
            & (keep_ref[t, a] == 1)
        )
        bias.append(jnp.where(ok, 0.0, NEG))
    return bias


def bounds_kernel(frame_ref, keep_ref, slot_ref, w_ref, gamma_ref, beta_ref, *outs):
    bound_ref, coef_ref, bias_ref, clipped_ref = outs
    w = w_ref[0].astype(jnp.float32)
    col_max = jnp.max(w, axis=0, keepdims=True)
    col_min = jnp.min(w, axis=0, keepdims=True)
    member = pl.program_id(0)
    sig_gamma = jax.nn.sigmoid(gamma_ref[pl.ds(member, 1), :])
    sig_beta = jax.nn.sigmoid(beta_ref[pl.ds(member, 1), :])
    upper = sig_gamma * col_max
    lower = sig_beta * col_min
    bound_ref[0, 0:1] = upper
    bound_ref[0, 1:2] = lower
    coef_ref[0, 0:1] = sig_gamma * (1.0 - sig_gamma) * col_max
    coef_ref[0, 1:2] = sig_beta * (1.0 - sig_beta) * col_min
    first = lax.axis_index("tm") * 2
    for i in range(2):
        for t, bias in enumerate(tile_bias(frame_ref, keep_ref, first + i)):
            bias_ref[i, t : t + 1] = jnp.full((1, HEAD), bias, jnp.float32)
        bias_ref[i, WINDOW:] = jnp.zeros((8 - WINDOW, HEAD), jnp.float32)
    _, count, depth, _ = clipped_ref.shape
    for slot in range(count):
        row = pl.multiple_of(slot_ref[slot] * depth, depth)
        block = w_ref[0, pl.ds(row, depth), :].astype(jnp.float32)
        clipped = jnp.minimum(jnp.maximum(block, lower), upper)
        clipped_ref[0, slot] = clipped.astype(jnp.bfloat16)


def bounds(w_qkv, gamma, beta, tile_frame, tile_keep, slots):
    members, rows, width = w_qkv.shape
    sorted_shape = (members, 8, rows // 8, width)
    whole = pl.BlockSpec((members, width), lambda p, *_: (0, 0))
    two = pl.BlockSpec((1, 2, width), lambda p, *_: (p, 0, 0))
    return pl.pallas_call(
        bounds_kernel,
        grid_spec=pltpu.PrefetchScalarGridSpec(
            num_scalar_prefetch=3,
            grid=(members,),
            in_specs=[pl.BlockSpec((1, rows, width), lambda p, *_: (p, 0, 0)), whole, whole],
            out_specs=[
                two,
                two,
                pl.BlockSpec((2, 8, HEAD), lambda p, *_: (0, 0, 0)),
                pl.BlockSpec((1,) + sorted_shape[1:], lambda p, *_: (p, 0, 0, 0)),
            ],
        ),
        out_shape=[pltpu.HBM((members, 2, width), jnp.float32)] * 2
        + [pltpu.HBM((2, 8, HEAD), jnp.float32), pltpu.HBM(sorted_shape, jnp.bfloat16)],
        compiler_params=pltpu.CompilerParams(vmem_limit_bytes=16 * MIB),
        cost_estimate=pl.CostEstimate(flops=0, bytes_accessed=7_000_000, transcendentals=0),
        name="clip_bounds",
    )(
        in_hbm(tile_frame),
        in_hbm(tile_keep.T),
        slots,
        in_hbm(w_qkv),
        in_hbm(gamma),
        in_hbm(beta),
    )


def load_rows(x_refs, x_scr, depth):
    col = row = 0
    for ref in x_refs:
        rows = ref.shape[0]
        x_scr[row : row + rows, col : col + depth] = ref[...]
        row += rows
        if row == x_scr.shape[0]:
            row, col = 0, col + depth


def fetch_rows(first_slot, first_member, load, slot_ref, w_ref, bound_ref, w_buf, w_sem, *bound):
    steps, count, depth, _ = w_buf.shape
    bound_copy = pltpu.make_async_copy(bound_ref, *bound)

    def copy(step, index):
        row = pl.multiple_of(slot_ref[first_slot + index] * depth, depth)
        return pltpu.make_async_copy(
            w_ref.at[step + first_member, pl.ds(row, depth), :],
            w_buf.at[step, index],
            w_sem.at[step, index],
        )

    step = pl.program_id(0)

    @pl.when(step == 0)
    def _():
        bound_copy.start()
        for index in range(count):
            copy(0, index).start()
        load()
        bound_copy.wait()

    for index in range(count):
        copy(step, index).wait()

    @pl.when(step == 0)
    def _():
        for other in range(1, steps):
            for index in range(count):
                copy(other, index).start()


def mask_rows(w_buf, step, member, bound_buf, out_scr):
    upper, lower = bound_buf[member, 0:1], bound_buf[member, 1:2]
    _, count, depth, width = w_buf.shape
    for index in range(count):
        block = w_buf[step, index].astype(jnp.float32)
        rows = slice(index * depth, (index + 1) * depth)
        out_scr[rows, 0:width] = jnp.where(block > upper, 1.0, 0.0).astype(jnp.bfloat16)
        out_scr[rows, width : 2 * width] = jnp.where(block < lower, 1.0, 0.0).astype(jnp.bfloat16)


def early_qkv_kernel(*refs):
    x_refs, (w_ref, q_ref, out_ref, x_scr, q_buf, q_sem) = refs[:-6], refs[-6:]
    step, steps = pl.program_id(0), pl.num_programs(0)
    _, _, depth, width = w_ref.shape

    @pl.when(step == 0)
    def _():
        load_rows(x_refs, x_scr, depth)

    result = dot(x_scr[...], w_ref[0].reshape(x_scr.shape[1], width))
    copy = pltpu.make_async_copy(q_buf, q_ref, q_sem)

    @pl.when(step == 0)
    def _():
        q_buf[...] = result
        copy.start()

    @pl.when(step > 0)
    def _():
        out_ref[0] = result

    @pl.when(step == steps - 1)
    def _():
        copy.wait()


def early_mask_kernel(slot_ref, *refs):
    x_refs, rest = refs[:-11], refs[-11:]
    w_ref, bound_ref, out_ref, x_scr, w_scr, w_buf, w_sem = rest[:7]
    bound_buf, bound_sem, out_buf, out_sem = rest[7:]
    step, steps = pl.program_id(0), w_buf.shape[0]
    load = lambda: load_rows(x_refs, x_scr, w_buf.shape[2])
    fetch_rows(0, 0, load, slot_ref, w_ref, bound_ref, w_buf, w_sem, bound_buf, bound_sem)
    mask_rows(w_buf, step, step, bound_buf, w_scr)
    out_buf[step] = dot(x_scr[...], w_scr[...]).astype(jnp.bfloat16)

    def copy(index):
        return pltpu.make_async_copy(out_buf.at[index], out_ref.at[index], out_sem.at[index])

    copy(step).start()

    @pl.when(step == steps - 1)
    def _():
        for index in range(steps):
            copy(index).wait()


def late_kv_kernel(*refs):
    x_refs, (w_ref, sum_ref, kv_ref, x_ref, x_scr, x_sem) = refs[:-6], refs[-6:]
    step, steps = pl.program_id(0), pl.num_programs(0)
    _, _, depth, width = w_ref.shape
    copy = pltpu.make_async_copy(x_scr, x_ref, x_sem)

    @pl.when(step == 0)
    def _():
        load_rows(x_refs, x_scr, depth)
        copy.start()

    result = dot(x_scr[...], w_ref[0].reshape(x_scr.shape[1], width))
    kv_ref[0] = (sum_ref[0] + result).astype(jnp.bfloat16)

    @pl.when(step == steps - 1)
    def _():
        copy.wait()


def late_rest_kernel(slot_ref, *refs):
    x_ref, w_ref, bound_ref, q_sum_ref, sum_ref, clipped_ref = refs[:6]
    q_ref, out_ref, last_ref = refs[6:9]
    x_scr, w_scr, w_buf, w_sem, bound_buf, bound_sem = refs[9:15]
    q_scr, q_scr_sem, q_buf, q_sem, sum_buf, sum_sem, x_sem = refs[15:]
    step, steps = pl.program_id(0), w_buf.shape[0]
    width = w_buf.shape[3]

    def copy(index):
        return pltpu.make_async_copy(sum_ref.at[index], sum_buf.at[index], sum_sem.at[index])

    x_copy = pltpu.make_async_copy(x_ref, x_scr, x_sem)
    q_copy = pltpu.make_async_copy(q_sum_ref, q_buf, q_sem)
    weights_copy = pltpu.make_async_copy(clipped_ref.at[0, pl.ds(4, 4)], q_scr, q_scr_sem)

    def load():
        x_copy.start()
        weights_copy.start()

    fetch_rows(4, 0, load, slot_ref, w_ref, bound_ref, w_buf, w_sem, bound_buf, bound_sem)

    @pl.when(step == 0)
    def _():
        q_copy.start()
        for index in range(steps):
            copy(index).start()
        x_copy.wait()
        weights_copy.wait()
        product = dot(x_scr[...], q_scr[...].reshape(x_scr.shape[1], width))
        q_copy.wait()
        q_ref[...] = ((q_buf[...] + product) * (SCALE * LOG2E)).astype(jnp.bfloat16)

    mask_rows(w_buf, step, step, bound_buf, w_scr)
    product = dot(x_scr[...], w_scr[...])
    copy(step).wait()
    result = (sum_buf[step].astype(jnp.float32) + product).astype(jnp.bfloat16)
    out_ref[0] = result
    last_ref[0, 0] = result[:, width - HEAD : width]
    last_ref[0, 1] = result[:, 2 * width - HEAD :]


def in_hbm(array):
    return pltpu.with_memory_space_constraint(array, pltpu.HBM)


def product_call(
    kernel, name, vmem, members, columns, slots, chunks, w_qkv, bound, sums, outs, scratch, cost
):
    _, count = members
    _, full, width = w_qkv.shape
    depth = full // 8
    rows = max(c.shape[0] for c in chunks)
    inner = sum(c.shape[0] * c.shape[1] for c in chunks) // rows
    stays = pl.BlockSpec(memory_space=pltpu.HBM)
    return pl.pallas_call(
        kernel,
        grid_spec=pltpu.PrefetchScalarGridSpec(
            num_scalar_prefetch=1,
            grid=(count,),
            in_specs=[
                stays if len(chunks) == 1 else pl.BlockSpec(c.shape, lambda p, s: (0, 0))
                for c in chunks
            ]
            + [stays, stays]
            + [stays if spec is None else spec for _, spec in sums],
            out_specs=[stays if spec is None else spec for spec, _ in outs],
            scratch_shapes=[
                pltpu.VMEM((rows, inner), jnp.bfloat16),
                pltpu.VMEM((inner, columns), jnp.bfloat16),
                pltpu.VMEM((count, inner // depth, depth, width), jnp.bfloat16),
                pltpu.SemaphoreType.DMA((count, inner // depth)),
                pltpu.VMEM(bound.shape, jnp.float32),
                pltpu.SemaphoreType.DMA(()),
            ]
            + scratch,
        ),
        out_shape=[shape for _, shape in outs],
        compiler_params=pltpu.CompilerParams(vmem_limit_bytes=vmem * MIB),
        cost_estimate=pl.CostEstimate(
            flops=int(2 * rows * inner * columns * count * cost),
            bytes_accessed=int(count * inner * width * 2 * cost),
            transcendentals=0,
        ),
        name=name,
    )(slots, *chunks, in_hbm(w_qkv), in_hbm(bound), *[a for a, _ in sums])


def rows_of(chunks):
    return max(c.shape[0] for c in chunks)


def members_out(members, rows, columns, dtype):
    spec = pl.BlockSpec((1, rows, columns), lambda p, s: (p, 0, 0))
    return spec, jax.ShapeDtypeStruct((members, rows, columns), dtype)


def qkv_call(kernel, name, members, half, chunks, clipped, sums, outs, scratch):
    first, count = members
    _, slots, depth, width = clipped.shape
    rows = rows_of(chunks)
    inner = slots // 2 * depth
    whole = lambda a: pl.BlockSpec(a.shape, lambda p: (0, 0))
    return pl.pallas_call(
        kernel,
        grid=(count,),
        in_specs=[whole(c) for c in chunks]
        + [pl.BlockSpec((1, slots // 2, depth, width), lambda p: (p + first, half, 0, 0))]
        + [spec for _, spec in sums],
        out_specs=[spec for spec, _ in outs],
        scratch_shapes=[pltpu.VMEM((rows, inner), jnp.bfloat16)] + scratch,
        out_shape=[shape for _, shape in outs],
        compiler_params=pltpu.CompilerParams(vmem_limit_bytes=19 * MIB),
        cost_estimate=pl.CostEstimate(
            flops=2 * rows * inner * width * count,
            bytes_accessed=count * inner * width * 2,
            transcendentals=0,
        ),
        name=name,
    )(*chunks, in_hbm(clipped), *[a for a, _ in sums])


def early_qkv(chunks, clipped):
    members, _, _, width = clipped.shape
    rows = rows_of(chunks)
    outs = [
        (pl.BlockSpec(memory_space=pltpu.HBM), pltpu.HBM((rows, width), jnp.float32)),
        (
            pl.BlockSpec((1, rows, width), lambda p: (jnp.maximum(p - 1, 0), 0, 0)),
            jax.ShapeDtypeStruct((members - 1, rows, width), jnp.float32),
        ),
    ]
    scratch = [pltpu.VMEM((rows, width), jnp.float32), pltpu.SemaphoreType.DMA(())]
    return qkv_call(
        early_qkv_kernel, "early_qkv", (0, members), 0, chunks, clipped, [], outs, scratch
    )


def early_masks(slots, chunks, w_qkv, bound):
    members, _, width = w_qkv.shape
    shape = (members, rows_of(chunks), 2 * width)
    outs = [(None, pltpu.HBM(shape, jnp.bfloat16))]
    scratch = [pltpu.VMEM(shape, jnp.bfloat16), pltpu.SemaphoreType.DMA((members,))]
    return product_call(
        early_mask_kernel,
        "early_masks",
        25,
        (0, members),
        2 * width,
        slots,
        chunks,
        w_qkv,
        bound,
        [],
        outs,
        scratch,
        1,
    )[0]


def late_kv(chunks, clipped, sums):
    members, slots, depth, width = clipped.shape
    rows = rows_of(chunks)
    spec = pl.BlockSpec((1, rows, width), lambda p: (p, 0, 0))
    outs = [
        (spec, jax.ShapeDtypeStruct((members - 1, rows, width), jnp.bfloat16)),
        (
            pl.BlockSpec(memory_space=pltpu.HBM),
            pltpu.HBM((rows, slots // 2 * depth), jnp.bfloat16),
        ),
    ]
    scratch = [pltpu.SemaphoreType.DMA(())]
    return qkv_call(
        late_kv_kernel,
        "late_kv",
        (1, members - 1),
        1,
        chunks,
        clipped,
        [(sums, spec)],
        outs,
        scratch,
    )


def late_rest(slots, chunks, w_qkv, bound, clipped, q_sums, sums):
    members, _, width = w_qkv.shape
    rows = rows_of(chunks)
    outs = [
        (
            pl.BlockSpec((rows, width), lambda p, s: (0, 0)),
            jax.ShapeDtypeStruct((rows, width), jnp.bfloat16),
        ),
        members_out(members, rows, 2 * width, jnp.bfloat16),
        (
            pl.BlockSpec((1, 2, rows, HEAD), lambda p, s: (jnp.maximum(p - 1, 0), 0, 0, 0)),
            jax.ShapeDtypeStruct((2, 2, rows, HEAD), jnp.bfloat16),
        ),
    ]
    scratch = [
        pltpu.VMEM((4, w_qkv.shape[1] // 8, width), jnp.bfloat16),
        pltpu.SemaphoreType.DMA(()),
        pltpu.VMEM((rows, width), jnp.float32),
        pltpu.SemaphoreType.DMA(()),
        pltpu.VMEM(sums.shape, sums.dtype),
        pltpu.SemaphoreType.DMA((members,)),
        pltpu.SemaphoreType.DMA(()),
    ]
    return product_call(
        late_rest_kernel,
        "late_rest",
        30,
        (0, members),
        2 * width,
        slots,
        chunks,
        w_qkv,
        bound,
        [(in_hbm(q_sums), None), (in_hbm(sums), None), (in_hbm(clipped), None)],
        outs,
        scratch,
        1,
    )


def attend_kernel(returns, *refs):
    bias_ref, q_ref, kv_ref, near_ref, other_ref, grad_ref, high_ref, low_ref, coef_ref = refs[0:9]
    if returns:
        att_ref, sum_ref, for_near_ref, for_other_ref, k_scr, v_scr, gk_scr, gv_scr = refs[9:]
    else:
        t_near_ref, t_other_ref, _, att_ref, sum_ref, k_scr, v_scr, gk_scr, gv_scr = refs[9:]
    position = lax.axis_index("tm")
    count = 2 * TILE
    even = 1 - lax.rem(position, 2)
    near_at = pl.multiple_of(2 * count * even, count)
    other_at = pl.multiple_of(2 * count * (1 - even), count)
    for member, scr in enumerate((k_scr, v_scr)):
        scr[count : 2 * count] = kv_ref[member]
        scr[pl.ds(near_at, count), :] = near_ref[member]
        scr[pl.ds(other_at, count), :] = other_ref[member]
    sums = [[0.0, 0.0] for _ in range(3)]

    def add(member, grad, high, low):
        for side, t in enumerate((high, low)):
            part = grad * t.astype(jnp.float32)
            sums[member][side] += jnp.sum(part, axis=0, keepdims=True)

    state = []
    for i in range(2):
        bias = [bias_ref[i, t : t + 1, 0:1] for t in range(WINDOW)]
        rows = slice(i * TILE, (i + 1) * TILE)
        keys = slice(i * TILE, i * TILE + WINDOW * TILE)
        q = q_ref[rows, :]
        grad = grad_ref[rows, :]
        k = k_scr[keys]
        v = v_scr[keys]
        scores = dot_nt(q, k)
        state.append((bias, rows, keys, q, grad, k, v, scores))
    for i in range(2):
        bias, rows, keys, q, grad, k, v, scores = state[i]
        parts = [scores[:, t * TILE : (t + 1) * TILE] for t in range(WINDOW)]
        peak = functools.reduce(
            jnp.maximum,
            [jnp.max(p, axis=1, keepdims=True) + bias[t] for t, p in enumerate(parts)],
        )
        weights = [jnp.exp2(p - (peak - bias[t])) for t, p in enumerate(parts)]
        total = sum(jnp.sum(w, axis=1, keepdims=True) for w in weights)
        e = jnp.concatenate(weights, axis=1)
        e_low = e.astype(jnp.bfloat16)
        inv = 1.0 / total
        out = dot(e_low, v) * inv
        att_ref[rows, :] = out.astype(jnp.bfloat16)
        grad_wide = grad.astype(jnp.float32)
        delta = jnp.sum(out * grad_wide, axis=1, keepdims=True)
        dprobs = dot_nt(grad, v)
        ds = (e * (dprobs - delta)).astype(jnp.bfloat16)
        gq = dot(ds, k) * (inv * SCALE)
        add(0, gq, high_ref[0, rows, :], low_ref[0, rows, :])
        q_scaled = (q.astype(jnp.float32) * (inv * (1.0 / LOG2E))).astype(jnp.bfloat16)
        grad_scaled = (grad_wide * inv).astype(jnp.bfloat16)
        gk = dot(q_scaled.T, ds)
        gv = dot(grad_scaled.T, e_low)
        if i == 0:
            gk_scr[:, keys] = gk
            gv_scr[:, keys] = gv
        else:
            span, head = WINDOW * TILE, slice(i * TILE, WINDOW * TILE)
            rest = slice(WINDOW * TILE, (WINDOW + 1) * TILE)
            gk_scr[:, head] += gk[:, 0 : span - TILE]
            gv_scr[:, head] += gv[:, 0 : span - TILE]
            gk_scr[:, rest] = gk[:, span - TILE :]
            gv_scr[:, rest] = gv[:, span - TILE :]
    for member, scr in enumerate((gk_scr, gv_scr)):
        own = scr[:, count : 2 * count].T
        for_near = scr[:, pl.ds(near_at, count)].T
        for_other = scr[:, pl.ds(other_at, count)].T
        add(member + 1, own, high_ref[member + 1], low_ref[member + 1])
        if returns:
            for_near_ref[member] = for_near.astype(jnp.bfloat16)
            for_other_ref[member] = for_other.astype(jnp.bfloat16)
        else:
            add(member + 1, for_near, t_near_ref[member, 0], t_near_ref[member, 1])
            add(member + 1, for_other, t_other_ref[member, 0], t_other_ref[member, 1])
    for member in range(3):
        for side in range(2):
            sum_ref[member, side : side + 1] = (
                sums[member][side] * coef_ref[member, side : side + 1]
            )


def attend(bias, first, count, query, kvs, out_grad, products, coef, last=None):
    rows, width = out_grad.shape
    heads = width // HEAD
    span = WINDOW * TILE
    column = pl.BlockSpec((rows, HEAD), lambda h: (0, h + first))
    pair = pl.BlockSpec((2, rows, HEAD), lambda h: (0, 0, h + first))
    halo = pl.BlockSpec((2, rows, HEAD), lambda h: (0, 0, h))
    high = pl.BlockSpec((3, rows, HEAD), lambda h: (0, 0, h + first))
    low = pl.BlockSpec((3, rows, HEAD), lambda h: (0, 0, h + first + heads))
    in_specs = [pl.BlockSpec((2, 8, HEAD), lambda h: (0, 0, 0))]
    in_specs += [column, pair, pair, pair, column, high, low]
    in_specs += [pl.BlockSpec((3, 2, HEAD), lambda h: (0, 0, h + first))]
    operands = [in_hbm(bias), query, *kvs, out_grad, products, products, in_hbm(coef)]
    out_specs = [column, pl.BlockSpec((3, 2, HEAD), lambda h: (0, 0, h))]
    out_shape = [
        jax.ShapeDtypeStruct((rows, width), jnp.bfloat16),
        jax.ShapeDtypeStruct((3, 2, count * HEAD), jnp.float32),
    ]
    aliases = {}
    if last is None:
        out_specs += [halo, halo]
        out_shape += [jax.ShapeDtypeStruct((2, rows, count * HEAD), jnp.bfloat16)] * 2
    else:
        near, other, attended = last
        in_specs += [pl.BlockSpec((2, 2, rows, HEAD), lambda h: (0, 0, 0, 0))] * 2
        in_specs += [pl.BlockSpec(memory_space=pl.ANY)]
        operands += [near, other, attended]
        aliases = {len(operands) - 1: 0}
    return pl.pallas_call(
        functools.partial(attend_kernel, last is None),
        grid=(count,),
        in_specs=in_specs,
        out_specs=out_specs,
        scratch_shapes=[pltpu.VMEM((6 * TILE, HEAD), jnp.bfloat16)] * 2
        + [pltpu.VMEM((HEAD, 6 * TILE), jnp.float32)] * 2,
        out_shape=out_shape,
        input_output_aliases=aliases,
        compiler_params=pltpu.CompilerParams(vmem_limit_bytes=34 * MIB),
        cost_estimate=pl.CostEstimate(
            flops=2 * 6 * rows * span * HEAD * count,
            bytes_accessed=5_000_000 * count,
            transcendentals=rows * span * count,
        ),
        name="attend",
    )(*operands)


def all_sums_kernel(near_ref, other_ref, high_ref, low_ref, coef_ref, first_ref, last_ref, out_ref):
    member = pl.program_id(0)
    width = near_ref.shape[2]
    out_ref[0, :, width:] = last_ref[0]

    @pl.when(member == 0)
    def _():
        out_ref[0, :, 0:width] = first_ref[0]

    @pl.when(member > 0)
    def _():
        grad = near_ref[0].astype(jnp.float32) + other_ref[0].astype(jnp.float32)
        for side, t_ref in enumerate((high_ref, low_ref)):
            part = grad * t_ref[0, :, 0:width].astype(jnp.float32)
            total = jnp.sum(part, axis=0, keepdims=True) * coef_ref[0, side : side + 1, 0:width]
            out_ref[0, side : side + 1, 0:width] = total + first_ref[0, side : side + 1]


def all_sums(near, other, products, coef, first, last):
    _, rows, narrow = near.shape
    width = products.shape[2] // 2
    grads = pl.BlockSpec((1, rows, narrow), lambda p: (jnp.maximum(p - 1, 0), 0, 0))
    two = lambda a: pl.BlockSpec((1, 2, a.shape[2]), lambda p: (p, 0, 0))
    return pl.pallas_call(
        all_sums_kernel,
        grid=(3,),
        in_specs=[
            grads,
            grads,
            pl.BlockSpec((1, rows, width), lambda p: (jnp.maximum(p, 1), 0, 0)),
            pl.BlockSpec((1, rows, width), lambda p: (jnp.maximum(p, 1), 0, 1)),
            two(coef),
            two(first),
            two(last),
        ],
        out_specs=two(coef),
        out_shape=jax.ShapeDtypeStruct((3, 2, width), jnp.float32),
        compiler_params=pltpu.CompilerParams(vmem_limit_bytes=16 * MIB),
        cost_estimate=pl.CostEstimate(flops=0, bytes_accessed=5_000_000, transcendentals=0),
        name="all_sums",
    )(near, other, products, products, coef, first, last)


def swap_near(block):
    count = lax.axis_size("tm")
    return lax.ppermute(block, "tm", [(i, i ^ 1) for i in range(count)])


def swap_other(block):
    count = lax.axis_size("tm")
    pairs = [(i, i + 1) for i in range(1, count - 1, 2)]
    return lax.ppermute(block, "tm", pairs + [(b, a) for a, b in pairs])


def sum_over_tm(part):
    count = lax.axis_size("tm")
    swapped = lambda step: lax.ppermute(part, "tm", [(i, i ^ step) for i in range(count)])
    part = part + swapped(1)
    part = part + swapped(8)
    return (part + swapped(2)) + (swapped(4) + swapped(6))


def body(tokens, w_qkv, gamma, beta, out_grad, tile_frame, tile_keep):
    up, down, swap = tensor_routes(4)
    half = tokens.shape[0] // 2
    slots = chunk_slots()
    bound, coef, bias, clipped = bounds(w_qkv, gamma, beta, tile_frame, tile_keep, slots)
    below, above, beside = send(tokens, up), send(tokens, down), send(tokens, swap)
    below, above, beside = (after(part, bound) for part in (below, above, beside))
    far = [send(below[:half], up), send(above[half:], down)]
    early = (in_hbm(tokens), below, above, beside)
    q_sums, kv_sums = early_qkv(early, clipped)
    beside = after(beside, kv_sums)
    beside_below, beside_above = send(beside, up), send(beside, down)
    beside_far = [send(part, swap) for part in far]
    early = (in_hbm(after(tokens, *far)),) + early[1:]
    mask_sums = early_masks(slots, early, w_qkv, bound)
    late = (after(beside_below, mask_sums), beside_above, *far, *beside_far)
    kv, late = late_kv(late, clipped, kv_sums)
    kvs = (kv, swap_near(kv), swap_other(kv))
    query, products, last_products = late_rest(slots, (in_hbm(late),), w_qkv, bound, clipped, q_sums, mask_sums)
    t_other, t_near = swap_other(last_products), swap_near(last_products)
    attended, first, for_near, for_other = attend(
        bias, 0, 2, query, kvs, out_grad, products, coef
    )
    from_other, from_near = swap_other(for_other), swap_near(for_near)
    attended, last = attend(
        bias,
        2,
        1,
        query,
        kvs,
        out_grad,
        products,
        coef,
        (t_near, t_other, attended),
    )
    totals = sum_over_tm(all_sums(from_near, from_other, products, coef, first, last))
    return attended, totals[:, 0], totals[:, 1]


def solution(mesh):
    return jax.shard_map(
        body,
        mesh=mesh,
        in_specs=(
            P("tm", "tensor"),
            P(None, None, "tensor"),
            P(None, "tensor"),
            P(None, "tensor"),
            P("tm", "tensor"),
            P(),
            P(),
        ),
        out_specs=(P("tm", "tensor"), P(None, "tensor"), P(None, "tensor")),
        check_vma=False,
    )
```

```python
import functools
import math

import jax
import jax.numpy as jnp
from jax import lax
from jax.experimental import pallas as pl
from jax.experimental.pallas import tpu as pltpu
from jax.sharding import PartitionSpec as P

HEAD = 128
TILE = 384
REACH = 2
WINDOW = 2 * REACH + 1
SCALE = HEAD**-0.5
LOG2E = math.log2(math.e)
NEG = -1e30
MIB = 1024 * 1024

NT = (((1,), (1,)), ((), ()))


def dot(a, b):
    return jnp.dot(a, b, preferred_element_type=jnp.float32)


def dot_nt(a, b):
    return lax.dot_general(a, b, NT, preferred_element_type=jnp.float32)


def tensor_routes(z_count):
    def route(f):
        return [(z * 2 + y, f(z, y)) for z in range(z_count) for y in range(2)]

    up = route(lambda z, y: ((z + 1) % z_count) * 2 + y)
    down = route(lambda z, y: ((z - 1) % z_count) * 2 + y)
    swap = route(lambda z, y: z * 2 + 1 - y)
    return up, down, swap


def send(block, route):
    return lax.ppermute(block, "tensor", route)


def after(value, *others):
    return lax.optimization_barrier((value,) + others)[0]


def chunk_slots():
    me = lax.axis_index("tensor")
    z, y = me // 2, lax.rem(me, 2)
    below, above, far = lax.rem(z + 3, 4), lax.rem(z + 1, 4), lax.rem(z + 2, 4)
    return jnp.stack(
        [
            z * 2 + y,
            below * 2 + y,
            above * 2 + y,
            z * 2 + 1 - y,
            below * 2 + 1 - y,
            above * 2 + 1 - y,
            far * 2 + y,
            far * 2 + 1 - y,
        ]
    ).astype(jnp.int32)


def tile_bias(frame_ref, keep_ref, a):
    tiles = frame_ref.shape[0]
    bias = []
    for t in range(WINDOW):
        b = a + (t - REACH)
        b_in = jnp.clip(b, 0, tiles - 1)
        ok = (
            (b >= 0)
            & (b < tiles)
            & (jnp.abs(frame_ref[a] - frame_ref[b_in]) <= 1)
            & (keep_ref[t, a] == 1)
        )
        bias.append(jnp.where(ok, 0.0, NEG))
    return bias


def bounds_kernel(frame_ref, keep_ref, slot_ref, w_ref, gamma_ref, beta_ref, *outs):
    bound_ref, coef_ref, bias_ref, clipped_ref = outs
    w = w_ref[0].astype(jnp.float32)
    col_max = jnp.max(w, axis=0, keepdims=True)
    col_min = jnp.min(w, axis=0, keepdims=True)
    member = pl.program_id(0)
    sig_gamma = jax.nn.sigmoid(gamma_ref[pl.ds(member, 1), :])
    sig_beta = jax.nn.sigmoid(beta_ref[pl.ds(member, 1), :])
    upper = sig_gamma * col_max
    lower = sig_beta * col_min
    bound_ref[0, 0:1] = upper
    bound_ref[0, 1:2] = lower
    coef_ref[0, 0:1] = sig_gamma * (1.0 - sig_gamma) * col_max
    coef_ref[0, 1:2] = sig_beta * (1.0 - sig_beta) * col_min
    first = lax.axis_index("tm") * 2
    for i in range(2):
        for t, bias in enumerate(tile_bias(frame_ref, keep_ref, first + i)):
            bias_ref[i, t : t + 1] = jnp.full((1, HEAD), bias, jnp.float32)
        bias_ref[i, WINDOW:] = jnp.zeros((8 - WINDOW, HEAD), jnp.float32)
    _, count, depth, _ = clipped_ref.shape
    for slot in range(count):
        row = pl.multiple_of(slot_ref[slot] * depth, depth)
        block = w_ref[0, pl.ds(row, depth), :].astype(jnp.float32)
        clipped = jnp.minimum(jnp.maximum(block, lower), upper)
        clipped_ref[0, slot] = clipped.astype(jnp.bfloat16)


def bounds(w_qkv, gamma, beta, tile_frame, tile_keep, slots):
    members, rows, width = w_qkv.shape
    sorted_shape = (members, 8, rows // 8, width)
    whole = pl.BlockSpec((members, width), lambda p, *_: (0, 0))
    two = pl.BlockSpec((1, 2, width), lambda p, *_: (p, 0, 0))
    return pl.pallas_call(
        bounds_kernel,
        grid_spec=pltpu.PrefetchScalarGridSpec(
            num_scalar_prefetch=3,
            grid=(members,),
            in_specs=[pl.BlockSpec((1, rows, width), lambda p, *_: (p, 0, 0)), whole, whole],
            out_specs=[
                two,
                two,
                pl.BlockSpec((2, 8, HEAD), lambda p, *_: (0, 0, 0)),
                pl.BlockSpec((1,) + sorted_shape[1:], lambda p, *_: (p, 0, 0, 0)),
            ],
        ),
        out_shape=[pltpu.HBM((members, 2, width), jnp.float32)] * 2
        + [pltpu.HBM((2, 8, HEAD), jnp.float32), pltpu.HBM(sorted_shape, jnp.bfloat16)],
        compiler_params=pltpu.CompilerParams(vmem_limit_bytes=16 * MIB),
        cost_estimate=pl.CostEstimate(flops=0, bytes_accessed=7_000_000, transcendentals=0),
        name="clip_bounds",
    )(
        in_hbm(tile_frame),
        in_hbm(tile_keep.T),
        slots,
        in_hbm(w_qkv),
        in_hbm(gamma),
        in_hbm(beta),
    )


def load_rows(x_refs, x_scr, depth):
    col = row = 0
    for ref in x_refs:
        rows = ref.shape[0]
        x_scr[row : row + rows, col : col + depth] = ref[...]
        row += rows
        if row == x_scr.shape[0]:
            row, col = 0, col + depth


def fetch_rows(first_slot, first_member, load, slot_ref, w_ref, bound_ref, w_buf, w_sem, *bound):
    steps, count, depth, _ = w_buf.shape
    bound_copy = pltpu.make_async_copy(bound_ref, *bound)

    def copy(step, index):
        row = pl.multiple_of(slot_ref[first_slot + index] * depth, depth)
        return pltpu.make_async_copy(
            w_ref.at[step + first_member, pl.ds(row, depth), :],
            w_buf.at[step, index],
            w_sem.at[step, index],
        )

    step = pl.program_id(0)

    @pl.when(step == 0)
    def _():
        bound_copy.start()
        for index in range(count):
            copy(0, index).start()
        load()
        bound_copy.wait()

    for index in range(count):
        copy(step, index).wait()

    @pl.when(step == 0)
    def _():
        for other in range(1, steps):
            for index in range(count):
                copy(other, index).start()


def mask_rows(w_buf, step, member, bound_buf, out_scr):
    upper, lower = bound_buf[member, 0:1], bound_buf[member, 1:2]
    _, count, depth, width = w_buf.shape
    for index in range(count):
        block = w_buf[step, index].astype(jnp.float32)
        rows = slice(index * depth, (index + 1) * depth)
        out_scr[rows, 0:width] = jnp.where(block > upper, 1.0, 0.0).astype(jnp.bfloat16)
        out_scr[rows, width : 2 * width] = jnp.where(block < lower, 1.0, 0.0).astype(jnp.bfloat16)


def early_qkv_kernel(*refs):
    x_refs, (w_ref, q_ref, out_ref, x_scr, q_buf, q_sem) = refs[:-6], refs[-6:]
    step, steps = pl.program_id(0), pl.num_programs(0)
    _, _, depth, width = w_ref.shape

    @pl.when(step == 0)
    def _():
        load_rows(x_refs, x_scr, depth)

    result = dot(x_scr[...], w_ref[0].reshape(x_scr.shape[1], width))
    copy = pltpu.make_async_copy(q_buf, q_ref, q_sem)

    @pl.when(step == 0)
    def _():
        q_buf[...] = result
        copy.start()

    @pl.when(step > 0)
    def _():
        out_ref[0] = result

    @pl.when(step == steps - 1)
    def _():
        copy.wait()


def early_mask_kernel(slot_ref, *refs):
    x_refs, rest = refs[:-11], refs[-11:]
    w_ref, bound_ref, out_ref, x_scr, w_scr, w_buf, w_sem = rest[:7]
    bound_buf, bound_sem, out_buf, out_sem = rest[7:]
    step, steps = pl.program_id(0), w_buf.shape[0]
    load = lambda: load_rows(x_refs, x_scr, w_buf.shape[2])
    fetch_rows(0, 0, load, slot_ref, w_ref, bound_ref, w_buf, w_sem, bound_buf, bound_sem)
    mask_rows(w_buf, step, step, bound_buf, w_scr)
    out_buf[step] = dot(x_scr[...], w_scr[...]).astype(jnp.bfloat16)

    def copy(index):
        return pltpu.make_async_copy(out_buf.at[index], out_ref.at[index], out_sem.at[index])

    copy(step).start()

    @pl.when(step == steps - 1)
    def _():
        for index in range(steps):
            copy(index).wait()


def late_kv_kernel(*refs):
    x_refs, (w_ref, sum_ref, kv_ref, x_ref, x_scr, x_sem) = refs[:-6], refs[-6:]
    step, steps = pl.program_id(0), pl.num_programs(0)
    _, _, depth, width = w_ref.shape
    copy = pltpu.make_async_copy(x_scr, x_ref, x_sem)

    @pl.when(step == 0)
    def _():
        load_rows(x_refs, x_scr, depth)
        copy.start()

    result = dot(x_scr[...], w_ref[0].reshape(x_scr.shape[1], width))
    kv_ref[0] = (sum_ref[0] + result).astype(jnp.bfloat16)

    @pl.when(step == steps - 1)
    def _():
        copy.wait()


def late_rest_kernel(slot_ref, *refs):
    x_ref, w_ref, bound_ref, q_sum_ref, sum_ref, clipped_ref = refs[:6]
    q_ref, out_ref, last_ref = refs[6:9]
    x_scr, w_scr, w_buf, w_sem, bound_buf, bound_sem = refs[9:15]
    q_scr, q_scr_sem, q_buf, q_sem, sum_buf, sum_sem, x_sem = refs[15:]
    step, steps = pl.program_id(0), w_buf.shape[0]
    width = w_buf.shape[3]

    def copy(index):
        return pltpu.make_async_copy(sum_ref.at[index + 1], sum_buf.at[index], sum_sem.at[index])

    x_copy = pltpu.make_async_copy(x_ref, x_scr, x_sem)
    q_copy = pltpu.make_async_copy(q_sum_ref, q_buf, q_sem)
    weights_copy = pltpu.make_async_copy(clipped_ref.at[0, pl.ds(4, 4)], q_scr, q_scr_sem)

    def load():
        x_copy.start()
        weights_copy.start()

    fetch_rows(4, 1, load, slot_ref, w_ref, bound_ref, w_buf, w_sem, bound_buf, bound_sem)

    @pl.when(step == 0)
    def _():
        q_copy.start()
        for index in range(steps):
            copy(index).start()
        x_copy.wait()
        weights_copy.wait()
        product = dot(x_scr[...], q_scr[...].reshape(x_scr.shape[1], width))
        q_copy.wait()
        q_ref[...] = ((q_buf[...] + product) * (SCALE * LOG2E)).astype(jnp.bfloat16)

    mask_rows(w_buf, step, step + 1, bound_buf, w_scr)
    product = dot(x_scr[...], w_scr[...])
    copy(step).wait()
    result = (sum_buf[step].astype(jnp.float32) + product).astype(jnp.bfloat16)
    out_ref[0] = result
    last_ref[0, 0] = result[:, width - HEAD : width]
    last_ref[0, 1] = result[:, 2 * width - HEAD :]


def query_sums_kernel(slot_ref, *refs):
    x_ref, w_ref, bound_ref, sum_ref, first_ref, last_ref, coef_ref, out_ref = refs[:8]
    x_scr, w_scr, w_buf, w_sem, bound_buf, bound_sem, sum_buf, sum_sem, x_sem = refs[8:]
    width, narrow = w_buf.shape[3], first_ref.shape[1]
    x_copy = pltpu.make_async_copy(x_ref, x_scr, x_sem)
    sum_copy = pltpu.make_async_copy(sum_ref.at[0], sum_buf, sum_sem)

    def load():
        x_copy.start()
        sum_copy.start()

    fetch_rows(4, 0, load, slot_ref, w_ref, bound_ref, w_buf, w_sem, bound_buf, bound_sem)
    mask_rows(w_buf, 0, 0, bound_buf, w_scr)
    x_copy.wait()
    sum_copy.wait()
    result = sum_buf[...].astype(jnp.float32) + dot(x_scr[...], w_scr[...])
    for ref, cols in ((first_ref, slice(0, narrow)), (last_ref, slice(narrow, width))):
        grad = ref[...].astype(jnp.float32)
        for side in range(2):
            at = slice(side * width + cols.start, side * width + cols.stop)
            total = jnp.sum(grad * result[:, at], axis=0, keepdims=True)
            out_ref[0, side : side + 1, cols] = total * coef_ref[0, side : side + 1, cols]


def in_hbm(array):
    return pltpu.with_memory_space_constraint(array, pltpu.HBM)


def product_call(
    kernel, name, vmem, members, columns, slots, chunks, w_qkv, bound, sums, outs, scratch, cost
):
    _, count = members
    _, full, width = w_qkv.shape
    depth = full // 8
    rows = max(c.shape[0] for c in chunks)
    inner = sum(c.shape[0] * c.shape[1] for c in chunks) // rows
    stays = pl.BlockSpec(memory_space=pltpu.HBM)
    return pl.pallas_call(
        kernel,
        grid_spec=pltpu.PrefetchScalarGridSpec(
            num_scalar_prefetch=1,
            grid=(count,),
            in_specs=[
                stays if len(chunks) == 1 else pl.BlockSpec(c.shape, lambda p, s: (0, 0))
                for c in chunks
            ]
            + [stays, stays]
            + [stays if spec is None else spec for _, spec in sums],
            out_specs=[stays if spec is None else spec for spec, _ in outs],
            scratch_shapes=[
                pltpu.VMEM((rows, inner), jnp.bfloat16),
                pltpu.VMEM((inner, columns), jnp.bfloat16),
                pltpu.VMEM((count, inner // depth, depth, width), jnp.bfloat16),
                pltpu.SemaphoreType.DMA((count, inner // depth)),
                pltpu.VMEM(bound.shape, jnp.float32),
                pltpu.SemaphoreType.DMA(()),
            ]
            + scratch,
        ),
        out_shape=[shape for _, shape in outs],
        compiler_params=pltpu.CompilerParams(vmem_limit_bytes=vmem * MIB),
        cost_estimate=pl.CostEstimate(
            flops=int(2 * rows * inner * columns * count * cost),
            bytes_accessed=int(count * inner * width * 2 * cost),
            transcendentals=0,
        ),
        name=name,
    )(slots, *chunks, in_hbm(w_qkv), in_hbm(bound), *[a for a, _ in sums])


def rows_of(chunks):
    return max(c.shape[0] for c in chunks)


def members_out(members, rows, columns, dtype):
    spec = pl.BlockSpec((1, rows, columns), lambda p, s: (p, 0, 0))
    return spec, jax.ShapeDtypeStruct((members, rows, columns), dtype)


def qkv_call(kernel, name, members, half, chunks, clipped, sums, outs, scratch):
    first, count = members
    _, slots, depth, width = clipped.shape
    rows = rows_of(chunks)
    inner = slots // 2 * depth
    whole = lambda a: pl.BlockSpec(a.shape, lambda p: (0, 0))
    return pl.pallas_call(
        kernel,
        grid=(count,),
        in_specs=[whole(c) for c in chunks]
        + [pl.BlockSpec((1, slots // 2, depth, width), lambda p: (p + first, half, 0, 0))]
        + [spec for _, spec in sums],
        out_specs=[spec for spec, _ in outs],
        scratch_shapes=[pltpu.VMEM((rows, inner), jnp.bfloat16)] + scratch,
        out_shape=[shape for _, shape in outs],
        compiler_params=pltpu.CompilerParams(vmem_limit_bytes=19 * MIB),
        cost_estimate=pl.CostEstimate(
            flops=2 * rows * inner * width * count,
            bytes_accessed=count * inner * width * 2,
            transcendentals=0,
        ),
        name=name,
    )(*chunks, in_hbm(clipped), *[a for a, _ in sums])


def early_qkv(chunks, clipped):
    members, _, _, width = clipped.shape
    rows = rows_of(chunks)
    outs = [
        (pl.BlockSpec(memory_space=pltpu.HBM), pltpu.HBM((rows, width), jnp.float32)),
        (
            pl.BlockSpec((1, rows, width), lambda p: (jnp.maximum(p - 1, 0), 0, 0)),
            jax.ShapeDtypeStruct((members - 1, rows, width), jnp.float32),
        ),
    ]
    scratch = [pltpu.VMEM((rows, width), jnp.float32), pltpu.SemaphoreType.DMA(())]
    return qkv_call(
        early_qkv_kernel, "early_qkv", (0, members), 0, chunks, clipped, [], outs, scratch
    )


def early_masks(slots, chunks, w_qkv, bound):
    members, _, width = w_qkv.shape
    shape = (members, rows_of(chunks), 2 * width)
    outs = [(None, pltpu.HBM(shape, jnp.bfloat16))]
    scratch = [pltpu.VMEM(shape, jnp.bfloat16), pltpu.SemaphoreType.DMA((members,))]
    return product_call(
        early_mask_kernel,
        "early_masks",
        25,
        (0, members),
        2 * width,
        slots,
        chunks,
        w_qkv,
        bound,
        [],
        outs,
        scratch,
        1,
    )[0]


def late_kv(chunks, clipped, sums):
    members, slots, depth, width = clipped.shape
    rows = rows_of(chunks)
    spec = pl.BlockSpec((1, rows, width), lambda p: (p, 0, 0))
    outs = [
        (spec, jax.ShapeDtypeStruct((members - 1, rows, width), jnp.bfloat16)),
        (
            pl.BlockSpec(memory_space=pltpu.HBM),
            pltpu.HBM((rows, slots // 2 * depth), jnp.bfloat16),
        ),
    ]
    scratch = [pltpu.SemaphoreType.DMA(())]
    return qkv_call(
        late_kv_kernel,
        "late_kv",
        (1, members - 1),
        1,
        chunks,
        clipped,
        [(sums, spec)],
        outs,
        scratch,
    )


def late_rest(slots, chunks, w_qkv, bound, clipped, q_sums, sums):
    members, _, width = w_qkv.shape
    rows = rows_of(chunks)
    outs = [
        (
            pl.BlockSpec((rows, width), lambda p, s: (0, 0)),
            jax.ShapeDtypeStruct((rows, width), jnp.bfloat16),
        ),
        members_out(members - 1, rows, 2 * width, jnp.bfloat16),
        (
            pl.BlockSpec((1, 2, rows, HEAD), lambda p, s: (p, 0, 0, 0)),
            jax.ShapeDtypeStruct((2, 2, rows, HEAD), jnp.bfloat16),
        ),
    ]
    scratch = [
        pltpu.VMEM((4, w_qkv.shape[1] // 8, width), jnp.bfloat16),
        pltpu.SemaphoreType.DMA(()),
        pltpu.VMEM((rows, width), jnp.float32),
        pltpu.SemaphoreType.DMA(()),
        pltpu.VMEM((members - 1,) + sums.shape[1:], sums.dtype),
        pltpu.SemaphoreType.DMA((members - 1,)),
        pltpu.SemaphoreType.DMA(()),
    ]
    return product_call(
        late_rest_kernel,
        "late_rest",
        30,
        (1, members - 1),
        2 * width,
        slots,
        chunks,
        w_qkv,
        bound,
        [(in_hbm(q_sums), None), (in_hbm(sums), None), (in_hbm(clipped), None)],
        outs,
        scratch,
        1,
    )


def query_sums(slots, chunks, w_qkv, bound, sums, first, last, coef):
    _, _, width = w_qkv.shape
    two = pl.BlockSpec((1, 2, width), lambda p, s: (0, 0, 0))
    grad = lambda a: pl.BlockSpec(a.shape, lambda p, s: (0, 0))
    return product_call(
        query_sums_kernel,
        "query_sums",
        24,
        (0, 1),
        2 * width,
        slots,
        chunks,
        w_qkv,
        bound,
        [(in_hbm(sums), None), (first, grad(first)), (last, grad(last)), (coef, two)],
        [(two, jax.ShapeDtypeStruct((1, 2, width), jnp.float32))],
        [
            pltpu.VMEM(sums.shape[1:], sums.dtype),
            pltpu.SemaphoreType.DMA(()),
            pltpu.SemaphoreType.DMA(()),
        ],
        1,
    )[0]


def attend_kernel(returns, *refs):
    bias_ref, q_ref, kv_ref, near_ref, other_ref, grad_ref, high_ref, low_ref, coef_ref = refs[0:9]
    if returns:
        att_ref, sum_ref, gq_ref, for_near_ref, for_other_ref, k_scr, v_scr, gk_scr, gv_scr = refs[9:]
    else:
        t_near_ref, t_other_ref, _, att_ref, sum_ref, gq_ref, k_scr, v_scr, gk_scr, gv_scr = refs[9:]
    position = lax.axis_index("tm")
    count = 2 * TILE
    even = 1 - lax.rem(position, 2)
    near_at = pl.multiple_of(2 * count * even, count)
    other_at = pl.multiple_of(2 * count * (1 - even), count)
    for member, scr in enumerate((k_scr, v_scr)):
        scr[count : 2 * count] = kv_ref[member]
        scr[pl.ds(near_at, count), :] = near_ref[member]
        scr[pl.ds(other_at, count), :] = other_ref[member]
    sums = [[0.0, 0.0] for _ in range(2)]

    def add(member, grad, high, low):
        for side, t in enumerate((high, low)):
            part = grad * t.astype(jnp.float32)
            sums[member][side] += jnp.sum(part, axis=0, keepdims=True)

    state = []
    for i in range(2):
        bias = [bias_ref[i, t : t + 1, 0:1] for t in range(WINDOW)]
        rows = slice(i * TILE, (i + 1) * TILE)
        keys = slice(i * TILE, i * TILE + WINDOW * TILE)
        q = q_ref[rows, :]
        grad = grad_ref[rows, :]
        k = k_scr[keys]
        v = v_scr[keys]
        scores = dot_nt(q, k)
        state.append((bias, rows, keys, q, grad, k, v, scores))
    for i in range(2):
        bias, rows, keys, q, grad, k, v, scores = state[i]
        parts = [scores[:, t * TILE : (t + 1) * TILE] for t in range(WINDOW)]
        peak = functools.reduce(
            jnp.maximum,
            [jnp.max(p, axis=1, keepdims=True) + bias[t] for t, p in enumerate(parts)],
        )
        weights = [jnp.exp2(p - (peak - bias[t])) for t, p in enumerate(parts)]
        total = sum(jnp.sum(w, axis=1, keepdims=True) for w in weights)
        e = jnp.concatenate(weights, axis=1)
        e_low = e.astype(jnp.bfloat16)
        inv = 1.0 / total
        out = dot(e_low, v) * inv
        att_ref[rows, :] = out.astype(jnp.bfloat16)
        grad_wide = grad.astype(jnp.float32)
        delta = jnp.sum(out * grad_wide, axis=1, keepdims=True)
        dprobs = dot_nt(grad, v)
        ds = (e * (dprobs - delta)).astype(jnp.bfloat16)
        gq_ref[rows, :] = (dot(ds, k) * (inv * SCALE)).astype(jnp.bfloat16)
        q_scaled = (q.astype(jnp.float32) * (inv * (1.0 / LOG2E))).astype(jnp.bfloat16)
        grad_scaled = (grad_wide * inv).astype(jnp.bfloat16)
        gk = dot(q_scaled.T, ds)
        gv = dot(grad_scaled.T, e_low)
        if i == 0:
            gk_scr[:, keys] = gk
            gv_scr[:, keys] = gv
        else:
            span, head = WINDOW * TILE, slice(i * TILE, WINDOW * TILE)
            rest = slice(WINDOW * TILE, (WINDOW + 1) * TILE)
            gk_scr[:, head] += gk[:, 0 : span - TILE]
            gv_scr[:, head] += gv[:, 0 : span - TILE]
            gk_scr[:, rest] = gk[:, span - TILE :]
            gv_scr[:, rest] = gv[:, span - TILE :]
    for member, scr in enumerate((gk_scr, gv_scr)):
        own = scr[:, count : 2 * count].T
        for_near = scr[:, pl.ds(near_at, count)].T
        for_other = scr[:, pl.ds(other_at, count)].T
        add(member, own, high_ref[member], low_ref[member])
        if returns:
            for_near_ref[member] = for_near.astype(jnp.bfloat16)
            for_other_ref[member] = for_other.astype(jnp.bfloat16)
        else:
            add(member, for_near, t_near_ref[member, 0], t_near_ref[member, 1])
            add(member, for_other, t_other_ref[member, 0], t_other_ref[member, 1])
    for member in range(2):
        for side in range(2):
            sum_ref[member, side : side + 1] = (
                sums[member][side] * coef_ref[member + 1, side : side + 1]
            )


def attend(bias, first, count, query, kvs, out_grad, products, coef, last=None):
    rows, width = out_grad.shape
    heads = width // HEAD
    span = WINDOW * TILE
    column = pl.BlockSpec((rows, HEAD), lambda h: (0, h + first))
    pair = pl.BlockSpec((2, rows, HEAD), lambda h: (0, 0, h + first))
    halo = pl.BlockSpec((2, rows, HEAD), lambda h: (0, 0, h))
    high = pl.BlockSpec((2, rows, HEAD), lambda h: (0, 0, h + first))
    low = pl.BlockSpec((2, rows, HEAD), lambda h: (0, 0, h + first + heads))
    in_specs = [pl.BlockSpec((2, 8, HEAD), lambda h: (0, 0, 0))]
    in_specs += [column, pair, pair, pair, column, high, low]
    in_specs += [pl.BlockSpec((3, 2, HEAD), lambda h: (0, 0, h + first))]
    operands = [in_hbm(bias), query, *kvs, out_grad, products, products, in_hbm(coef)]
    out_specs = [column, pl.BlockSpec((2, 2, HEAD), lambda h: (0, 0, h))]
    out_specs += [pl.BlockSpec((rows, HEAD), lambda h: (0, h))]
    out_shape = [
        jax.ShapeDtypeStruct((rows, width), jnp.bfloat16),
        jax.ShapeDtypeStruct((2, 2, count * HEAD), jnp.float32),
        jax.ShapeDtypeStruct((rows, count * HEAD), jnp.bfloat16),
    ]
    aliases = {}
    if last is None:
        out_specs += [halo, halo]
        out_shape += [jax.ShapeDtypeStruct((2, rows, count * HEAD), jnp.bfloat16)] * 2
    else:
        near, other, attended = last
        in_specs += [pl.BlockSpec((2, 2, rows, HEAD), lambda h: (0, 0, 0, 0))] * 2
        in_specs += [pl.BlockSpec(memory_space=pl.ANY)]
        operands += [near, other, attended]
        aliases = {len(operands) - 1: 0}
    return pl.pallas_call(
        functools.partial(attend_kernel, last is None),
        grid=(count,),
        in_specs=in_specs,
        out_specs=out_specs,
        scratch_shapes=[pltpu.VMEM((6 * TILE, HEAD), jnp.bfloat16)] * 2
        + [pltpu.VMEM((HEAD, 6 * TILE), jnp.float32)] * 2,
        out_shape=out_shape,
        input_output_aliases=aliases,
        compiler_params=pltpu.CompilerParams(vmem_limit_bytes=34 * MIB),
        cost_estimate=pl.CostEstimate(
            flops=2 * 6 * rows * span * HEAD * count,
            bytes_accessed=5_000_000 * count,
            transcendentals=rows * span * count,
        ),
        name="attend",
    )(*operands)


def all_sums_kernel(near_ref, other_ref, high_ref, low_ref, coef_ref, *refs):
    query_ref, first_ref, last_ref, out_ref = refs
    member = pl.program_id(0)
    width = near_ref.shape[2]

    @pl.when(member == 0)
    def _():
        out_ref[0] = query_ref[0]

    @pl.when(member > 0)
    def _():
        out_ref[0, :, width:] = last_ref[0]
        grad = near_ref[0].astype(jnp.float32) + other_ref[0].astype(jnp.float32)
        for side, t_ref in enumerate((high_ref, low_ref)):
            part = grad * t_ref[0, :, 0:width].astype(jnp.float32)
            total = jnp.sum(part, axis=0, keepdims=True) * coef_ref[0, side : side + 1, 0:width]
            out_ref[0, side : side + 1, 0:width] = total + first_ref[0, side : side + 1]


def all_sums(near, other, products, coef, query, first, last):
    _, rows, narrow = near.shape
    width = products.shape[2] // 2
    grads = pl.BlockSpec((1, rows, narrow), lambda p: (jnp.maximum(p - 1, 0), 0, 0))
    two = lambda a: pl.BlockSpec((1, 2, a.shape[2]), lambda p: (p, 0, 0))
    pair = lambda a: pl.BlockSpec((1, 2, a.shape[2]), lambda p: (jnp.maximum(p - 1, 0), 0, 0))
    return pl.pallas_call(
        all_sums_kernel,
        grid=(3,),
        in_specs=[
            grads,
            grads,
            pl.BlockSpec((1, rows, width), lambda p: (jnp.maximum(p - 1, 0), 0, 0)),
            pl.BlockSpec((1, rows, width), lambda p: (jnp.maximum(p - 1, 0), 0, 1)),
            two(coef),
            pl.BlockSpec(query.shape, lambda p: (0, 0, 0)),
            pair(first),
            pair(last),
        ],
        out_specs=two(coef),
        out_shape=jax.ShapeDtypeStruct((3, 2, width), jnp.float32),
        compiler_params=pltpu.CompilerParams(vmem_limit_bytes=16 * MIB),
        cost_estimate=pl.CostEstimate(flops=0, bytes_accessed=5_000_000, transcendentals=0),
        name="all_sums",
    )(near, other, products, products, coef, query, first, last)


def swap_near(block):
    count = lax.axis_size("tm")
    return lax.ppermute(block, "tm", [(i, i ^ 1) for i in range(count)])


def swap_other(block):
    count = lax.axis_size("tm")
    pairs = [(i, i + 1) for i in range(1, count - 1, 2)]
    return lax.ppermute(block, "tm", pairs + [(b, a) for a, b in pairs])


def sum_over_tm(part):
    count = lax.axis_size("tm")
    swapped = lambda step: lax.ppermute(part, "tm", [(i, i ^ step) for i in range(count)])
    part = part + swapped(1)
    part = (part + swapped(2)) + (swapped(4) + swapped(6))
    return part + swapped(8)


def body(tokens, w_qkv, gamma, beta, out_grad, tile_frame, tile_keep):
    up, down, swap = tensor_routes(4)
    half = tokens.shape[0] // 2
    slots = chunk_slots()
    bound, coef, bias, clipped = bounds(w_qkv, gamma, beta, tile_frame, tile_keep, slots)
    below, above, beside = send(tokens, up), send(tokens, down), send(tokens, swap)
    beside = after(beside, bound)
    far = [send(below[:half], up), send(above[half:], down)]
    early = (in_hbm(tokens), below, above, beside)
    q_sums, kv_sums = early_qkv(early, clipped)
    beside = after(beside, kv_sums)
    beside_below, beside_above = send(beside, up), send(beside, down)
    beside_far = [send(part, swap) for part in far]
    early = (in_hbm(after(tokens, *far)),) + early[1:]
    mask_sums = early_masks(slots, early, w_qkv, bound)
    late = (after(beside_below, mask_sums), beside_above, *far, *beside_far)
    kv, late = late_kv(late, clipped, kv_sums)
    kvs = (kv, swap_near(kv), swap_other(kv))
    query, products, last_products = late_rest(slots, (in_hbm(late),), w_qkv, bound, clipped, q_sums, mask_sums)
    t_other, t_near = swap_other(last_products), swap_near(last_products)
    attended, first, gq_first, for_near, for_other = attend(
        bias, 0, 2, query, kvs, out_grad, products, coef
    )
    from_other, from_near = swap_other(for_other), swap_near(for_near)
    attended, last, gq_last = attend(
        bias,
        2,
        1,
        query,
        kvs,
        out_grad,
        products,
        coef,
        (t_near, t_other, attended),
    )
    query_part = query_sums(
        slots, (in_hbm(late),), w_qkv, bound, mask_sums, gq_first, gq_last, coef
    )
    part = all_sums(from_near, from_other, products, coef, query_part, first, last)
    totals = sum_over_tm(part)
    return attended, totals[:, 0], totals[:, 1]


def solution(mesh):
    return jax.shard_map(
        body,
        mesh=mesh,
        in_specs=(
            P("tm", "tensor"),
            P(None, None, "tensor"),
            P(None, "tensor"),
            P(None, "tensor"),
            P("tm", "tensor"),
            P(),
            P(),
        ),
        out_specs=(P("tm", "tensor"), P(None, "tensor"), P(None, "tensor")),
        check_vma=False,
    )
```

```python
import functools
import math

import jax
import jax.numpy as jnp
from jax import lax
from jax.experimental import pallas as pl
from jax.experimental.pallas import tpu as pltpu
from jax.sharding import PartitionSpec as P

HEAD = 128
TILE = 384
REACH = 2
WINDOW = 2 * REACH + 1
SCALE = HEAD**-0.5
LOG2E = math.log2(math.e)
NEG = -1e30
MIB = 1024 * 1024

NT = (((1,), (1,)), ((), ()))


def dot(a, b):
    return jnp.dot(a, b, preferred_element_type=jnp.float32)


def dot_nt(a, b):
    return lax.dot_general(a, b, NT, preferred_element_type=jnp.float32)


def tensor_routes(z_count):
    def route(f):
        return [(z * 2 + y, f(z, y)) for z in range(z_count) for y in range(2)]

    up = route(lambda z, y: ((z + 1) % z_count) * 2 + y)
    down = route(lambda z, y: ((z - 1) % z_count) * 2 + y)
    swap = route(lambda z, y: z * 2 + 1 - y)
    return up, down, swap


def send(block, route):
    return lax.ppermute(block, "tensor", route)


def after(value, *others):
    return lax.optimization_barrier((value,) + others)[0]


def chunk_slots():
    me = lax.axis_index("tensor")
    z, y = me // 2, lax.rem(me, 2)
    below, above, far = lax.rem(z + 3, 4), lax.rem(z + 1, 4), lax.rem(z + 2, 4)
    return jnp.stack(
        [
            z * 2 + y,
            below * 2 + y,
            above * 2 + y,
            z * 2 + 1 - y,
            below * 2 + 1 - y,
            above * 2 + 1 - y,
            far * 2 + y,
            far * 2 + 1 - y,
        ]
    ).astype(jnp.int32)


def tile_bias(frame_ref, keep_ref, a):
    tiles = frame_ref.shape[0]
    bias = []
    for t in range(WINDOW):
        b = a + (t - REACH)
        b_in = jnp.clip(b, 0, tiles - 1)
        ok = (
            (b >= 0)
            & (b < tiles)
            & (jnp.abs(frame_ref[a] - frame_ref[b_in]) <= 1)
            & (keep_ref[t, a] == 1)
        )
        bias.append(jnp.where(ok, 0.0, NEG))
    return bias


def bounds_kernel(frame_ref, keep_ref, slot_ref, w_ref, gamma_ref, beta_ref, *outs):
    bound_ref, coef_ref, bias_ref, clipped_ref = outs
    w = w_ref[0].astype(jnp.float32)
    col_max = jnp.max(w, axis=0, keepdims=True)
    col_min = jnp.min(w, axis=0, keepdims=True)
    member = pl.program_id(0)
    sig_gamma = jax.nn.sigmoid(gamma_ref[pl.ds(member, 1), :])
    sig_beta = jax.nn.sigmoid(beta_ref[pl.ds(member, 1), :])
    upper = sig_gamma * col_max
    lower = sig_beta * col_min
    bound_ref[0, 0:1] = upper
    bound_ref[0, 1:2] = lower
    coef_ref[0, 0:1] = sig_gamma * (1.0 - sig_gamma) * col_max
    coef_ref[0, 1:2] = sig_beta * (1.0 - sig_beta) * col_min
    first = lax.axis_index("tm") * 2
    for i in range(2):
        for t, bias in enumerate(tile_bias(frame_ref, keep_ref, first + i)):
            bias_ref[i, t : t + 1] = jnp.full((1, HEAD), bias, jnp.float32)
        bias_ref[i, WINDOW:] = jnp.zeros((8 - WINDOW, HEAD), jnp.float32)
    _, count, depth, _ = clipped_ref.shape
    for slot in range(count):
        row = pl.multiple_of(slot_ref[slot] * depth, depth)
        block = w_ref[0, pl.ds(row, depth), :].astype(jnp.float32)
        clipped = jnp.minimum(jnp.maximum(block, lower), upper)
        clipped_ref[0, slot] = clipped.astype(jnp.bfloat16)


def bounds(w_qkv, gamma, beta, tile_frame, tile_keep, slots):
    members, rows, width = w_qkv.shape
    sorted_shape = (members, 8, rows // 8, width)
    whole = pl.BlockSpec((members, width), lambda p, *_: (0, 0))
    two = pl.BlockSpec((1, 2, width), lambda p, *_: (p, 0, 0))
    return pl.pallas_call(
        bounds_kernel,
        grid_spec=pltpu.PrefetchScalarGridSpec(
            num_scalar_prefetch=3,
            grid=(members,),
            in_specs=[pl.BlockSpec((1, rows, width), lambda p, *_: (p, 0, 0)), whole, whole],
            out_specs=[
                two,
                two,
                pl.BlockSpec((2, 8, HEAD), lambda p, *_: (0, 0, 0)),
                pl.BlockSpec((1,) + sorted_shape[1:], lambda p, *_: (p, 0, 0, 0)),
            ],
        ),
        out_shape=[pltpu.HBM((members, 2, width), jnp.float32)] * 2
        + [pltpu.HBM((2, 8, HEAD), jnp.float32), pltpu.HBM(sorted_shape, jnp.bfloat16)],
        compiler_params=pltpu.CompilerParams(vmem_limit_bytes=16 * MIB),
        cost_estimate=pl.CostEstimate(flops=0, bytes_accessed=7_000_000, transcendentals=0),
        name="clip_bounds",
    )(
        in_hbm(tile_frame),
        in_hbm(tile_keep.T),
        slots,
        in_hbm(w_qkv),
        in_hbm(gamma),
        in_hbm(beta),
    )


def load_rows(x_refs, x_scr, depth):
    col = row = 0
    for ref in x_refs:
        rows = ref.shape[0]
        x_scr[row : row + rows, col : col + depth] = ref[...]
        row += rows
        if row == x_scr.shape[0]:
            row, col = 0, col + depth


def fetch_rows(first_slot, first_member, load, slot_ref, w_ref, bound_ref, w_buf, w_sem, *bound):
    steps, count, depth, _ = w_buf.shape
    bound_copy = pltpu.make_async_copy(bound_ref, *bound)

    def copy(step, index):
        row = pl.multiple_of(slot_ref[first_slot + index] * depth, depth)
        return pltpu.make_async_copy(
            w_ref.at[step + first_member, pl.ds(row, depth), :],
            w_buf.at[step, index],
            w_sem.at[step, index],
        )

    step = pl.program_id(0)

    @pl.when(step == 0)
    def _():
        bound_copy.start()
        for index in range(count):
            copy(0, index).start()
        load()
        bound_copy.wait()

    for index in range(count):
        copy(step, index).wait()

    @pl.when(step == 0)
    def _():
        for other in range(1, steps):
            for index in range(count):
                copy(other, index).start()


def mask_rows(w_buf, step, member, bound_buf, out_scr):
    upper, lower = bound_buf[member, 0:1], bound_buf[member, 1:2]
    _, count, depth, width = w_buf.shape
    for index in range(count):
        block = w_buf[step, index].astype(jnp.float32)
        rows = slice(index * depth, (index + 1) * depth)
        out_scr[rows, 0:width] = jnp.where(block > upper, 1.0, 0.0).astype(jnp.bfloat16)
        out_scr[rows, width : 2 * width] = jnp.where(block < lower, 1.0, 0.0).astype(jnp.bfloat16)


def early_kv_kernel(*refs):
    x_refs, (w_ref, out_ref, x_scr) = refs[:-3], refs[-3:]
    _, _, depth, width = w_ref.shape

    @pl.when(pl.program_id(0) == 0)
    def _():
        load_rows(x_refs, x_scr, depth)

    out_ref[0] = dot(x_scr[...], w_ref[0].reshape(x_scr.shape[1], width))


def early_mask_kernel(slot_ref, *refs):
    x_refs, rest = refs[:-17], refs[-17:]
    w_ref, bound_ref, clipped_ref, out_ref, q_ref, x_scr, w_scr, w_buf, w_sem = rest[:9]
    bound_buf, bound_sem, out_buf, out_sem, q_scr, q_scr_sem, q_buf, q_sem = rest[9:]
    step, steps = pl.program_id(0), w_buf.shape[0]
    weights_copy = pltpu.make_async_copy(clipped_ref.at[0, pl.ds(0, 4)], q_scr, q_scr_sem)
    q_copy = pltpu.make_async_copy(q_buf, q_ref, q_sem)

    def load():
        weights_copy.start()
        load_rows(x_refs, x_scr, w_buf.shape[2])

    fetch_rows(0, 0, load, slot_ref, w_ref, bound_ref, w_buf, w_sem, bound_buf, bound_sem)

    @pl.when(step == 0)
    def _():
        weights_copy.wait()
        q_buf[...] = dot(x_scr[...], q_scr[...].reshape(x_scr.shape[1], w_buf.shape[3]))
        q_copy.start()

    mask_rows(w_buf, step, step, bound_buf, w_scr)
    out_buf[step] = dot(x_scr[...], w_scr[...]).astype(jnp.bfloat16)

    def copy(index):
        return pltpu.make_async_copy(out_buf.at[index], out_ref.at[index], out_sem.at[index])

    copy(step).start()

    @pl.when(step == steps - 1)
    def _():
        for index in range(steps):
            copy(index).wait()
        q_copy.wait()


def late_kv_kernel(*refs):
    x_refs, (w_ref, sum_ref, kv_ref, x_ref, x_scr, x_sem) = refs[:-6], refs[-6:]
    step, steps = pl.program_id(0), pl.num_programs(0)
    _, _, depth, width = w_ref.shape
    copy = pltpu.make_async_copy(x_scr, x_ref, x_sem)

    @pl.when(step == 0)
    def _():
        load_rows(x_refs, x_scr, depth)
        copy.start()

    result = dot(x_scr[...], w_ref[0].reshape(x_scr.shape[1], width))
    kv_ref[0] = (sum_ref[0] + result).astype(jnp.bfloat16)

    @pl.when(step == steps - 1)
    def _():
        copy.wait()


def late_rest_kernel(slot_ref, *refs):
    x_ref, w_ref, bound_ref, q_sum_ref, sum_ref, clipped_ref = refs[:6]
    q_ref, out_ref, last_ref = refs[6:9]
    x_scr, w_scr, w_buf, w_sem, bound_buf, bound_sem = refs[9:15]
    q_scr, q_scr_sem, q_buf, q_sem, sum_buf, sum_sem, x_sem = refs[15:]
    step, steps = pl.program_id(0), w_buf.shape[0]
    width = w_buf.shape[3]

    def copy(index):
        return pltpu.make_async_copy(sum_ref.at[index + 1], sum_buf.at[index], sum_sem.at[index])

    x_copy = pltpu.make_async_copy(x_ref, x_scr, x_sem)
    q_copy = pltpu.make_async_copy(q_sum_ref, q_buf, q_sem)
    weights_copy = pltpu.make_async_copy(clipped_ref.at[0, pl.ds(4, 4)], q_scr, q_scr_sem)

    def load():
        x_copy.start()
        weights_copy.start()

    fetch_rows(4, 1, load, slot_ref, w_ref, bound_ref, w_buf, w_sem, bound_buf, bound_sem)

    @pl.when(step == 0)
    def _():
        q_copy.start()
        for index in range(steps):
            copy(index).start()
        x_copy.wait()
        weights_copy.wait()
        product = dot(x_scr[...], q_scr[...].reshape(x_scr.shape[1], width))
        q_copy.wait()
        q_ref[...] = ((q_buf[...] + product) * (SCALE * LOG2E)).astype(jnp.bfloat16)

    mask_rows(w_buf, step, step + 1, bound_buf, w_scr)
    product = dot(x_scr[...], w_scr[...])
    copy(step).wait()
    result = (sum_buf[step].astype(jnp.float32) + product).astype(jnp.bfloat16)
    out_ref[0] = result
    last_ref[0, 0] = result[:, width - HEAD : width]
    last_ref[0, 1] = result[:, 2 * width - HEAD :]


def query_sums_kernel(slot_ref, *refs):
    x_ref, w_ref, bound_ref, sum_ref, first_ref, last_ref, coef_ref, out_ref = refs[:8]
    x_scr, w_scr, w_buf, w_sem, bound_buf, bound_sem, sum_buf, sum_sem, x_sem = refs[8:]
    width, narrow = w_buf.shape[3], first_ref.shape[1]
    x_copy = pltpu.make_async_copy(x_ref, x_scr, x_sem)
    sum_copy = pltpu.make_async_copy(sum_ref.at[0], sum_buf, sum_sem)

    def load():
        x_copy.start()
        sum_copy.start()

    fetch_rows(4, 0, load, slot_ref, w_ref, bound_ref, w_buf, w_sem, bound_buf, bound_sem)
    mask_rows(w_buf, 0, 0, bound_buf, w_scr)
    x_copy.wait()
    sum_copy.wait()
    result = sum_buf[...].astype(jnp.float32) + dot(x_scr[...], w_scr[...])
    for ref, cols in ((first_ref, slice(0, narrow)), (last_ref, slice(narrow, width))):
        grad = ref[...].astype(jnp.float32)
        for side in range(2):
            at = slice(side * width + cols.start, side * width + cols.stop)
            total = jnp.sum(grad * result[:, at], axis=0, keepdims=True)
            out_ref[0, side : side + 1, cols] = total * coef_ref[0, side : side + 1, cols]


def in_hbm(array):
    return pltpu.with_memory_space_constraint(array, pltpu.HBM)


def product_call(
    kernel, name, vmem, members, columns, slots, chunks, w_qkv, bound, sums, outs, scratch, cost
):
    _, count = members
    _, full, width = w_qkv.shape
    depth = full // 8
    rows = max(c.shape[0] for c in chunks)
    inner = sum(c.shape[0] * c.shape[1] for c in chunks) // rows
    stays = pl.BlockSpec(memory_space=pltpu.HBM)
    return pl.pallas_call(
        kernel,
        grid_spec=pltpu.PrefetchScalarGridSpec(
            num_scalar_prefetch=1,
            grid=(count,),
            in_specs=[
                stays if len(chunks) == 1 else pl.BlockSpec(c.shape, lambda p, s: (0, 0))
                for c in chunks
            ]
            + [stays, stays]
            + [stays if spec is None else spec for _, spec in sums],
            out_specs=[stays if spec is None else spec for spec, _ in outs],
            scratch_shapes=[
                pltpu.VMEM((rows, inner), jnp.bfloat16),
                pltpu.VMEM((inner, columns), jnp.bfloat16),
                pltpu.VMEM((count, inner // depth, depth, width), jnp.bfloat16),
                pltpu.SemaphoreType.DMA((count, inner // depth)),
                pltpu.VMEM(bound.shape, jnp.float32),
                pltpu.SemaphoreType.DMA(()),
            ]
            + scratch,
        ),
        out_shape=[shape for _, shape in outs],
        compiler_params=pltpu.CompilerParams(vmem_limit_bytes=vmem * MIB),
        cost_estimate=pl.CostEstimate(
            flops=int(2 * rows * inner * columns * count * cost),
            bytes_accessed=int(count * inner * width * 2 * cost),
            transcendentals=0,
        ),
        name=name,
    )(slots, *chunks, in_hbm(w_qkv), in_hbm(bound), *[a for a, _ in sums])


def rows_of(chunks):
    return max(c.shape[0] for c in chunks)


def members_out(members, rows, columns, dtype):
    spec = pl.BlockSpec((1, rows, columns), lambda p, s: (p, 0, 0))
    return spec, jax.ShapeDtypeStruct((members, rows, columns), dtype)


def qkv_call(kernel, name, members, half, chunks, clipped, sums, outs, scratch):
    first, count = members
    _, slots, depth, width = clipped.shape
    rows = rows_of(chunks)
    inner = slots // 2 * depth
    whole = lambda a: pl.BlockSpec(a.shape, lambda p: (0, 0))
    return pl.pallas_call(
        kernel,
        grid=(count,),
        in_specs=[whole(c) for c in chunks]
        + [pl.BlockSpec((1, slots // 2, depth, width), lambda p: (p + first, half, 0, 0))]
        + [spec for _, spec in sums],
        out_specs=[spec for spec, _ in outs],
        scratch_shapes=[pltpu.VMEM((rows, inner), jnp.bfloat16)] + scratch,
        out_shape=[shape for _, shape in outs],
        compiler_params=pltpu.CompilerParams(vmem_limit_bytes=19 * MIB),
        cost_estimate=pl.CostEstimate(
            flops=2 * rows * inner * width * count,
            bytes_accessed=count * inner * width * 2,
            transcendentals=0,
        ),
        name=name,
    )(*chunks, in_hbm(clipped), *[a for a, _ in sums])


def early_kv(chunks, clipped):
    members, _, _, width = clipped.shape
    rows = rows_of(chunks)
    spec = pl.BlockSpec((1, rows, width), lambda p: (p, 0, 0))
    outs = [(spec, jax.ShapeDtypeStruct((members - 1, rows, width), jnp.float32))]
    return qkv_call(
        early_kv_kernel, "early_kv", (1, members - 1), 0, chunks, clipped, [], outs, []
    )[0]


def early_rest(slots, chunks, w_qkv, bound, clipped):
    members, _, width = w_qkv.shape
    rows = rows_of(chunks)
    shape = (members, rows, 2 * width)
    outs = [(None, pltpu.HBM(shape, jnp.bfloat16)), (None, pltpu.HBM((rows, width), jnp.float32))]
    scratch = [
        pltpu.VMEM(shape, jnp.bfloat16),
        pltpu.SemaphoreType.DMA((members,)),
        pltpu.VMEM((4, w_qkv.shape[1] // 8, width), jnp.bfloat16),
        pltpu.SemaphoreType.DMA(()),
        pltpu.VMEM((rows, width), jnp.float32),
        pltpu.SemaphoreType.DMA(()),
    ]
    return product_call(
        early_mask_kernel,
        "early_rest",
        27,
        (0, members),
        2 * width,
        slots,
        chunks,
        w_qkv,
        bound,
        [(in_hbm(clipped), None)],
        outs,
        scratch,
        1,
    )


def late_kv(chunks, clipped, sums):
    members, slots, depth, width = clipped.shape
    rows = rows_of(chunks)
    spec = pl.BlockSpec((1, rows, width), lambda p: (p, 0, 0))
    outs = [
        (spec, jax.ShapeDtypeStruct((members - 1, rows, width), jnp.bfloat16)),
        (
            pl.BlockSpec(memory_space=pltpu.HBM),
            pltpu.HBM((rows, slots // 2 * depth), jnp.bfloat16),
        ),
    ]
    scratch = [pltpu.SemaphoreType.DMA(())]
    return qkv_call(
        late_kv_kernel,
        "late_kv",
        (1, members - 1),
        1,
        chunks,
        clipped,
        [(sums, spec)],
        outs,
        scratch,
    )


def late_rest(slots, chunks, w_qkv, bound, clipped, q_sums, sums):
    members, _, width = w_qkv.shape
    rows = rows_of(chunks)
    outs = [
        (
            pl.BlockSpec((rows, width), lambda p, s: (0, 0)),
            jax.ShapeDtypeStruct((rows, width), jnp.bfloat16),
        ),
        members_out(members - 1, rows, 2 * width, jnp.bfloat16),
        (
            pl.BlockSpec((1, 2, rows, HEAD), lambda p, s: (p, 0, 0, 0)),
            jax.ShapeDtypeStruct((2, 2, rows, HEAD), jnp.bfloat16),
        ),
    ]
    scratch = [
        pltpu.VMEM((4, w_qkv.shape[1] // 8, width), jnp.bfloat16),
        pltpu.SemaphoreType.DMA(()),
        pltpu.VMEM((rows, width), jnp.float32),
        pltpu.SemaphoreType.DMA(()),
        pltpu.VMEM((members - 1,) + sums.shape[1:], sums.dtype),
        pltpu.SemaphoreType.DMA((members - 1,)),
        pltpu.SemaphoreType.DMA(()),
    ]
    return product_call(
        late_rest_kernel,
        "late_rest",
        30,
        (1, members - 1),
        2 * width,
        slots,
        chunks,
        w_qkv,
        bound,
        [(in_hbm(q_sums), None), (in_hbm(sums), None), (in_hbm(clipped), None)],
        outs,
        scratch,
        1,
    )


def query_sums(slots, chunks, w_qkv, bound, sums, first, last, coef):
    _, _, width = w_qkv.shape
    two = pl.BlockSpec((1, 2, width), lambda p, s: (0, 0, 0))
    grad = lambda a: pl.BlockSpec(a.shape, lambda p, s: (0, 0))
    return product_call(
        query_sums_kernel,
        "query_sums",
        24,
        (0, 1),
        2 * width,
        slots,
        chunks,
        w_qkv,
        bound,
        [(in_hbm(sums), None), (first, grad(first)), (last, grad(last)), (coef, two)],
        [(two, jax.ShapeDtypeStruct((1, 2, width), jnp.float32))],
        [
            pltpu.VMEM(sums.shape[1:], sums.dtype),
            pltpu.SemaphoreType.DMA(()),
            pltpu.SemaphoreType.DMA(()),
        ],
        1,
    )[0]


def attend_kernel(returns, *refs):
    bias_ref, q_ref, kv_ref, near_ref, other_ref, grad_ref, high_ref, low_ref, coef_ref = refs[0:9]
    if returns:
        att_ref, sum_ref, gq_ref, for_near_ref, for_other_ref, k_scr, v_scr, gk_scr, gv_scr = refs[9:]
    else:
        t_near_ref, t_other_ref, _, att_ref, sum_ref, gq_ref, k_scr, v_scr, gk_scr, gv_scr = refs[9:]
    position = lax.axis_index("tm")
    count = 2 * TILE
    even = 1 - lax.rem(position, 2)
    near_at = pl.multiple_of(2 * count * even, count)
    other_at = pl.multiple_of(2 * count * (1 - even), count)
    for member, scr in enumerate((k_scr, v_scr)):
        scr[count : 2 * count] = kv_ref[member]
        scr[pl.ds(near_at, count), :] = near_ref[member]
        scr[pl.ds(other_at, count), :] = other_ref[member]
    sums = [[0.0, 0.0] for _ in range(2)]

    def add(member, grad, high, low):
        for side, t in enumerate((high, low)):
            part = grad * t.astype(jnp.float32)
            sums[member][side] += jnp.sum(part, axis=0, keepdims=True)

    state = []
    for i in range(2):
        bias = [bias_ref[i, t : t + 1, 0:1] for t in range(WINDOW)]
        rows = slice(i * TILE, (i + 1) * TILE)
        keys = slice(i * TILE, i * TILE + WINDOW * TILE)
        q = q_ref[rows, :]
        grad = grad_ref[rows, :]
        k = k_scr[keys]
        v = v_scr[keys]
        scores = dot_nt(q, k)
        state.append((bias, rows, keys, q, grad, k, v, scores))
    for i in range(2):
        bias, rows, keys, q, grad, k, v, scores = state[i]
        parts = [scores[:, t * TILE : (t + 1) * TILE] for t in range(WINDOW)]
        peak = functools.reduce(
            jnp.maximum,
            [jnp.max(p, axis=1, keepdims=True) + bias[t] for t, p in enumerate(parts)],
        )
        weights = [jnp.exp2(p - (peak - bias[t])) for t, p in enumerate(parts)]
        total = sum(jnp.sum(w, axis=1, keepdims=True) for w in weights)
        e = jnp.concatenate(weights, axis=1)
        e_low = e.astype(jnp.bfloat16)
        inv = 1.0 / total
        out = dot(e_low, v) * inv
        att_ref[rows, :] = out.astype(jnp.bfloat16)
        grad_wide = grad.astype(jnp.float32)
        delta = jnp.sum(out * grad_wide, axis=1, keepdims=True)
        dprobs = dot_nt(grad, v)
        ds = (e * (dprobs - delta)).astype(jnp.bfloat16)
        gq_ref[rows, :] = (dot(ds, k) * (inv * SCALE)).astype(jnp.bfloat16)
        q_scaled = (q.astype(jnp.float32) * (inv * (1.0 / LOG2E))).astype(jnp.bfloat16)
        grad_scaled = (grad_wide * inv).astype(jnp.bfloat16)
        gk = dot(q_scaled.T, ds)
        gv = dot(grad_scaled.T, e_low)
        if i == 0:
            gk_scr[:, keys] = gk
            gv_scr[:, keys] = gv
        else:
            span, head = WINDOW * TILE, slice(i * TILE, WINDOW * TILE)
            rest = slice(WINDOW * TILE, (WINDOW + 1) * TILE)
            gk_scr[:, head] += gk[:, 0 : span - TILE]
            gv_scr[:, head] += gv[:, 0 : span - TILE]
            gk_scr[:, rest] = gk[:, span - TILE :]
            gv_scr[:, rest] = gv[:, span - TILE :]
    for member, scr in enumerate((gk_scr, gv_scr)):
        own = scr[:, count : 2 * count].T
        for_near = scr[:, pl.ds(near_at, count)].T
        for_other = scr[:, pl.ds(other_at, count)].T
        add(member, own, high_ref[member], low_ref[member])
        if returns:
            for_near_ref[member] = for_near.astype(jnp.bfloat16)
            for_other_ref[member] = for_other.astype(jnp.bfloat16)
        else:
            add(member, for_near, t_near_ref[member, 0], t_near_ref[member, 1])
            add(member, for_other, t_other_ref[member, 0], t_other_ref[member, 1])
    for member in range(2):
        for side in range(2):
            sum_ref[member, side : side + 1] = (
                sums[member][side] * coef_ref[member + 1, side : side + 1]
            )


def attend(bias, first, count, query, kvs, out_grad, products, coef, last=None):
    rows, width = out_grad.shape
    heads = width // HEAD
    span = WINDOW * TILE
    column = pl.BlockSpec((rows, HEAD), lambda h: (0, h + first))
    pair = pl.BlockSpec((2, rows, HEAD), lambda h: (0, 0, h + first))
    halo = pl.BlockSpec((2, rows, HEAD), lambda h: (0, 0, h))
    high = pl.BlockSpec((2, rows, HEAD), lambda h: (0, 0, h + first))
    low = pl.BlockSpec((2, rows, HEAD), lambda h: (0, 0, h + first + heads))
    in_specs = [pl.BlockSpec((2, 8, HEAD), lambda h: (0, 0, 0))]
    in_specs += [column, pair, pair, pair, column, high, low]
    in_specs += [pl.BlockSpec((3, 2, HEAD), lambda h: (0, 0, h + first))]
    operands = [in_hbm(bias), query, *kvs, out_grad, products, products, in_hbm(coef)]
    out_specs = [column, pl.BlockSpec((2, 2, HEAD), lambda h: (0, 0, h))]
    out_specs += [pl.BlockSpec((rows, HEAD), lambda h: (0, h))]
    out_shape = [
        jax.ShapeDtypeStruct((rows, width), jnp.bfloat16),
        jax.ShapeDtypeStruct((2, 2, count * HEAD), jnp.float32),
        jax.ShapeDtypeStruct((rows, count * HEAD), jnp.bfloat16),
    ]
    aliases = {}
    if last is None:
        out_specs += [halo, halo]
        out_shape += [jax.ShapeDtypeStruct((2, rows, count * HEAD), jnp.bfloat16)] * 2
    else:
        near, other, attended = last
        in_specs += [pl.BlockSpec((2, 2, rows, HEAD), lambda h: (0, 0, 0, 0))] * 2
        in_specs += [pl.BlockSpec(memory_space=pl.ANY)]
        operands += [near, other, attended]
        aliases = {len(operands) - 1: 0}
    return pl.pallas_call(
        functools.partial(attend_kernel, last is None),
        grid=(count,),
        in_specs=in_specs,
        out_specs=out_specs,
        scratch_shapes=[pltpu.VMEM((6 * TILE, HEAD), jnp.bfloat16)] * 2
        + [pltpu.VMEM((HEAD, 6 * TILE), jnp.float32)] * 2,
        out_shape=out_shape,
        input_output_aliases=aliases,
        compiler_params=pltpu.CompilerParams(vmem_limit_bytes=34 * MIB),
        cost_estimate=pl.CostEstimate(
            flops=2 * 6 * rows * span * HEAD * count,
            bytes_accessed=5_000_000 * count,
            transcendentals=rows * span * count,
        ),
        name="attend",
    )(*operands)


def all_sums_kernel(near_ref, other_ref, high_ref, low_ref, coef_ref, *refs):
    query_ref, first_ref, last_ref, out_ref = refs
    member = pl.program_id(0)
    width = near_ref.shape[2]

    @pl.when(member == 0)
    def _():
        out_ref[0] = query_ref[0]

    @pl.when(member > 0)
    def _():
        out_ref[0, :, width:] = last_ref[0]
        grad = near_ref[0].astype(jnp.float32) + other_ref[0].astype(jnp.float32)
        for side, t_ref in enumerate((high_ref, low_ref)):
            part = grad * t_ref[0, :, 0:width].astype(jnp.float32)
            total = jnp.sum(part, axis=0, keepdims=True) * coef_ref[0, side : side + 1, 0:width]
            out_ref[0, side : side + 1, 0:width] = total + first_ref[0, side : side + 1]


def all_sums(near, other, products, coef, query, first, last):
    _, rows, narrow = near.shape
    width = products.shape[2] // 2
    grads = pl.BlockSpec((1, rows, narrow), lambda p: (jnp.maximum(p - 1, 0), 0, 0))
    two = lambda a: pl.BlockSpec((1, 2, a.shape[2]), lambda p: (p, 0, 0))
    pair = lambda a: pl.BlockSpec((1, 2, a.shape[2]), lambda p: (jnp.maximum(p - 1, 0), 0, 0))
    return pl.pallas_call(
        all_sums_kernel,
        grid=(3,),
        in_specs=[
            grads,
            grads,
            pl.BlockSpec((1, rows, width), lambda p: (jnp.maximum(p - 1, 0), 0, 0)),
            pl.BlockSpec((1, rows, width), lambda p: (jnp.maximum(p - 1, 0), 0, 1)),
            two(coef),
            pl.BlockSpec(query.shape, lambda p: (0, 0, 0)),
            pair(first),
            pair(last),
        ],
        out_specs=two(coef),
        out_shape=jax.ShapeDtypeStruct((3, 2, width), jnp.float32),
        compiler_params=pltpu.CompilerParams(vmem_limit_bytes=16 * MIB),
        cost_estimate=pl.CostEstimate(flops=0, bytes_accessed=5_000_000, transcendentals=0),
        name="all_sums",
    )(near, other, products, products, coef, query, first, last)


def swap_near(block):
    count = lax.axis_size("tm")
    return lax.ppermute(block, "tm", [(i, i ^ 1) for i in range(count)])


def swap_other(block):
    count = lax.axis_size("tm")
    pairs = [(i, i + 1) for i in range(1, count - 1, 2)]
    return lax.ppermute(block, "tm", pairs + [(b, a) for a, b in pairs])


def sum_over_tm(part):
    count = lax.axis_size("tm")
    swapped = lambda step: lax.ppermute(part, "tm", [(i, i ^ step) for i in range(count)])
    part = part + swapped(1)
    part = (part + swapped(2)) + (swapped(4) + swapped(6))
    return part + swapped(8)


def body(tokens, w_qkv, gamma, beta, out_grad, tile_frame, tile_keep):
    up, down, swap = tensor_routes(4)
    half = tokens.shape[0] // 2
    slots = chunk_slots()
    bound, coef, bias, clipped = bounds(w_qkv, gamma, beta, tile_frame, tile_keep, slots)
    below, above, beside = send(tokens, up), send(tokens, down), send(tokens, swap)
    above, beside = after(above, bound), after(beside, bound)
    far = [send(below[:half], up), send(above[half:], down)]
    early = (in_hbm(tokens), below, above, beside)
    kv_sums = early_kv(early, clipped)
    beside = after(beside, kv_sums)
    beside_below, beside_above = send(beside, up), send(beside, down)
    beside_far = [send(part, swap) for part in far]
    early = (in_hbm(after(tokens, *far)),) + early[1:]
    mask_sums, q_sums = early_rest(slots, early, w_qkv, bound, clipped)
    late = (after(beside_below, mask_sums), beside_above, *far, *beside_far)
    kv, late = late_kv(late, clipped, kv_sums)
    kvs = (kv, swap_near(kv), swap_other(kv))
    query, products, last_products = late_rest(slots, (in_hbm(late),), w_qkv, bound, clipped, q_sums, mask_sums)
    t_other, t_near = swap_other(last_products), swap_near(last_products)
    attended, first, gq_first, for_near, for_other = attend(
        bias, 0, 2, query, kvs, out_grad, products, coef
    )
    from_other, from_near = swap_other(for_other), swap_near(for_near)
    attended, last, gq_last = attend(
        bias,
        2,
        1,
        query,
        kvs,
        out_grad,
        products,
        coef,
        (t_near, t_other, attended),
    )
    query_part = query_sums(
        slots, (in_hbm(late),), w_qkv, bound, mask_sums, gq_first, gq_last, coef
    )
    part = all_sums(from_near, from_other, products, coef, query_part, first, last)
    totals = sum_over_tm(part)
    return attended, totals[:, 0], totals[:, 1]


def solution(mesh):
    return jax.shard_map(
        body,
        mesh=mesh,
        in_specs=(
            P("tm", "tensor"),
            P(None, None, "tensor"),
            P(None, "tensor"),
            P(None, "tensor"),
            P("tm", "tensor"),
            P(),
            P(),
        ),
        out_specs=(P("tm", "tensor"), P(None, "tensor"), P(None, "tensor")),
        check_vma=False,
    )
```
